32 devices in a mesh: seq: 8 (over z, x), head: 4 (over y, core).
Axes of the slice: x: 2, y: 2, z: 4, core: 2. Of those that a mesh axis runs over, the one named last changes fastest.
Arguments:
- tokens: bfloat16 [2, 8192, 1024], P(None, 'seq', 'head'), may hold values from -250 to 250
- cotangent: bfloat16 [2, 8192, 1024], P(None, 'seq', 'head'), may hold values from -6 to 6
- query_weight: float32 [1024, 4, 256], P('seq', 'head'), may hold values from -0.1875 to 0.1875
- query_mean: float32 [1024, 4, 256], P('seq', 'head'), may hold values from -24 to 24
- query_square: float32 [1024, 4, 256], P('seq', 'head'), may hold values from 1.47456 to 5.89824
- value_weight: float32 [1024, 4, 512], P('seq', 'head'), may hold values from -0.1875 to 0.1875
- value_mean: float32 [1024, 4, 512], P('seq', 'head'), may hold values from -32 to 32
- value_square: float32 [1024, 4, 512], P('seq', 'head'), may hold values from 2.62144 to 10.48576
- squeeze_weight: float32 [1024, 16], P('seq'), may hold values from -1 to 1
- squeeze_mean: float32 [1024, 16], P('seq'), may hold values from -24 to 24
- squeeze_square: float32 [1024, 16], P('seq'), may hold values from 1.47456 to 5.89824
- expand_weight: float32 [17, 512], replicated, may hold values from -2 to 12
- expand_mean: float32 [17, 512], replicated, may hold values from -4 to 4
- expand_square: float32 [17, 512], replicated, may hold values from 0.04096 to 0.16384
- group_weight: float32 [256], replicated, may hold values from 0.5 to 1.5
- group_mean: float32 [256], replicated, may hold values from -80 to 80
- group_square: float32 [256], replicated, may hold values from 16.384 to 65.536
- output_weight: float32 [1024, 1024], P('head', 'seq'), may hold values from -0.1875 to 0.1875
- output_mean: float32 [1024, 1024], P('head', 'seq'), may hold values from -48 to 48
- output_square: float32 [1024, 1024], P('head', 'seq'), may hold values from 5.89824 to 23.59296
- ffn_weight: float32 [1024, 2, 2816], P('seq', None, 'head'), may hold values from -0.1875 to 0.1875
- ffn_mean: float32 [1024, 2, 2816], P('seq', None, 'head'), may hold values from -24 to 24
- ffn_square: float32 [1024, 2, 2816], P('seq', None, 'head'), may hold values from 1.47456 to 5.89824
- down_weight: float32 [2816, 1024], P('head', 'seq'), may hold values from -0.109375 to 0.109375
- down_mean: float32 [2816, 1024], P('head', 'seq'), may hold values from -40 to 40
- down_square: float32 [2816, 1024], P('head', 'seq'), may hold values from 4.096 to 16.384
- norms_weight: float32 [2, 1024], P(None, 'seq'), may hold values from 0.5 to 1.5
- norms_mean: float32 [2, 1024], P(None, 'seq'), may hold values from -80 to 80
- norms_square: float32 [2, 1024], P(None, 'seq'), may hold values from 16.384 to 65.536
Outputs:
- block_out: bfloat16 [2, 8192, 1024], P(None, 'seq', 'head')
- tokens_grad: float32 [2, 8192, 1024], P(None, 'seq', 'head')
- query_new: float32 [1024, 4, 256], P('seq', 'head')
- query_newmean: float32 [1024, 4, 256], P('seq', 'head')
- query_newsquare: float32 [1024, 4, 256], P('seq', 'head')
- value_new: float32 [1024, 4, 512], P('seq', 'head')
- value_newmean: float32 [1024, 4, 512], P('seq', 'head')
- value_newsquare: float32 [1024, 4, 512], P('seq', 'head')
- squeeze_new: float32 [1024, 16], P('seq')
- squeeze_newmean: float32 [1024, 16], P('seq')
- squeeze_newsquare: float32 [1024, 16], P('seq')
- expand_new: float32 [17, 512], replicated
- expand_newmean: float32 [17, 512], replicated
- expand_newsquare: float32 [17, 512], replicated
- group_new: float32 [256], replicated
- group_newmean: float32 [256], replicated
- group_newsquare: float32 [256], replicated
- output_new: float32 [1024, 1024], P('head', 'seq')
- output_newmean: float32 [1024, 1024], P('head', 'seq')
- output_newsquare: float32 [1024, 1024], P('head', 'seq')
- ffn_new: float32 [1024, 2, 2816], P('seq', None, 'head')
- ffn_newmean: float32 [1024, 2, 2816], P('seq', None, 'head')
- ffn_newsquare: float32 [1024, 2, 2816], P('seq', None, 'head')
- down_new: float32 [2816, 1024], P('head', 'seq')
- down_newmean: float32 [2816, 1024], P('head', 'seq')
- down_newsquare: float32 [2816, 1024], P('head', 'seq')
- norms_new: float32 [2, 1024], P(None, 'seq')
- norms_newmean: float32 [2, 1024], P(None, 'seq')
- norms_newsquare: float32 [2, 1024], P(None, 'seq')
The draws below stay inside these ranges and needn't reach their ends.
All inputs are finite; a program needn't handle non-finite values.
Results may differ from the reference program's by a relative error of at most 0.012.
The reference program's roundings to bfloat16 on the way count: a program that leaves them out, or rounds other values in their place, can miss the bound.
Values may be sent and summed in bfloat16 or wider, within the bound.
No kernel may reach another device: no remote copies, remote signals or barrier semaphores. Data moves between devices by JAX's collectives and lax.ppermute only.
A program may use at most 192 MiB of HBM per device.

```python
import math
import jax
import jax.numpy as jnp
from jax import lax

MODEL_DIMENSION = 1024
KD = 512
VD = 1024
HEADS = 4
RANK = 16
FF = 2816
SPAN = 64
STEP = 10
SEQS = 2
LEN = 8192
HK = 128
HV = 256


def rank_columns(key):
    noise = jax.random.normal(jax.random.fold_in(key, 7), (MODEL_DIMENSION, RANK), jnp.float32)
    return jnp.clip(noise, -6.0, 6.0) / math.sqrt(MODEL_DIMENSION)


def draw_squeeze_weight(key, part):
    return rank_columns(key)


def draw_tokens(key, part):
    subkeys = jax.random.split(jax.random.fold_in(key, 3), 4)
    full_shape = (SEQS, LEN, MODEL_DIMENSION)
    noise = jax.random.normal(subkeys[0], full_shape, jnp.float32)
    noise = jnp.clip(noise, -5.0, 5.0)
    column = jax.random.uniform(subkeys[1], (MODEL_DIMENSION,), jnp.float32, 0.0, 1.0)
    column_scale = jnp.exp(math.log(0.3) + math.log(10.0) * column)
    row_scale = jnp.exp(jax.random.uniform(subkeys[2], (SEQS, LEN, 1), jnp.float32, 0.0, math.log(10.0)))
    value_entries = noise * column_scale * row_scale
    update_direction = rank_columns(key)[:, 0] * (2.0 * math.sqrt(MODEL_DIMENSION))
    token_position = jnp.arange(SEQS * LEN).reshape(SEQS, LEN, 1)
    device_locations = jax.random.randint(subkeys[3], (8,), 0, SEQS * LEN)
    sliced_row_group = jnp.any(token_position == device_locations.reshape(1, 1, 8), axis=2, keepdims=True)
    return jnp.where(sliced_row_group, update_direction.reshape(1, 1, MODEL_DIMENSION), value_entries).astype(jnp.bfloat16)


def draw_expand_weight(key, part):
    subkeys = jax.random.split(jax.random.fold_in(key, 5), 4)
    matrix = jnp.clip(jax.random.normal(subkeys[0], (RANK, KD), jnp.float32), -6.0, 6.0) / math.sqrt(RANK)
    fast_share = 0.5
    fast_mask = jax.random.uniform(subkeys[1], (KD,), jnp.float32) < fast_share
    fast_bias = jax.random.uniform(subkeys[2], (KD,), jnp.float32, 0.0, 1.2)
    slow_bias = math.log(LEN / 16.0) + jax.random.uniform(subkeys[3], (KD,), jnp.float32, 0.0, 2.0)
    bias_row = jnp.where(fast_mask, fast_bias, slow_bias)
    return jnp.concatenate([matrix, bias_row[None, :]], axis=0)


def levels(key, shape, cuts, least, high):
    factor_of, own = 1.0, jax.random.fold_in(key, 6)
    for axis_at, parts in cuts:
        steps = jnp.exp(jax.random.uniform(jax.random.fold_in(own, axis_at), (parts,), jnp.float32, least / len(cuts), high / len(cuts)))
        factor_of = factor_of * jnp.repeat(steps, shape[axis_at] // parts).reshape([-1 if axis == axis_at else 1 for axis in range(len(shape))])
    return factor_of


def centred(rng, dims, width, most, shards=(), held_as=jnp.bfloat16):
    drawn = width * jax.random.normal(rng, dims, jnp.float32)
    if shards:
        drawn = drawn * levels(rng, dims, shards, -0.22, 0.18)
    return jnp.clip(drawn, -most, most).astype(held_as)


def setup_inputs(seed: int = 0) -> dict:
    streams_of = jax.random.split(jax.random.key(seed), 30)
    tokens = draw_tokens(jax.random.fold_in(streams_of[29], 71), 0)
    cotangent = centred(streams_of[1], (SEQS, LEN, MODEL_DIMENSION), 1.0, 6.0, ((1, 8), (2, 4)))
    query_weight = centred(streams_of[2], (MODEL_DIMENSION, HEADS, 2 * HK), MODEL_DIMENSION ** -0.5, 0.1875, ((0, 8), (1, 4)), jnp.float32)
    query_mean = centred(streams_of[3], (MODEL_DIMENSION, HEADS, 2 * HK), (0.033 * (SEQS * LEN) ** 0.5), 24.0, ((0, 8), (1, 4)), jnp.float32)
    query_square = jnp.clip(jnp.exp(math.log(5.89824) - 1.3862944 * jax.random.uniform(streams_of[4], (MODEL_DIMENSION, HEADS, 2 * HK), jnp.float32) ** levels(streams_of[4], (MODEL_DIMENSION, HEADS, 2 * HK), ((0, 8), (1, 4)), -0.2, 0.2)), 1.47456, 5.89824)
    value_weight = centred(streams_of[5], (MODEL_DIMENSION, HEADS, 2 * HV), MODEL_DIMENSION ** -0.5, 0.1875, ((0, 8), (1, 4)), jnp.float32)
    value_mean = centred(streams_of[6], (MODEL_DIMENSION, HEADS, 2 * HV), (0.044 * (SEQS * LEN) ** 0.5), 32.0, ((0, 8), (1, 4)), jnp.float32)
    value_square = jnp.clip(jnp.exp(math.log(10.48576) - 1.3862944 * jax.random.uniform(streams_of[7], (MODEL_DIMENSION, HEADS, 2 * HV), jnp.float32) ** levels(streams_of[7], (MODEL_DIMENSION, HEADS, 2 * HV), ((0, 8), (1, 4)), -0.2, 0.2)), 2.62144, 10.48576)
    squeeze_weight = draw_squeeze_weight(jax.random.fold_in(streams_of[29], 71), 0)
    squeeze_mean = centred(streams_of[9], (MODEL_DIMENSION, RANK), (0.033 * (SEQS * LEN) ** 0.5), 24.0, ((0, 8),), jnp.float32)
    squeeze_square = jnp.clip(jnp.exp(math.log(5.89824) - 1.3862944 * jax.random.uniform(streams_of[10], (MODEL_DIMENSION, RANK), jnp.float32) ** levels(streams_of[10], (MODEL_DIMENSION, RANK), ((0, 8),), -0.2, 0.2)), 1.47456, 5.89824)
    expand_weight = draw_expand_weight(jax.random.fold_in(streams_of[29], 71), 0)
    expand_mean = centred(streams_of[12], (RANK + 1, KD), (0.0056 * (SEQS * LEN) ** 0.5), 4.0, (), jnp.float32)
    expand_square = jnp.clip(jnp.exp(jax.random.uniform(streams_of[13], (RANK + 1, KD), jnp.float32, math.log(0.04096), math.log(0.16384))), 0.04096, 0.16384)
    group_weight = jnp.clip(1.0 + 0.1 * jax.random.normal(streams_of[14], (HV,), jnp.float32), 0.5, 1.5)
    group_mean = centred(streams_of[15], (HV,), (0.111 * (SEQS * LEN) ** 0.5), 80.0, (), jnp.float32)
    group_square = jnp.clip(jnp.exp(jax.random.uniform(streams_of[16], (HV,), jnp.float32, math.log(16.384), math.log(65.536))), 16.384, 65.536)
    output_weight = centred(streams_of[17], (VD, MODEL_DIMENSION), VD ** -0.5, 0.1875, ((0, 4), (1, 8)), jnp.float32)
    output_mean = centred(streams_of[18], (VD, MODEL_DIMENSION), (0.067 * (SEQS * LEN) ** 0.5), 48.0, ((0, 4), (1, 8)), jnp.float32)
    output_square = jnp.clip(jnp.exp(math.log(23.59296) - 1.3862944 * jax.random.uniform(streams_of[19], (VD, MODEL_DIMENSION), jnp.float32) ** levels(streams_of[19], (VD, MODEL_DIMENSION), ((0, 4), (1, 8)), -0.2, 0.2)), 5.89824, 23.59296)
    ffn_weight = centred(streams_of[20], (MODEL_DIMENSION, 2, FF), MODEL_DIMENSION ** -0.5, 0.1875, ((0, 8), (2, 4)), jnp.float32)
    ffn_mean = centred(streams_of[21], (MODEL_DIMENSION, 2, FF), (0.033 * (SEQS * LEN) ** 0.5), 24.0, ((0, 8), (2, 4)), jnp.float32)
    ffn_square = jnp.clip(jnp.exp(math.log(5.89824) - 1.3862944 * jax.random.uniform(streams_of[22], (MODEL_DIMENSION, 2, FF), jnp.float32) ** levels(streams_of[22], (MODEL_DIMENSION, 2, FF), ((0, 8), (2, 4)), -0.2, 0.2)), 1.47456, 5.89824)
    down_weight = centred(streams_of[23], (FF, MODEL_DIMENSION), FF ** -0.5, 0.109375, ((0, 4), (1, 8)), jnp.float32)
    down_mean = centred(streams_of[24], (FF, MODEL_DIMENSION), (0.056 * (SEQS * LEN) ** 0.5), 40.0, ((0, 4), (1, 8)), jnp.float32)
    down_square = jnp.clip(jnp.exp(math.log(16.384) - 1.3862944 * jax.random.uniform(streams_of[25], (FF, MODEL_DIMENSION), jnp.float32) ** levels(streams_of[25], (FF, MODEL_DIMENSION), ((0, 4), (1, 8)), -0.2, 0.2)), 4.096, 16.384)
    norms_weight = jnp.clip(1.0 + 0.1 * jax.random.normal(streams_of[26], (2, MODEL_DIMENSION), jnp.float32), 0.5, 1.5)
    norms_mean = centred(streams_of[27], (2, MODEL_DIMENSION), (0.111 * (SEQS * LEN) ** 0.5), 80.0, ((1, 8),), jnp.float32)
    norms_square = jnp.clip(jnp.exp(math.log(65.536) - 1.3862944 * jax.random.uniform(streams_of[28], (2, MODEL_DIMENSION), jnp.float32) ** levels(streams_of[28], (2, MODEL_DIMENSION), ((1, 8),), -0.2, 0.2)), 16.384, 65.536)
    return dict(tokens=tokens, cotangent=cotangent, query_weight=query_weight, query_mean=query_mean, query_square=query_square, value_weight=value_weight, value_mean=value_mean, value_square=value_square, squeeze_weight=squeeze_weight, squeeze_mean=squeeze_mean, squeeze_square=squeeze_square, expand_weight=expand_weight, expand_mean=expand_mean, expand_square=expand_square, group_weight=group_weight, group_mean=group_mean, group_square=group_square, output_weight=output_weight, output_mean=output_mean, output_square=output_square, ffn_weight=ffn_weight, ffn_mean=ffn_mean, ffn_square=ffn_square, down_weight=down_weight, down_mean=down_mean, down_square=down_square, norms_weight=norms_weight, norms_mean=norms_mean, norms_square=norms_square)


@jax.custom_vjp
def low(v):
    return lax.optimization_barrier(v.astype(jnp.bfloat16)).astype(jnp.float32)

@jax.custom_vjp
def low_back(v):
    return v

def low_keep(v):
    return (low(v), None)

def low_pass(kept, grad):
    return (grad,)

def back_keep(v):
    return (v, None)

def back_low(kept, grad):
    return (low(grad),)
low.defvjp(low_keep, low_pass)
low_back.defvjp(back_keep, back_low)
eps_norm = 1e-06
gate_scale = 16.0
beta_one = 0.9
beta_two = 0.999
eps_adam = 1e-06
decay_rate = 0.01
learn_rate = 0.5
highest = lax.Precision.HIGHEST

def both_ways(value_entries):
    return low(low_back(value_entries))

def exact(left, right):
    return jnp.dot(left, right, precision=highest)

def rms_scale(value_entries, gain_vector):
    return value_entries * lax.rsqrt(lax.optimization_barrier(jnp.mean(value_entries * value_entries, axis=-1, keepdims=True)) + eps_norm) * gain_vector

def span_step(running, element):
    queries, key_rows, value_entries, decay_factors = element
    cumulate = jnp.cumsum(decay_factors, axis=0)
    closing = cumulate[-1:]
    query_decayed = queries * jnp.exp(cumulate)
    key_inverse = key_rows * jnp.exp(-cumulate)
    key_closing = key_rows * jnp.exp(closing - cumulate)
    scores = jnp.einsum('ihc,jhc->hij', query_decayed, key_inverse, precision=highest)
    causal = jnp.arange(SPAN)[:, None] >= jnp.arange(SPAN)[None, :]
    scores = jnp.where(causal[None], scores, 0.0)
    within = jnp.einsum('hij,jhv->ihv', scores, value_entries, precision=highest)
    across = jnp.einsum('ihc,hcv->ihv', query_decayed, running, precision=highest)
    updated = jnp.exp(closing[0])[:, :, None] * running + jnp.einsum('jhc,jhv->hcv', key_closing, value_entries, precision=highest)
    return (updated, (within + across) * HK ** (-0.5))

def to_spans(value_entries):
    return value_entries.reshape(LEN // SPAN, SPAN, HEADS, value_entries.shape[-1])

def layer(sequence_rows, params):
    query_weight, value_weight, squeeze_weight, expand_weight, group_weight, output_weight, ffn_weight, down_weight, norms_weight = params
    norm_gains = low(norms_weight)
    normed = low(rms_scale(sequence_rows, norm_gains[0]))
    query_key = exact(normed, low(query_weight).reshape(MODEL_DIMENSION, HEADS * 2 * HK)).reshape(LEN, HEADS, 2 * HK)
    queries = both_ways(query_key[:, :, :HK])
    key_rows = both_ways(query_key[:, :, HK:])
    value_gate = exact(normed, low(value_weight).reshape(MODEL_DIMENSION, HEADS * 2 * HV)).reshape(LEN, HEADS, 2 * HV)
    value_entries = both_ways(value_gate[:, :, :HV])
    gate_values = low_back(value_gate[:, :, HV:])
    rank_values = low_back(exact(normed, low(squeeze_weight)))
    logits = exact(rank_values, expand_weight[:RANK]) + expand_weight[RANK]
    decay_factors = (jax.nn.log_sigmoid(logits) / gate_scale).reshape(LEN, HEADS, HK)
    start_state = jnp.zeros((HEADS, HK, HV), jnp.float32)
    final_state, outputs = lax.scan(jax.checkpoint(span_step), start_state, (to_spans(queries), to_spans(key_rows), to_spans(value_entries), to_spans(decay_factors)))
    recurrent = outputs.reshape(LEN, HEADS, HV)
    mixed = low(rms_scale(recurrent, group_weight) * jax.nn.silu(gate_values)).reshape(LEN, VD)
    residual = sequence_rows + low_back(exact(mixed, low(output_weight)))
    normed_two = low(rms_scale(residual, norm_gains[1]))
    gate_part = low_back(exact(normed_two, low(ffn_weight[:, 0, :])))
    up_part = low_back(exact(normed_two, low(ffn_weight[:, 1, :])))
    hidden = low(jax.nn.silu(gate_part) * up_part)
    return residual + low_back(exact(hidden, low(down_weight)))

def adam_direction(master, gradient, first_moment, second_moment, fix_one, second_correction):
    new_first = beta_one * first_moment + (1.0 - beta_one) * gradient
    new_second = beta_two * second_moment + (1.0 - beta_two) * gradient * gradient
    update_direction = new_first / fix_one / (jnp.sqrt(new_second / second_correction) + eps_adam) + decay_rate * master
    return (new_first, new_second, update_direction)

def reference(tokens, cotangent, query_weight, query_mean, query_square, value_weight, value_mean, value_square, squeeze_weight, squeeze_mean, squeeze_square, expand_weight, expand_mean, expand_square, group_weight, group_mean, group_square, output_weight, output_mean, output_square, ffn_weight, ffn_mean, ffn_square, down_weight, down_mean, down_square, norms_weight, norms_mean, norms_square):
    masters = (query_weight, value_weight, squeeze_weight, expand_weight, group_weight, output_weight, ffn_weight, down_weight, norms_weight)
    firsts = (query_mean, value_mean, squeeze_mean, expand_mean, group_mean, output_mean, ffn_mean, down_mean, norms_mean)
    seconds = (query_square, value_square, squeeze_square, expand_square, group_square, output_square, ffn_square, down_square, norms_square)

    def sequence_step(running, element):
        sequence_rows, pulled = element
        out_rows, pullback = jax.vjp(layer, sequence_rows, masters)
        rows_grad, params_grad = pullback(pulled)
        return (jax.tree.map(jnp.add, running, params_grad), (out_rows, rows_grad))
    zero_grads = jax.tree.map(jnp.zeros_like, masters)
    grads, (outputs, tokens_grad) = lax.scan(sequence_step, zero_grads, (tokens.astype(jnp.float32), cotangent.astype(jnp.float32)))
    step_float = jnp.asarray(STEP, jnp.float32)
    fix_one = 1.0 - jnp.power(beta_one, step_float)
    second_correction = 1.0 - jnp.power(beta_two, step_float)
    results = []
    for master, gradient, first_moment, second_moment in zip(masters, grads, firsts, seconds):
        new_first, new_second, update_direction = adam_direction(master, gradient, first_moment, second_moment, fix_one, second_correction)
        trust_ratio = jnp.sqrt(jnp.sum(master * master)) / (jnp.sqrt(jnp.sum(update_direction * update_direction)) + eps_adam)
        results.append(master - learn_rate * trust_ratio * update_direction)
        results.append(new_first)
        results.append(new_second)
    return (outputs.astype(jnp.bfloat16), tokens_grad, results[0], results[1], results[2], results[3], results[4], results[5], results[6], results[7], results[8], results[9], results[10], results[11], results[12], results[13], results[14], results[15], results[16], results[17], results[18], results[19], results[20], results[21], results[22], results[23], results[24], results[25], results[26])
```

```python
import jax
import jax.numpy as jnp
from jax import lax
from jax.sharding import PartitionSpec as P

SPAN = 64
STEP = 10


eps_norm = 1e-06
gate_scale = 16.0
beta_one = 0.9
beta_two = 0.999
eps_adam = 1e-06
decay_rate = 0.01
learn_rate = 0.5
highest = lax.Precision.HIGHEST


def to_half(value_entries):
    return value_entries.astype(jnp.bfloat16)


def to_float(value_entries):
    return value_entries.astype(jnp.float32)


def mm(pattern, left, right):
    return jnp.einsum(pattern, left, right, preferred_element_type=jnp.float32)


def exact(pattern, left, right):
    return jnp.einsum(pattern, left, right, precision=highest)


def swap(value_entries, axis, bit):
    peers = lax.axis_size(axis)
    return lax.ppermute(value_entries, axis, [(i, i ^ bit) for i in range(peers)])


def bit_of(axis, bit):
    return (lax.axis_index(axis) // bit) % 2


def pick(value_entries, at, axis=0):
    return lax.dynamic_index_in_dim(value_entries, at, axis, keepdims=False)


def ordered(mine, other, upper):
    return (jnp.where(upper == 0, mine, other), jnp.where(upper == 0, other, mine))


def seq_bits():
    bits, bit = [], lax.axis_size("seq") // 2
    while bit:
        bits.append(("seq", bit))
        bit //= 2
    return bits


def gather_cube(part, stages):
    held = []
    rank = [("head", 2)] + seq_bits()
    for axis, bit in stages:
        low, high = ordered(part, swap(part, axis, bit), bit_of(axis, bit))
        held = sorted(held + [(axis, bit)], key=rank.index)
        part = jnp.stack([low, high], axis=held.index((axis, bit)))
    return part.reshape((2, lax.axis_size("seq")) + part.shape[len(held) :])


def scatter_cube(part, stages):
    held = [("head", 2)] + seq_bits()
    part = part.reshape((2,) * len(held) + part.shape[2:])
    for axis, bit in stages:
        at = held.index((axis, bit))
        held.pop(at)
        upper = bit_of(axis, bit)
        moved = swap(to_half(pick(part, 1 - upper, at)), axis, bit)
        part = to_float(pick(part, upper, at)) + to_float(moved)
    return part


def sum_everywhere(value_entries):
    for axis, bit in [("head", 1), ("head", 2)] + seq_bits()[::-1]:
        value_entries = value_entries + swap(value_entries, axis, bit)
    return value_entries


def scan_blocks(decay, state, reverse):
    before_decay, before_state = (jnp.ones_like(decay), jnp.zeros_like(state))
    for axis, bit in seq_bits()[::-1]:
        upper = bit_of(axis, bit) == (0 if reverse else 1)
        other_decay, other_state = (swap(decay, axis, bit), swap(state, axis, bit))
        before_state = jnp.where(
            upper, before_decay[:, :, None] * other_state + before_state, before_state
        )
        before_decay = jnp.where(upper, before_decay * other_decay, before_decay)
        state = jnp.where(
            upper,
            decay[:, :, None] * other_state + state,
            other_decay[:, :, None] * state + other_state,
        )
        decay = decay * other_decay
    return before_state


def norm_piece(value_entries, gain_vector):
    return (
        value_entries
        * lax.rsqrt(jnp.mean(value_entries * value_entries, axis=-1, keepdims=True) + eps_norm)
        * gain_vector
    )


def gate_piece(recurrent, gate_values, gain_vector):
    return norm_piece(recurrent, gain_vector) * jax.nn.silu(gate_values)


def swish_product(gate_part, up_part):
    return jax.nn.silu(gate_part) * up_part


def span_local(queries, key_rows, value_entries, decay_factors):
    sequences, tokens, key_width = queries.shape
    value_width = value_entries.shape[-1]
    blocks = tokens // SPAN
    cumulate = jnp.cumsum(decay_factors.reshape(sequences, blocks, SPAN, key_width), axis=2)
    closing = cumulate[:, :, -1:, :]
    query_decayed = queries.reshape(sequences, blocks, SPAN, key_width) * jnp.exp(cumulate)
    key_blocks = key_rows.reshape(sequences, blocks, SPAN, key_width)
    key_inverse = key_blocks * jnp.exp(-cumulate)
    key_closing = key_blocks * jnp.exp(closing - cumulate)
    value_blocks = value_entries.reshape(sequences, blocks, SPAN, value_width)
    scores = jnp.einsum("sbic,sbjc->sbij", query_decayed, key_inverse, precision=highest)
    causal = jnp.arange(SPAN)[:, None] >= jnp.arange(SPAN)[None, :]
    scores = jnp.where(causal, scores, 0.0)
    within = jnp.einsum("sbij,sbjv->sbiv", scores, value_blocks, precision=highest)
    block_states = jnp.einsum("sbjc,sbjv->sbcv", key_closing, value_blocks, precision=highest)

    def advance(running, element):
        decay_item, state_item = element
        return (decay_item[:, :, None] * running + state_item, running)

    start_state = jnp.zeros((sequences, key_width, value_width), jnp.float32)
    final_state, starting = lax.scan(
        advance,
        start_state,
        (jnp.moveaxis(jnp.exp(closing[:, :, 0, :]), 1, 0), jnp.moveaxis(block_states, 1, 0)),
    )
    starting = jnp.moveaxis(starting, 0, 1)
    across = jnp.einsum("sbic,sbcv->sbiv", query_decayed, starting, precision=highest)
    outputs = (within + across).reshape(sequences, tokens, value_width) * key_width ** (-0.5)
    return (outputs, final_state)


def carried(queries, decay_factors, incoming):
    sequences, tokens, key_width = queries.shape
    blocks = tokens // SPAN
    cumulate = jnp.cumsum(decay_factors.reshape(sequences, blocks, SPAN, key_width), axis=2)
    totals = cumulate[:, :, -1, :]
    offsets = jnp.cumsum(totals, axis=1) - totals
    through = (cumulate + offsets[:, :, None, :]).reshape(sequences, tokens, key_width)
    decayed = queries * jnp.exp(through)
    return jnp.einsum("stc,scv->stv", decayed, incoming, precision=highest) * key_width ** (-0.5)


def adam_direction(master, gradient, first_moment, second_moment, fix_one, second_correction):
    new_first = beta_one * first_moment + (1.0 - beta_one) * gradient
    new_second = beta_two * second_moment + (1.0 - beta_two) * gradient * gradient
    update_direction = (
        new_first / fix_one / (jnp.sqrt(new_second / second_correction) + eps_adam)
        + decay_rate * master
    )
    return (new_first, new_second, update_direction)


def per_device(
    tokens,
    cotangent,
    query_weight,
    query_mean,
    query_square,
    value_weight,
    value_mean,
    value_square,
    squeeze_weight,
    squeeze_mean,
    squeeze_square,
    expand_weight,
    expand_mean,
    expand_square,
    group_weight,
    group_mean,
    group_square,
    output_weight,
    output_mean,
    output_square,
    ffn_weight,
    ffn_mean,
    ffn_square,
    down_weight,
    down_mean,
    down_square,
    norms_weight,
    norms_mean,
    norms_square,
):
    sequences, segment, column_count = tokens.shape
    head_index = lax.axis_index("head")
    chip, core = (head_index // 2, head_index % 2)
    rows = query_weight.shape[0]
    peers = lax.axis_size("seq")
    model_width = rows * peers
    key_width = query_weight.shape[2] // 2
    value_width = value_weight.shape[2] // 2
    half_segment = segment // 2
    seq_stages = seq_bits()

    small = jnp.concatenate([squeeze_weight, norms_weight.T], axis=1)
    rank_count = squeeze_weight.shape[1]
    small = jnp.pad(small, ((0, 0), (0, 128 - small.shape[1])))
    first = gather_cube(
        to_half(jnp.concatenate([query_weight[:, 0, :], small], axis=1)),
        [("head", 2), ("seq", 1)] + seq_stages[:-1],
    ).reshape(2, model_width, 2 * key_width + 128)
    value_full = gather_cube(
        to_half(value_weight[:, 0, :]), seq_stages + [("head", 2)]
    ).reshape(2, model_width, 2 * value_width)
    query_full = first[:, :, : 2 * key_width]
    small_full = first[0, :, 2 * key_width :]
    squeeze_full = small_full[:, :rank_count]
    gains = to_float(small_full[:, rank_count : rank_count + 2])
    gain_one, gain_two = (gains[:, 0], gains[:, 1])
    output_mine = to_half(output_weight.T)
    output_pair = jnp.stack(ordered(output_mine, swap(output_mine, "head", 2), chip))
    output_full = jnp.moveaxis(lax.all_gather(output_pair, "seq", axis=0), 0, 1).reshape(
        2, model_width, value_width
    )
    ffn_mine = to_half(jnp.stack([ffn_weight[:, 0, :], ffn_weight[:, 1, :], down_weight.T]))
    ffn_full = jnp.moveaxis(lax.all_gather(ffn_mine, "seq", axis=0), 0, 1).reshape(
        3, model_width, ffn_weight.shape[2]
    )

    def full_rows(mine, other):
        pair = jnp.stack(ordered(mine, other, chip))
        low, high = ordered(pair, swap(pair, "head", 1), core)
        return jnp.concatenate([low[0], high[0], low[1], high[1]], axis=-1)

    input_half = full_rows(pick(tokens, chip), swap(pick(tokens, 1 - chip), "head", 2))
    cot_full = full_rows(cotangent, swap(cotangent, "head", 2))
    cot_own, cot_other = (pick(cot_full, chip), pick(cot_full, 1 - chip))
    inputs = to_float(input_half)
    scale_one = lax.rsqrt(jnp.mean(inputs * inputs, axis=1, keepdims=True) + eps_norm)
    normed = to_half(inputs * scale_one * gain_one)

    query_key = mm("td,hdc->htc", normed, query_full)
    queries = to_half(query_key[:, :, :key_width])
    key_rows = to_half(query_key[:, :, key_width:])
    value_gate = mm("td,hdc->htc", normed, value_full)
    value_entries = to_half(value_gate[:, :, :value_width])
    gate_values = value_gate[:, :, value_width:]
    rank_values = mm("td,dr->tr", normed, squeeze_full)
    expand_columns = pick(expand_weight.reshape(rank_count + 1, 2, 2, key_width), core, 2)
    logits = (
        exact("tr,rhc->htc", rank_values, expand_columns[:rank_count])
        + expand_columns[rank_count][:, None, :]
    )
    decay_factors = jax.nn.log_sigmoid(logits) / gate_scale
    (local_out, block_state), pull_local = jax.vjp(
        span_local, to_float(queries), to_float(key_rows), to_float(value_entries), decay_factors
    )
    block_decay = jnp.exp(jnp.sum(decay_factors, axis=1))
    state_in = scan_blocks(block_decay, block_state, False)
    carried_out, pull_carried = jax.vjp(carried, to_float(queries), decay_factors, state_in)
    recurrent = local_out + carried_out
    mixed_value, pull_gate = jax.vjp(gate_piece, recurrent, gate_values, group_weight)
    mixed_half = to_half(mixed_value)
    mixer_part = to_half(mm("htv,hdv->td", mixed_half, output_full))
    residual = inputs + (to_float(mixer_part) + to_float(swap(mixer_part, "head", 1)))
    scale_two = lax.rsqrt(jnp.mean(residual * residual, axis=1, keepdims=True) + eps_norm)
    normed_two = to_half(residual * scale_two * gain_two)

    moved = swap(lax.dynamic_slice_in_dim(normed_two, core * half_segment, half_segment, 0), "head", 2)
    normed_two_other = jnp.concatenate(ordered(moved, swap(moved, "head", 1), core), axis=0)

    def feed_forward(normed_rows, cot_rows):
        gate_part = mm("td,df->tf", normed_rows, ffn_full[0])
        up_part = mm("td,df->tf", normed_rows, ffn_full[1])
        hidden_value, pull_hidden = jax.vjp(swish_product, gate_part, up_part)
        hidden = to_half(hidden_value)
        out_part = mm("tf,df->td", hidden, ffn_full[2])
        hidden_grad = mm("td,df->tf", cot_rows, ffn_full[2])
        gate_grad, up_grad = map(to_half, pull_hidden(hidden_grad))
        rows_grad = mm("tf,df->td", gate_grad, ffn_full[0]) + mm("tf,df->td", up_grad, ffn_full[1])
        return out_part, rows_grad, hidden, gate_grad, up_grad

    own = feed_forward(normed_two, cot_own)
    other = feed_forward(normed_two_other, cot_other)
    other_rows = other[1].reshape(2, half_segment, model_width)
    other_sum = pick(other_rows, core) + to_float(
        swap(to_half(pick(other_rows, 1 - core)), "head", 1)
    )
    home = to_float(swap(to_half(other_sum), "head", 2))
    own_grad = to_half(
        own[1]
        + lax.dynamic_update_slice_in_dim(jnp.zeros_like(own[1]), home, core * half_segment, 0)
    )
    normed_two_grad = to_float(own_grad) + to_float(swap(own_grad, "head", 1))
    out_rows = jnp.stack([own[0], other[0]]).reshape(2, segment, 2, 2, column_count)
    out_rows = pick(out_rows, core, 3) + to_float(
        swap(to_half(pick(out_rows, 1 - core, 3)), "head", 1)
    )
    residual_cols = pick(residual.reshape(segment, 2, 2, column_count), core, 2)
    out_rows = out_rows + jnp.stack([residual_cols, jnp.zeros_like(residual_cols)])
    out_home = to_float(swap(to_half(pick(out_rows, 1 - chip, 2)), "head", 2))
    block_out = to_half(
        jnp.stack(ordered(*(pick(out_rows, chip, 2) + out_home[::-1]), chip))
    )

    normed_two_both = jnp.concatenate([normed_two, normed_two_other])
    ffn_grad = jnp.stack(
        [
            mm("td,tf->df", normed_two_both, jnp.concatenate([own[3], other[3]])),
            mm("td,tf->df", normed_two_both, jnp.concatenate([own[4], other[4]])),
            mm("td,tf->df", jnp.concatenate([cot_own, cot_other]), jnp.concatenate([own[2], other[2]])),
        ]
    )
    ffn_sum = to_float(
        lax.psum_scatter(
            jnp.moveaxis(to_half(ffn_grad).reshape(3, peers, rows, -1), 1, 0),
            "seq",
            scatter_dimension=0,
            tiled=False,
        )
    )
    ffn_sum_grad = jnp.stack([ffn_sum[0], ffn_sum[1]], axis=1)
    down_sum_grad = ffn_sum[2].T

    weighted_two = normed_two_grad * gain_two
    inner_two = jnp.mean(weighted_two * residual, axis=1, keepdims=True)
    residual_grad = (
        to_float(cot_own)
        + scale_two * weighted_two
        - residual * (scale_two * scale_two * scale_two * inner_two)
    )
    gain_two_grad = jnp.sum(normed_two_grad * residual * scale_two, axis=0)
    residual_half = to_half(residual_grad)
    output_grad = mm("td,htv->hdv", residual_half, mixed_half).reshape(2, peers, rows, value_width)
    mixed_grad = mm("td,hdv->htv", residual_half, output_full)
    recurrent_grad, gate_values_grad, group_grad = pull_gate(mixed_grad)
    query_grad_carried, decays_grad_carried, state_in_grad = pull_carried(recurrent_grad)
    later_grad = scan_blocks(block_decay, state_in_grad, True)
    log_block_grad = jnp.sum(state_in * later_grad, axis=2) * block_decay
    query_grad_local, key_grad, value_grad, decays_grad_local = pull_local(
        (recurrent_grad, later_grad)
    )
    query_grad = query_grad_carried + query_grad_local
    decays_grad = decays_grad_carried + decays_grad_local + log_block_grad[:, None, :]
    logit_grad = decays_grad * jax.nn.sigmoid(-logits) / gate_scale
    expand_grad = jnp.concatenate(
        [exact("tr,htc->rhc", rank_values, logit_grad), jnp.sum(logit_grad, axis=1)[None]], axis=0
    )
    rank_grad_part = exact("htc,rhc->rt", logit_grad, expand_columns[:rank_count])
    query_key_grad = to_half(jnp.concatenate([query_grad, key_grad], axis=2))
    value_gate_grad = to_half(jnp.concatenate([value_grad, gate_values_grad], axis=2))
    query_weight_grad = mm("td,htc->hdc", normed, query_key_grad)
    value_weight_grad = mm("td,htc->hdc", normed, value_gate_grad)
    normed_part = to_half(
        mm("htc,hdc->td", query_key_grad, query_full) + mm("htc,hdc->td", value_gate_grad, value_full)
    )
    rank_half = to_half(rank_grad_part + swap(rank_grad_part, "head", 1))
    squeeze_grad = mm("td,rt->dr", normed, rank_half)
    normed_grad = (
        to_float(normed_part)
        + to_float(swap(normed_part, "head", 1))
        + mm("rt,dr->td", rank_half, squeeze_full)
    )
    weighted_one = normed_grad * gain_one
    inner_one = jnp.mean(weighted_one * inputs, axis=1, keepdims=True)
    inputs_grad = (
        residual_grad
        + scale_one * weighted_one
        - inputs * (scale_one * scale_one * scale_one * inner_one)
    )
    gain_one_grad = jnp.sum(normed_grad * inputs * scale_one, axis=0)
    grad_cols = pick(inputs_grad.reshape(segment, 2, 2, column_count), core, 2)
    grad_home = to_float(swap(to_half(pick(grad_cols, 1 - chip, 1)), "head", 2))
    tokens_grad = jnp.stack(ordered(pick(grad_cols, chip, 1), grad_home, chip))

    late_stages = seq_stages[:-1][::-1]
    small_grad = jnp.concatenate([squeeze_grad, gain_one_grad[:, None], gain_two_grad[:, None]], axis=1)
    small_grad = jnp.pad(small_grad, ((0, 0), (0, 128 - small_grad.shape[1])))
    first_grad = jnp.concatenate(
        [query_weight_grad, jnp.broadcast_to(small_grad[None], (2,) + small_grad.shape)], axis=2
    ).reshape(2, peers, rows, -1)
    first_sum = scatter_cube(first_grad, [("seq", 1), ("head", 2)] + late_stages)
    value_sum_grad = scatter_cube(
        value_weight_grad.reshape(2, peers, rows, -1), [("head", 2), ("seq", 1)] + late_stages
    )[:, None, :]
    query_sum_grad = first_sum[:, None, : 2 * key_width]
    squeeze_sum_grad = first_sum[:, 2 * key_width : 2 * key_width + rank_count]
    norms_sum_grad = first_sum[:, 2 * key_width + rank_count : 2 * key_width + rank_count + 2].T
    output_give = to_half(pick(output_grad, 1 - chip))
    output_two = pick(output_grad, chip) + to_float(swap(output_give, "head", 2))
    output_sum_grad = to_float(
        lax.psum_scatter(to_half(output_two), "seq", scatter_dimension=0, tiled=False)
    ).T

    step_float = jnp.asarray(STEP, jnp.float32)
    fix_one = 1.0 - jnp.power(beta_one, step_float)
    second_correction = 1.0 - jnp.power(beta_two, step_float)
    owner_share = (head_index == 0).astype(jnp.float32)
    sharded = [
        (query_weight, query_sum_grad, query_mean, query_square, 1.0),
        (value_weight, value_sum_grad, value_mean, value_square, 1.0),
        (squeeze_weight, squeeze_sum_grad, squeeze_mean, squeeze_square, owner_share),
        (output_weight, output_sum_grad, output_mean, output_square, 1.0),
        (ffn_weight, ffn_sum_grad, ffn_mean, ffn_square, 1.0),
        (down_weight, down_sum_grad, down_mean, down_square, 1.0),
        (norms_weight, norms_sum_grad, norms_mean, norms_square, owner_share),
    ]
    updates = []
    squares = []
    for master, gradient, first_moment, second_moment, weighting in sharded:
        new_first, new_second, update_direction = adam_direction(
            master, gradient, first_moment, second_moment, fix_one, second_correction
        )
        updates.append((master, new_first, new_second, update_direction))
        squares.append(jnp.sum(master * master) * weighting)
        squares.append(jnp.sum(update_direction * update_direction) * weighting)
    total_squares = sum_everywhere(jnp.stack(squares)[None, :])[0]
    expand_pad = jnp.zeros((rank_count + 1, 2, 2, key_width), jnp.float32)
    expand_pad = lax.dynamic_update_index_in_dim(expand_pad, expand_grad, core, 2)
    replicas = jnp.concatenate(
        [expand_pad.reshape(rank_count + 1, -1), jnp.pad(group_grad[None, :], ((0, 0), (0, 4 * key_width - value_width)))]
    )
    replicas = sum_everywhere(replicas)
    expand_total = replicas[: rank_count + 1]
    group_total = replicas[rank_count + 1, :value_width]
    results = []
    for position, packed in enumerate(updates):
        master, new_first, new_second, update_direction = packed
        trust_ratio = jnp.sqrt(total_squares[2 * position]) / (
            jnp.sqrt(total_squares[2 * position + 1]) + eps_adam
        )
        results.append(
            (master - learn_rate * trust_ratio * update_direction, new_first, new_second)
        )
    replicated = []
    for master, gradient, first_moment, second_moment in (
        (expand_weight, expand_total, expand_mean, expand_square),
        (group_weight, group_total, group_mean, group_square),
    ):
        new_first, new_second, update_direction = adam_direction(
            master, gradient, first_moment, second_moment, fix_one, second_correction
        )
        trust_ratio = jnp.sqrt(jnp.sum(master * master)) / (
            jnp.sqrt(jnp.sum(update_direction * update_direction)) + eps_adam
        )
        replicated.append(
            (master - learn_rate * trust_ratio * update_direction, new_first, new_second)
        )
    return (
        block_out,
        tokens_grad,
        results[0][0],
        results[0][1],
        results[0][2],
        results[1][0],
        results[1][1],
        results[1][2],
        results[2][0],
        results[2][1],
        results[2][2],
        replicated[0][0],
        replicated[0][1],
        replicated[0][2],
        replicated[1][0],
        replicated[1][1],
        replicated[1][2],
        results[3][0],
        results[3][1],
        results[3][2],
        results[4][0],
        results[4][1],
        results[4][2],
        results[5][0],
        results[5][1],
        results[5][2],
        results[6][0],
        results[6][1],
        results[6][2],
    )


def solution(mesh):
    in_specs = (
        P(None, "seq", "head"),
        P(None, "seq", "head"),
        P("seq", "head", None),
        P("seq", "head", None),
        P("seq", "head", None),
        P("seq", "head", None),
        P("seq", "head", None),
        P("seq", "head", None),
        P("seq", None),
        P("seq", None),
        P("seq", None),
        P(),
        P(),
        P(),
        P(),
        P(),
        P(),
        P("head", "seq"),
        P("head", "seq"),
        P("head", "seq"),
        P("seq", None, "head"),
        P("seq", None, "head"),
        P("seq", None, "head"),
        P("head", "seq"),
        P("head", "seq"),
        P("head", "seq"),
        P(None, "seq"),
        P(None, "seq"),
        P(None, "seq"),
    )
    out_specs = (
        P(None, "seq", "head"),
        P(None, "seq", "head"),
        P("seq", "head", None),
        P("seq", "head", None),
        P("seq", "head", None),
        P("seq", "head", None),
        P("seq", "head", None),
        P("seq", "head", None),
        P("seq", None),
        P("seq", None),
        P("seq", None),
        P(),
        P(),
        P(),
        P(),
        P(),
        P(),
        P("head", "seq"),
        P("head", "seq"),
        P("head", "seq"),
        P("seq", None, "head"),
        P("seq", None, "head"),
        P("seq", None, "head"),
        P("head", "seq"),
        P("head", "seq"),
        P("head", "seq"),
        P(None, "seq"),
        P(None, "seq"),
        P(None, "seq"),
    )
    return jax.shard_map(
        per_device, mesh=mesh, in_specs=in_specs, out_specs=out_specs, check_vma=False
    )
```

```python
import jax
import jax.numpy as jnp
from jax import lax
from jax.experimental import pallas as pl
from jax.experimental.pallas import tpu as pltpu
from jax.sharding import PartitionSpec as P

SPAN = 64
STEP = 10


eps_norm = 1e-06
gate_scale = 16.0
beta_one = 0.9
beta_two = 0.999
eps_adam = 1e-06
decay_rate = 0.01
learn_rate = 0.5
highest = lax.Precision.HIGHEST


def to_half(value_entries):
    return value_entries.astype(jnp.bfloat16)


def to_float(value_entries):
    return value_entries.astype(jnp.float32)


def mm(pattern, left, right):
    return jnp.einsum(pattern, left, right, preferred_element_type=jnp.float32)


def exact(pattern, left, right):
    return jnp.einsum(pattern, left, right, precision=highest)


def swap(value_entries, axis, bit):
    peers = lax.axis_size(axis)
    return lax.ppermute(value_entries, axis, [(i, i ^ bit) for i in range(peers)])


def bit_of(axis, bit):
    return (lax.axis_index(axis) // bit) % 2


def pick(value_entries, at, axis=0):
    return lax.dynamic_index_in_dim(value_entries, at, axis, keepdims=False)


def ordered(mine, other, upper):
    return (jnp.where(upper == 0, mine, other), jnp.where(upper == 0, other, mine))


def seq_bits():
    bits, bit = [], lax.axis_size("seq") // 2
    while bit:
        bits.append(("seq", bit))
        bit //= 2
    return bits


def cube_rank():
    return [("head", 2)] + seq_bits()


def grow(part, held, stages):
    for stage in stages:
        low, high = ordered(part, swap(part, *stage), bit_of(*stage))
        held = sorted(held + [stage], key=cube_rank().index)
        part = jnp.stack([low, high], axis=held.index(stage))
    return part, held


def grown(part, held):
    return part.reshape((2, lax.axis_size("seq")) + part.shape[len(held) :])


def gather_cube(part, stages):
    return grown(*grow(part, [], stages))


def split(part, held, stage):
    if held is None:
        held = cube_rank()
        part = part.reshape((2,) * len(held) + part.shape[2:])
    at = held.index(stage)
    return pick(part, bit_of(*stage), at), to_half(pick(part, 1 - bit_of(*stage), at))


def shrink(part, held, stages, pin=lambda at, moved: moved):
    if held is None:
        held = cube_rank()
        part = part.reshape((2,) * len(held) + part.shape[2:])
    held = list(held)
    for number, (axis, bit) in enumerate(stages):
        at = held.index((axis, bit))
        held.pop(at)
        upper = bit_of(axis, bit)
        moved = pin(number, swap(to_half(pick(part, 1 - upper, at)), axis, bit))
        part = to_float(pick(part, upper, at)) + to_float(moved)
    return [part, held]


def scatter_cube(part, stages, pin=lambda at, moved: moved):
    return shrink(part, None, stages, pin)[0]


def sum_everywhere(value_entries):
    for axis, bit in [("head", 1), ("head", 2)] + seq_bits()[::-1]:
        value_entries = value_entries + swap(value_entries, axis, bit)
    return value_entries


def after(value_entries, *others):
    return lax.optimization_barrier((value_entries, others))[0]


def scan_blocks(decay, state, reverse):
    before_decay, before_state = (jnp.ones_like(decay), jnp.zeros_like(state))
    heard = []
    for axis, bit in seq_bits()[::-1]:
        upper = bit_of(axis, bit) == (0 if reverse else 1)
        other_decay = swap(decay, axis, bit)
        heard.append(swap(to_half(state), axis, bit))
        other_state = to_float(heard[-1])
        before_state = jnp.where(upper, before_decay * other_state + before_state, before_state)
        before_decay = jnp.where(upper, before_decay * other_decay, before_decay)
        state = jnp.where(
            upper,
            decay * other_state + state,
            other_decay * state + other_state,
        )
        decay = decay * other_decay
    return before_state, heard


TILE = 256
LANES = 128
VALUES = 256
VMEM_LIMIT = 50 * 1024 * 1024


def mul(left, right, left_dim=1, right_dim=0):
    return lax.dot_general(
        to_half(left),
        to_half(right),
        (((left_dim,), (right_dim,)), ((), ())),
        preferred_element_type=jnp.float32,
    )


def mul_exact(left, right, left_dim=1, right_dim=0):
    return lax.dot_general(
        left,
        right,
        (((left_dim,), (right_dim,)), ((), ())),
        precision=highest,
        preferred_element_type=jnp.float32,
    )


def mul_ones(ones, right):
    total = None
    for _ in range(3):
        part = to_half(right)
        right = right - to_float(part)
        product = mul(ones, part)
        total = product if total is None else total + product
    return total


def at_or_after(size):
    row = lax.broadcasted_iota(jnp.int32, (size, size), 0)
    column = lax.broadcasted_iota(jnp.int32, (size, size), 1)
    return row >= column


def ones_where(mask):
    return jnp.where(mask, 1.0, 0.0).astype(jnp.bfloat16)


def log_sigmoid(z):
    decay = jnp.exp(-jnp.abs(z))
    ratio = decay / (2.0 + decay)
    square = ratio * ratio
    series = 1.0 / 15.0
    for odd in (13.0, 11.0, 9.0, 7.0, 5.0, 3.0, 1.0):
        series = series * square + 1.0 / odd
    return jnp.minimum(z, 0.0) - 2.0 * ratio * series


def call(body, steps, ins, outs, reverse=False, scratch=(), cost=0):
    def spec(shape, axis):
        block = tuple(n // steps if d == axis else n for d, n in enumerate(shape))

        def where(i):
            return tuple((steps - 1 - i if reverse else i) if d == axis else 0 for d in range(len(shape)))

        return pl.BlockSpec(block, where)

    return pl.pallas_call(
        body,
        grid=(steps,),
        in_specs=[spec(array.shape, axis) for array, axis in ins],
        out_specs=[spec(shape, axis) for shape, _, axis in outs],
        out_shape=[jax.ShapeDtypeStruct(shape, dtype) for shape, dtype, _ in outs],
        scratch_shapes=list(scratch),
        compiler_params=pltpu.CompilerParams(vmem_limit_bytes=VMEM_LIMIT),
        cost_estimate=pl.CostEstimate(flops=1, bytes_accessed=0, transcendentals=0) if cost else None,
    )(*[array for array, _ in ins])


def heads(width):
    return [slice(h * width, (h + 1) * width) for h in range(2)]


def whole_tile(within):
    spans, offset = [], jnp.zeros_like(within[:1])
    for j in range(TILE // SPAN):
        spans.append(within[j * SPAN : (j + 1) * SPAN] + offset)
        offset = spans[-1][SPAN - 1 :]
    return jnp.concatenate(spans, axis=0)


def first_step(body):
    pl.when(pl.program_id(0) == 0)(body)


def model_rows(ref, h, first, blocks=1):
    parts = [
        ref[h, :, first + LANES * b : first + LANES * (b + 1), :].reshape(-1, LANES)
        for b in range(blocks)
    ]
    return parts[0] if blocks == 1 else jnp.concatenate(parts, axis=1)


def project_kernel(
    x_ref, key_ref, value_ref, expand_ref,
    normed_ref, key_out_ref, value_out_ref, rank_ref, within_ref, slope_ref, state_ref, log_ref, gain_ref, small_ref,
):
    @first_step
    def _():
        state_ref[...] = jnp.zeros_like(state_ref)
        log_ref[...] = jnp.zeros_like(log_ref)
        small_ref[32:] = jnp.zeros_like(small_ref[32:])
        for s in range(key_ref.shape[1]):
            small_ref[:32, s * LANES : (s + 1) * LANES] = key_ref[0, s, LANES : LANES + 32]
        gain_ref[...] = to_float(small_ref[16:24])

    x = to_float(x_ref[...])
    scale = lax.rsqrt(jnp.mean(x * x, axis=1, keepdims=True) + eps_norm)
    normed = to_half(x * scale * gain_ref[0:1])
    normed_ref[...] = normed
    rank_values = mul(normed, small_ref[...], 1, 1)
    column = lax.broadcasted_iota(jnp.int32, rank_values.shape, 1)
    rank_values = jnp.where(column < 16, rank_values, jnp.where(column == 16, 1.0, 0.0))
    rank_ref[...] = rank_values
    logits = mul_exact(rank_values, expand_ref[...])
    decays = log_sigmoid(logits) * (1.0 / gate_scale)
    slope_ref[...] = 1.0 / (gate_scale * (1.0 + jnp.exp(logits)))
    sums = mul_ones(ones_where(at_or_after(TILE)), decays)
    log_ref[...] += sums[TILE - 1 :]
    for j in range(TILE // SPAN):
        part = sums[j * SPAN : (j + 1) * SPAN]
        within_ref[j * SPAN : (j + 1) * SPAN, :] = part - sums[j * SPAN - 1 : j * SPAN] if j else part
    closing = sums[TILE - 1 :]
    rest = jnp.exp(closing - sums)
    decay = jnp.exp(closing)
    for h, (k, v) in enumerate(zip(heads(LANES), heads(VALUES))):
        keys = to_half(mul(normed, model_rows(key_ref, h, 0)))
        key_out_ref[:, k] = keys
        values = to_half(mul(normed, value_ref[h]))
        value_out_ref[:, v] = values
        state_ref[h] = state_ref[h] * decay[:, k] + mul(values, to_float(keys) * rest[:, k], 0, 0)


def project_late_kernel(normed_ref, weight_ref, query_ref, gate_ref):
    normed = normed_ref[...]
    for h, (k, v) in enumerate(zip(heads(LANES), heads(VALUES))):
        query_ref[:, k] = to_half(mul(normed, model_rows(weight_ref, h, 0)))
        gate_ref[:, v] = mul(normed, model_rows(weight_ref, h, LANES, 2))


def load_output(late_ref, output_ref):
    for s in range(late_ref.shape[1]):
        output_ref[:, :, s * LANES : (s + 1) * LANES] = late_ref[:, s, 3 * LANES :]


def forward_kernel(
    query_ref, key_ref, value_ref, gate_ref, within_ref, incoming_ref, group_ref, late_ref,
    recurrent_ref, start_ref, mixed_ref, part_ref, state_ref, output_ref,
):
    @first_step
    def _():
        state_ref[...] = incoming_ref[...]
        load_output(late_ref, output_ref)

    causal = at_or_after(SPAN)
    total = None
    for h, (k, v) in enumerate(zip(heads(LANES), heads(VALUES))):
        state = state_ref[h]
        outs = []
        for j in range(TILE // SPAN):
            span = pl.ds(j * SPAN, SPAN)
            within = within_ref[span, k]
            closing = within[SPAN - 1 :]
            values = value_ref[span, v]
            queries = to_half(to_float(query_ref[span, k]) * jnp.exp(within))
            keys = to_float(key_ref[span, k])
            start = to_half(state)
            start_ref[j, h] = start
            scores = jnp.where(causal, mul(queries, keys * jnp.exp(-within), 1, 1), 0.0)
            outs.append(mul(scores, values) + mul(queries, start, 1, 1))
            state = state * jnp.exp(closing) + mul(values, keys * jnp.exp(closing - within), 0, 0)
        state_ref[h] = state
        recurrent = jnp.concatenate(outs, axis=0) * LANES ** (-0.5)
        recurrent_ref[:, v] = recurrent
        scale = lax.rsqrt(jnp.mean(recurrent * recurrent, axis=1, keepdims=True) + eps_norm)
        gate = gate_ref[:, v]
        mixed = to_half(recurrent * scale * group_ref[...] * (gate * jax.nn.sigmoid(gate)))
        mixed_ref[:, v] = mixed
        part = mul(mixed, output_ref[h])
        total = part if total is None else total + part
    part_ref[...] = to_half(total)


def residual_kernel(x_ref, mine_ref, other_ref, gain_ref, residual_ref, normed_ref):
    residual = to_float(x_ref[...]) + (to_float(mine_ref[...]) + to_float(other_ref[...]))
    scale = lax.rsqrt(jnp.mean(residual * residual, axis=1, keepdims=True) + eps_norm)
    residual_ref[...] = residual
    normed_ref[...] = to_half(residual * scale * gain_ref[1:2])


def feed_forward_kernel(
    normed_ref, cot_ref, weight_ref,
    hidden_ref, gate_grad_ref, up_grad_ref, out_ref, rows_grad_ref, all_ref,
):
    width = weight_ref.shape[2]

    @first_step
    def _():
        all_ref[:, width:] = jnp.zeros_like(all_ref[:, width:])
        for s in range(weight_ref.shape[0]):
            all_ref[:, :width, s * LANES : (s + 1) * LANES] = weight_ref[s]

    normed = normed_ref[...]
    gate = mul(normed, all_ref[0], 1, 1)
    up = mul(normed, all_ref[1], 1, 1)
    hidden_grad = mul(cot_ref[...], all_ref[2], 1, 1)
    sigmoid = jax.nn.sigmoid(gate)
    silu = gate * sigmoid
    hidden = to_half(silu * up)
    hidden_ref[...] = hidden.T
    gate_grad = to_half(hidden_grad * up * sigmoid * (1.0 + gate * (1.0 - sigmoid)))
    gate_grad_ref[...] = gate_grad.T
    up_grad = to_half(hidden_grad * silu)
    up_grad_ref[...] = up_grad.T
    rows_grad_ref[...] = to_half(mul(gate_grad, all_ref[0]) + mul(up_grad, all_ref[1]))
    out_ref[...] = to_half(mul(hidden, all_ref[2]))


def feed_forward_weights_kernel(
    own_ref, other_ref, cot_own_ref, cot_other_ref,
    gate_own_ref, gate_other_ref, up_own_ref, up_other_ref, hidden_own_ref, hidden_other_ref,
    out_ref,
):
    width = out_ref.shape[2]
    for i, (left, left_other, right, right_other) in enumerate(
        [
            (gate_own_ref, gate_other_ref, own_ref, other_ref),
            (up_own_ref, up_other_ref, own_ref, other_ref),
            (hidden_own_ref, hidden_other_ref, cot_own_ref, cot_other_ref),
        ]
    ):
        total = to_half(mul(left[...], right[...]) + mul(left_other[...], right_other[...]))
        for s in range(out_ref.shape[0]):
            out_ref[s, i] = total[:width, s * LANES : (s + 1) * LANES]


def residual_backward_kernel(
    residual_ref, cot_ref, mine_ref, other_ref, home_ref, gain_ref,
    grad_ref, half_ref, gain_grad_ref,
):
    @first_step
    def _():
        gain_grad_ref[...] = jnp.zeros_like(gain_grad_ref)

    residual = residual_ref[...]
    scale = lax.rsqrt(jnp.mean(residual * residual, axis=1, keepdims=True) + eps_norm)
    normed = residual * scale
    pulled = to_float(mine_ref[...]) + to_float(other_ref[...]) + to_float(home_ref[...])
    gain_grad_ref[...] += jnp.sum(pulled * normed, axis=0, keepdims=True)
    weighted = pulled * gain_ref[1:2]
    grad = to_float(cot_ref[...]) + scale * (
        weighted - normed * jnp.mean(weighted * normed, axis=1, keepdims=True)
    )
    grad_ref[...] = grad
    half_ref[...] = to_half(grad)


def gate_backward_kernel(
    grad_ref, late_ref, recurrent_ref, gate_ref, query_ref, within_ref, group_ref,
    recurrent_grad_ref, gate_grad_ref, group_grad_ref, state_grad_ref, output_ref,
):
    @first_step
    def _():
        load_output(late_ref, output_ref)
        group_grad_ref[...] = jnp.zeros_like(group_grad_ref)
        state_grad_ref[...] = jnp.zeros_like(state_grad_ref)

    for h, (k, v) in enumerate(zip(heads(LANES), heads(VALUES))):
        mixed_grad = mul(grad_ref[...], output_ref[h], 1, 1)
        recurrent = recurrent_ref[:, v]
        gate = gate_ref[:, v]
        scale = lax.rsqrt(jnp.mean(recurrent * recurrent, axis=1, keepdims=True) + eps_norm)
        sigmoid = jax.nn.sigmoid(gate)
        silu = gate * sigmoid
        normed = recurrent * scale
        group = group_ref[...]
        pulled = mixed_grad * normed
        group_grad_ref[...] += jnp.sum(pulled * silu, axis=0, keepdims=True)
        gate_grad_ref[:, v] = to_half(pulled * group * sigmoid * (1.0 + gate * (1.0 - sigmoid)))
        weighted = mixed_grad * group * silu
        recurrent_grad = scale * (weighted - normed * jnp.mean(weighted * normed, axis=1, keepdims=True))
        recurrent_grad = to_half(recurrent_grad * LANES ** (-0.5))
        recurrent_grad_ref[:, v] = recurrent_grad
        sums = whole_tile(within_ref[:, k])
        queries = to_float(query_ref[:, k]) * jnp.exp(sums)
        state_grad_ref[h] = state_grad_ref[h] * jnp.exp(sums[TILE - 1 :]) + mul(recurrent_grad, queries, 0, 0)


def query_backward_kernel(
    query_ref, key_ref, value_ref, within_ref, recurrent_grad_ref, start_ref, gate_grad_ref, weight_ref,
    query_grad_ref, kept_ref, normed_grad_ref,
):
    causal = at_or_after(SPAN)
    total = None
    for h, (k, v) in enumerate(zip(heads(LANES), heads(VALUES))):
        for j in range(TILE // SPAN):
            span = pl.ds(j * SPAN, SPAN)
            within = within_ref[span, k]
            pulled = recurrent_grad_ref[span, v]
            keys_in = to_float(key_ref[span, k]) * jnp.exp(-within)
            scores_grad = jnp.where(causal, mul(pulled, value_ref[span, v], 1, 1), 0.0)
            query_grad = (mul(scores_grad, keys_in) + mul(pulled, start_ref[j, h])) * jnp.exp(within)
            query_grad_ref[span, k] = to_half(query_grad)
            kept_ref[span, k] = query_grad * to_float(query_ref[span, k])
        part = mul(query_grad_ref[:, k], model_rows(weight_ref, h, 0), 1, 1) + mul(
            gate_grad_ref[:, v], model_rows(weight_ref, h, LANES, 2), 1, 1
        )
        total = part if total is None else total + part
    normed_grad_ref[...] = total


def backward_kernel(
    query_ref, key_ref, value_ref, within_ref, recurrent_grad_ref, start_ref, slope_ref, rank_ref, kept_ref,
    normed_grad_ref, key_weight_ref, value_weight_ref, expand_ref, later_ref,
    key_grad_ref, value_grad_ref, rank_grad_ref, expand_grad_ref, part_ref, state_grad_ref,
):
    @first_step
    def _():
        state_grad_ref[...] = later_ref[...]
        expand_grad_ref[...] = jnp.zeros_like(expand_grad_ref)

    causal = at_or_after(SPAN)
    last = lax.broadcasted_iota(jnp.int32, (SPAN, LANES), 0) == SPAN - 1
    until = ones_where(
        lax.broadcasted_iota(jnp.int32, (SPAN, SPAN), 0) <= lax.broadcasted_iota(jnp.int32, (SPAN, SPAN), 1)
    )
    total = normed_grad_ref[...]
    logit_grads = []
    for h, (k, v) in enumerate(zip(heads(LANES), heads(VALUES))):
        later = state_grad_ref[h]
        spans = []
        for j in reversed(range(TILE // SPAN)):
            span = pl.ds(j * SPAN, SPAN)
            within = within_ref[span, k]
            closing = within[SPAN - 1 :]
            values = value_ref[span, v]
            pulled = recurrent_grad_ref[span, v]
            keys = to_float(key_ref[span, k])
            shrink, rest = (jnp.exp(-within), jnp.exp(closing - within))
            queries = to_half(to_float(query_ref[span, k]) * jnp.exp(within))
            keys_in = keys * shrink
            keys_out = keys * rest
            later_half = to_half(later)
            scores = jnp.where(causal, mul(queries, keys_in, 1, 1), 0.0)
            scores_grad = jnp.where(causal, mul(pulled, values, 1, 1), 0.0)
            keys_in_grad = mul(scores_grad, queries, 0, 0)
            keys_out_grad = mul(values, later_half)
            value_grad_ref[span, v] = to_half(mul(scores, pulled, 0, 0) + mul(keys_out, later_half, 1, 1))
            key_grad_ref[span, k] = to_half(keys_in_grad * shrink + keys_out_grad * rest)
            kept = keys_out_grad * keys_out
            sums_grad = kept_ref[span, k] - keys_in_grad * keys_in - kept
            closing_grad = jnp.sum(kept, axis=0, keepdims=True) + jnp.sum(
                later * to_float(start_ref[j, h]), axis=0, keepdims=True
            ) * jnp.exp(closing)
            spans.append(mul_ones(until, sums_grad + jnp.where(last, closing_grad, 0.0)))
            later = later * jnp.exp(closing) + mul(pulled, queries, 0, 0)
        state_grad_ref[h] = later
        logit_grads.append(jnp.concatenate(spans[::-1], axis=0) * slope_ref[:, k])
        total = total + (
            mul(key_grad_ref[:, k], model_rows(key_weight_ref, h, 0), 1, 1)
            + mul(value_grad_ref[:, v], value_weight_ref[h], 1, 1)
        )
    part_ref[...] = to_half(total)
    logit_grad = jnp.concatenate(logit_grads, axis=1)
    rank_grad_ref[...] = mul_exact(expand_ref[:16], logit_grad, 1, 1)
    expand_grad_ref[...] += mul_exact(rank_ref[...], logit_grad, 0, 0)[:24]


def store_rows(out_ref, h, first, total):
    for s in range(out_ref.shape[1]):
        for b in range(total.shape[1] // LANES):
            out_ref[h, s, first + LANES * b : first + LANES * (b + 1)] = to_half(
                total[s * LANES : (s + 1) * LANES, b * LANES : (b + 1) * LANES]
            )


def weights_kernel(rows_ref, first_ref, second_ref, out_ref):
    rows = rows_ref[...]
    for h, (k, v) in enumerate(zip(heads(LANES), heads(VALUES))):
        store_rows(out_ref, h, 0, mul(rows, first_ref[:, k]))
        store_rows(out_ref, h, LANES, mul(rows, second_ref[:, v]))


def late_weights_kernel(rows_ref, query_ref, gate_ref, mixed_ref, grad_ref, out_ref):
    weights_kernel(rows_ref, query_ref, gate_ref, out_ref)
    for h, v in enumerate(heads(VALUES)):
        total = mul(mixed_ref[v, :], grad_ref[...])
        for s in range(out_ref.shape[1]):
            out_ref[h, s, 3 * LANES :] = to_half(total[:, s * LANES : (s + 1) * LANES])


def inputs_backward_kernel(
    core_ref, x_ref, grad_ref, mine_ref, other_ref, rank_grad_ref, small_ref, gain_ref, normed_ref,
    out_ref, gain_grad_ref, squeeze_grad_ref,
):
    @first_step
    def _():
        gain_grad_ref[...] = jnp.zeros_like(gain_grad_ref)
        squeeze_grad_ref[...] = jnp.zeros_like(squeeze_grad_ref)

    rank_grad = to_half(rank_grad_ref[...])
    x = to_float(x_ref[...])
    scale = lax.rsqrt(jnp.mean(x * x, axis=1, keepdims=True) + eps_norm)
    normed = x * scale
    pulled = (
        to_float(mine_ref[...])
        + to_float(other_ref[...])
        + mul(rank_grad, small_ref[:16], 0, 0)
    )
    squeeze_grad_ref[...] += mul(rank_grad, normed_ref[...])
    gain_grad_ref[...] += jnp.sum(pulled * normed, axis=0, keepdims=True)
    weighted = pulled * gain_ref[0:1]
    grad = grad_ref[...] + scale * (weighted - normed * jnp.mean(weighted * normed, axis=1, keepdims=True))
    columns = out_ref.shape[2]
    for b in range(2):
        low, high = (grad[:, (2 * b + i) * columns : (2 * b + i + 1) * columns] for i in range(2))
        out_ref[b] = jnp.where(core_ref[0, 0] == 0, low, high)


def adam_kernel(count, joins, *refs):
    grads = refs[: len(refs) - 6 * count - 2]
    refs = refs[len(grads) :]
    share, ins, outs = refs[0], refs[1 : 1 + 3 * count], refs[1 + 3 * count :]
    squares = outs[3 * count]
    squares[...] = jnp.zeros_like(squares)
    for p, (join, shared) in enumerate(joins):
        gradient = to_float(join(*grads))
        master, first, second = (ref[...].reshape(gradient.shape) for ref in ins[3 * p : 3 * p + 3])
        new_first, new_second, direction = adam_direction(master, gradient, first, second)
        for ref, value in zip(outs[3 * p : 3 * p + 3], (new_first, new_second, direction)):
            ref[...] = value.reshape(ref.shape)
        for row, value in ((p, master), (8 + p, direction)):
            total = value * value
            while total.ndim > 2:
                total = jnp.sum(total, axis=0)
            total = jnp.sum(jnp.sum(total, axis=0, keepdims=True), axis=1, keepdims=True)
            if shared:
                total = total * share[0:1, 0:1]
            squares[row : row + 1] = jnp.broadcast_to(total, (1, LANES))


def trust_kernel(rows, squares_ref, *refs):
    count = len(rows)
    for p, row in enumerate(rows):
        master, direction, out = refs[p], refs[count + p], refs[2 * count + p]
        norm = jnp.sqrt(squares_ref[row : row + 1, 0:1])
        ratio = norm / (jnp.sqrt(squares_ref[row + 8 : row + 9, 0:1]) + eps_adam)
        shape = (1,) * len(master.shape)
        out[...] = master[...] - (learn_rate * ratio).reshape(shape) * direction[...]


def whole_call(body, ins, outs):
    return pl.pallas_call(
        body,
        out_shape=[jax.ShapeDtypeStruct(shape, jnp.float32) for shape in outs],
        compiler_params=pltpu.CompilerParams(vmem_limit_bytes=VMEM_LIMIT),
        cost_estimate=pl.CostEstimate(flops=1, bytes_accessed=0, transcendentals=0),
    )(*ins)


def adam_group(share, grads, joins, params):
    count = len(params)
    outs = []
    for param in params:
        outs += [param[0].shape] * 3
    results = whole_call(
        lambda *refs: adam_kernel(count, joins, *refs),
        list(grads) + [share] + [array for param in params for array in param],
        outs + [(16, LANES)],
    )
    return [tuple(results[3 * p : 3 * p + 3]) for p in range(count)], results[-1]


def adam_direction(master, gradient, first_moment, second_moment):
    fix_one = 1.0 - beta_one**STEP
    second_correction = 1.0 - beta_two**STEP
    new_first = beta_one * first_moment + (1.0 - beta_one) * gradient
    new_second = beta_two * second_moment + (1.0 - beta_two) * gradient * gradient
    update_direction = (
        new_first * (1.0 / fix_one) / (jnp.sqrt(new_second * (1.0 / second_correction)) + eps_adam)
        + decay_rate * master
    )
    return (new_first, new_second, update_direction)


def per_device(
    tokens,
    cotangent,
    query_weight,
    query_mean,
    query_square,
    value_weight,
    value_mean,
    value_square,
    squeeze_weight,
    squeeze_mean,
    squeeze_square,
    expand_weight,
    expand_mean,
    expand_square,
    group_weight,
    group_mean,
    group_square,
    output_weight,
    output_mean,
    output_square,
    ffn_weight,
    ffn_mean,
    ffn_square,
    down_weight,
    down_mean,
    down_square,
    norms_weight,
    norms_mean,
    norms_square,
):
    sequences, segment, column_count = tokens.shape
    head_index = lax.axis_index("head")
    chip, core = (head_index // 2, head_index % 2)
    rows = query_weight.shape[0]
    peers = lax.axis_size("seq")
    seq_index = lax.axis_index("seq")
    model_width = rows * peers
    key_width = query_weight.shape[2] // 2
    value_width = value_weight.shape[2] // 2
    ffn_width = ffn_weight.shape[2]
    ffn_padded = -(-ffn_width // 256) * 256
    rank_count = squeeze_weight.shape[1]
    half_segment = segment // 2
    steps = segment // TILE
    half, full = (jnp.bfloat16, jnp.float32)
    aligned = rows % LANES == 0
    blocks = model_width // LANES
    along = seq_bits()[:-1]
    beside = ("seq", 1)
    across = ("head", 2)

    def column_pair(a):
        parts = [a[:, i * column_count : (i + 1) * column_count] for i in range(4)]
        return [jnp.where(core == 0, parts[2 * b], parts[2 * b + 1]) for b in range(2)]

    def other_pair(a):
        parts = [a[:, i * column_count : (i + 1) * column_count] for i in range(4)]
        return [jnp.where(core == 0, parts[2 * b + 1], parts[2 * b]) for b in range(2)]

    def full_rows(mine, other):
        pair = jnp.stack(ordered(mine, other, chip))
        low, high = ordered(pair, swap(pair, "head", 1), core)
        return jnp.concatenate([low[0], high[0], low[1], high[1]], axis=-1)

    ffn_mine = jnp.concatenate([jnp.moveaxis(ffn_weight, 0, 2), down_weight[None]])
    ffn_mine = to_half(ffn_mine if aligned else jnp.moveaxis(ffn_mine, 2, 1))
    small_mine = jnp.concatenate(
        [
            squeeze_weight.T,
            jnp.zeros((16 - rank_count, rows), jnp.float32),
            norms_weight,
            jnp.zeros((14, rows), jnp.float32),
        ]
    )
    key_mine = query_weight[:, 0, key_width:]
    value_mine = to_half(value_weight[:, 0, :value_width])
    late_mine = jnp.concatenate(
        [
            query_weight[:, 0, :key_width],
            value_weight[:, 0, value_width : value_width + LANES],
            value_weight[:, 0, value_width + LANES :],
        ]
    )
    tokens_moved = swap(pick(tokens, 1 - chip), *across)
    value_mine, ffn_mine = lax.optimization_barrier((value_mine, ffn_mine))
    ffn_all = lax.all_gather(ffn_mine, "seq", axis=0)
    if not aligned:
        ffn_all = ffn_all.reshape(blocks, LANES // rows, 3, rows, ffn_width)
        ffn_all = ffn_all.transpose(0, 2, 4, 1, 3).reshape(blocks, 3, ffn_width, LANES)

    input_half = full_rows(pick(tokens, chip), tokens_moved)
    value_part, held = grow(value_mine, [], along)
    if aligned:
        key_part, held = grow(to_half(jnp.concatenate([key_mine, small_mine])), [], along)
        late_mine = to_half(jnp.concatenate([late_mine, output_weight]))
        late_part, late_held = grow(after(late_mine, key_part, value_part), [], along[:1])
        key_all = grown(*grow(key_part, held, [across, beside]))
        value_part, value_held = grow(value_part, held, [beside])
        late_part, _ = grow(after(late_part, value_part), late_held, along[1:])
        value_part = after(value_part, input_half)
        value_full = grown(*grow(value_part, value_held, [across])).reshape(
            2, model_width, value_width
        )
        late_part, key_all, value_full = lax.optimization_barrier((late_part, key_all, value_full))
        cut = 5 * LANES // 2
        late_halves = [
            grow(late_part[..., :cut, :], held, [across]),
            grow(late_part[..., cut:, :], held, [beside]),
        ]
    else:
        value_full = grown(*grow(value_part, held, [beside, across])).reshape(
            2, model_width, value_width
        )
        stages = along + [across, beside]
        small_all = gather_cube(to_half(small_mine.T), stages)
        small_all = jnp.moveaxis(small_all.reshape(2, blocks, LANES, 32), 3, 2)
        key_all = gather_cube(to_half(key_mine), stages).reshape(2, blocks, LANES, key_width)
        key_all = jnp.concatenate([key_all, small_all], axis=2)
        late_all = gather_cube(to_half(late_mine), stages).reshape(2, peers, 3, rows, LANES)
        late_all = jnp.moveaxis(late_all, 2, 1).reshape(2, 3, blocks, LANES, LANES)
        late_all = jnp.moveaxis(late_all, 1, 2).reshape(2, blocks, 3 * LANES, LANES)
        output_all = gather_cube(to_half(output_weight.T), stages)
        output_all = jnp.moveaxis(output_all.reshape(2, blocks, LANES, value_width), 3, 2)
        late_all = jnp.concatenate([late_all, output_all], axis=2)

    expand_columns = pick(expand_weight.reshape(rank_count + 1, 2, 2, key_width), core, 2)
    expand_columns = jnp.pad(
        expand_columns.reshape(rank_count + 1, 2 * key_width), ((0, LANES - 1 - rank_count), (0, 0))
    )
    (
        normed, keys, value_entries, rank_values, within, slope, block_state, log_block, gains, small_full,
    ) = call(
        project_kernel,
        steps,
        [(input_half, 0), (key_all, None), (value_full, None), (expand_columns, None)],
        [
            ((segment, model_width), half, 0),
            ((segment, 2 * key_width), half, 0),
            ((segment, 2 * value_width), half, 0),
            ((segment, LANES), full, 0),
            ((segment, 2 * key_width), full, 0),
            ((segment, 2 * key_width), full, 0),
            ((2, value_width, key_width), full, None),
            ((1, 2 * key_width), full, None),
            ((8, model_width), full, None),
            ((LANES, model_width), half, None),
        ],
        cost=4,
    )
    block_decay = jnp.exp(log_block).reshape(2, 1, key_width)
    if aligned:
        block_state, late_halves = lax.optimization_barrier((block_state, [a for a, _ in late_halves]))
        late_helds = [sorted(held + [link], key=cube_rank().index) for link in (across, beside)]
    state_in, heard = scan_blocks(block_decay, block_state, False)
    if aligned:
        late_halves = [(after(late_halves[0], heard[0]), late_helds[0]), (late_halves[1], late_helds[1])]
        late_all = jnp.concatenate(
            [
                grown(*grow(*late_halves[0], [beside])),
                grown(*grow(*late_halves[1], [across])),
            ],
            axis=2,
        )
    queries, gate_values = call(
        project_late_kernel,
        steps,
        [(normed, 0), (late_all, None)],
        [((segment, 2 * key_width), half, 0), ((segment, 2 * value_width), full, 0)],
        cost=4,
    )
    cot_moved = swap(after(cotangent, late_all), *across)
    recurrent, starts, mixed_half, mixer_part = call(
        forward_kernel,
        steps,
        [
            (queries, 0),
            (keys, 0),
            (value_entries, 0),
            (gate_values, 0),
            (within, 0),
            (state_in, None),
            (group_weight[None, :], None),
            (late_all, None),
        ],
        [
            ((segment, 2 * value_width), full, 0),
            ((segment // SPAN, 2, value_width, key_width), half, 0),
            ((segment, 2 * value_width), half, 0),
            ((segment, model_width), half, 0),
        ],
        scratch=[
            pltpu.VMEM((2, value_width, key_width), jnp.float32),
            pltpu.VMEM((2, value_width, model_width), jnp.bfloat16),
        ],
        cost=4,
    )
    cot_moved = after(cot_moved, mixer_part)
    cot_own = full_rows(pick(cotangent, chip), pick(cot_moved, chip))
    cot_other = full_rows(pick(cotangent, 1 - chip), pick(cot_moved, 1 - chip))
    residual, normed_two = call(
        residual_kernel,
        steps,
        [(input_half, 0), (mixer_part, 0), (swap(mixer_part, "head", 1), 0), (gains, None)],
        [((segment, model_width), full, 0), ((segment, model_width), half, 0)],
        cost=2,
    )

    moved = swap(lax.dynamic_slice_in_dim(normed_two, core * half_segment, half_segment, 0), *across)

    def feed_forward(normed_rows, cot_rows):
        return call(
            feed_forward_kernel,
            steps,
            [(normed_rows, 0), (cot_rows, 0), (ffn_all, None)],
            [((ffn_padded, segment), half, 1)] * 3 + [((segment, model_width), half, 0)] * 2,
            scratch=[pltpu.VMEM((3, ffn_padded, model_width), jnp.bfloat16)],
            cost=12,
        )

    own = feed_forward(normed_two, cot_own)
    normed_t, mixed_t = (after(normed, own[0]).T, after(mixed_half, own[0]).T)
    moved, own, normed_t, mixed_t = lax.optimization_barrier((moved, own, normed_t, mixed_t))
    normed_two_other = jnp.concatenate(ordered(moved, swap(moved, "head", 1), core), axis=0)
    other = feed_forward(normed_two_other, cot_other)
    other_rows = other[4].reshape(2, half_segment, model_width)
    other_sum = to_half(
        to_float(pick(other_rows, core)) + to_float(swap(pick(other_rows, 1 - core), "head", 1))
    )
    home = swap(other_sum, *across)
    (ffn_grad,) = call(
        feed_forward_weights_kernel,
        4,
        [
            (normed_two, 1),
            (normed_two_other, 1),
            (cot_own, 1),
            (cot_other, 1),
            (own[1], None),
            (other[1], None),
            (own[2], None),
            (other[2], None),
            (own[0], None),
            (other[0], None),
        ],
        [((blocks, 3, ffn_width, LANES), half, 0)],
        cost=12,
    )
    own_grad = after(own[4], other_sum)
    own_beside = swap(own_grad, "head", 1)
    home, ffn_grad, own_beside = lax.optimization_barrier((home, ffn_grad, own_beside))
    home_full = jnp.concatenate(ordered(home, swap(home, "head", 1), core), axis=0)
    residual_grad, residual_half, gain_two_grad = call(
        residual_backward_kernel,
        steps,
        [
            (residual, 0),
            (cot_own, 0),
            (own_grad, 0),
            (own_beside, 0),
            (home_full, 0),
            (gains, None),
        ],
        [
            ((segment, model_width), full, 0),
            ((segment, model_width), half, 0),
            ((1, model_width), full, None),
        ],
        cost=2,
    )
    if not aligned:
        ffn_grad = ffn_grad.reshape(blocks, 3, ffn_width, LANES // rows, rows)
        ffn_grad = ffn_grad.transpose(0, 3, 1, 4, 2).reshape(peers, 3, rows, ffn_width)
    ffn_sum = lax.psum_scatter(ffn_grad, "seq", scatter_dimension=0, tiled=False)
    if not aligned:
        ffn_sum = jnp.moveaxis(ffn_sum, 1, 2)

    recurrent_grad, gate_grad, group_grad, state_in_grad = call(
        gate_backward_kernel,
        steps,
        [
            (residual_half, 0),
            (late_all, None),
            (recurrent, 0),
            (gate_values, 0),
            (queries, 0),
            (within, 0),
            (group_weight[None, :], None),
        ],
        [
            ((segment, 2 * value_width), half, 0),
            ((segment, 2 * value_width), half, 0),
            ((1, value_width), full, None),
            ((2, value_width, key_width), full, None),
        ],
        reverse=True,
        scratch=[pltpu.VMEM((2, value_width, model_width), jnp.bfloat16)],
        cost=3,
    )
    later_grad, heard = scan_blocks(block_decay, state_in_grad, True)
    own_out, other_out, residual_cols = after((own[3], other[3], residual), residual_half)
    give = jnp.stack([jnp.stack(other_pair(a)) for a in (own_out, other_out)])
    out_beside = swap(give, "head", 1)
    own_out, other_out, residual_cols = after((own_out, other_out, residual_cols), state_in_grad)
    keep = jnp.stack([jnp.stack(column_pair(a)) for a in (own_out, other_out)])
    out_rows = to_float(keep) + to_float(out_beside)
    residual_cols = jnp.stack(column_pair(residual_cols))
    out_rows = out_rows + jnp.stack([residual_cols, jnp.zeros_like(residual_cols)])
    out_give = to_half(pick(out_rows, 1 - chip, 1))
    out_mine = pick(out_rows, chip, 1)
    gate_grad, out_give, out_mine = lax.optimization_barrier((gate_grad, out_give, out_mine))
    out_moved = swap(out_give, *across)
    query_grad, kept, normed_grad = call(
        query_backward_kernel,
        steps,
        [
            (queries, 0),
            (keys, 0),
            (value_entries, 0),
            (within, 0),
            (recurrent_grad, 0),
            (starts, 0),
            (gate_grad, 0),
            (late_all, None),
        ],
        [
            ((segment, 2 * key_width), half, 0),
            ((segment, 2 * key_width), full, 0),
            ((segment, model_width), full, 0),
        ],
        cost=4,
    )
    (late_grad,) = call(
        late_weights_kernel,
        4,
        [(normed_t, 0), (query_grad, None), (gate_grad, None), (mixed_t, None), (residual_half, 1)],
        [((2, blocks, 5 * LANES, LANES), half, 1)],
        cost=4,
    )
    late_grad, later_grad, out_moved = lax.optimization_barrier((late_grad, later_grad, out_moved))
    back = along[::-1]
    if aligned:
        cut = 5 * LANES // 2
        late_splits = [
            split(late_grad[:, :, :cut], None, beside),
            split(late_grad[:, :, cut:], None, across),
        ]
        later_grad, late_splits = lax.optimization_barrier((later_grad, late_splits))
        late_moved = [swap(late_splits[0][1], *beside), swap(late_splits[1][1], *across)]
    key_grad, value_grad, rank_grad_part, expand_grad, normed_part = call(
        backward_kernel,
        steps,
        [
            (queries, 0),
            (keys, 0),
            (value_entries, 0),
            (within, 0),
            (recurrent_grad, 0),
            (starts, 0),
            (slope, 0),
            (rank_values, 0),
            (kept, 0),
            (normed_grad, 0),
            (key_all, None),
            (value_full, None),
            (expand_columns, None),
            (later_grad, None),
        ],
        [
            ((segment, 2 * key_width), half, 0),
            ((segment, 2 * value_width), half, 0),
            ((rank_count, segment), full, 1),
            ((24, 2 * key_width), full, None),
            ((segment, model_width), half, 0),
        ],
        reverse=True,
        scratch=[pltpu.VMEM((2, value_width, key_width), jnp.float32)],
        cost=5,
    )
    if aligned:
        key_grad, value_grad, normed_part, rank_grad_part, late_moved = lax.optimization_barrier(
            (key_grad, value_grad, normed_part, rank_grad_part, late_moved)
        )
        late_held = [[link for link in cube_rank() if link != gone] for gone in (beside, across)]
        late_splits = [
            split(to_float(splits[0]) + to_float(moved), held, link)
            for splits, moved, held, link in zip(
                late_splits, late_moved, late_held, (across, beside)
            )
        ]
    normed_beside, rank_beside = (swap(normed_part, "head", 1), swap(rank_grad_part, "head", 1))
    (state_weight_grad,) = call(
        weights_kernel,
        4,
        [(normed_t, 0), (key_grad, None), (value_grad, None)],
        [((2, blocks, 3 * LANES, LANES), half, 1)],
        cost=3,
    )
    normed_beside, rank_beside, state_weight_grad = lax.optimization_barrier(
        (normed_beside, rank_beside, state_weight_grad)
    )
    rank_grad = rank_grad_part + rank_beside
    grad_cols, gain_one_grad, squeeze_grad = call(
        inputs_backward_kernel,
        steps,
        [
            (core.reshape(1, 1), None),
            (input_half, 0),
            (residual_grad, 0),
            (normed_part, 0),
            (normed_beside, 0),
            (rank_grad, 1),
            (small_full, None),
            (gains, None),
            (normed, 0),
        ],
        [
            ((2, segment, column_count), full, 1),
            ((1, model_width), full, None),
            ((rank_count, model_width), full, None),
        ],
        cost=2,
    )
    if aligned:
        heard = []

        def listen(number, moved):
            if number == 0:
                moved = after(moved, gain_one_grad)
            heard.append(moved)
            return moved

        state_sum = scatter_cube(state_weight_grad, [across, beside] + back, listen)
        late_moved = [swap(late_splits[0][1], *across), swap(late_splits[1][1], *beside)]
        late_part = jnp.concatenate(
            [to_float(splits[0]) + to_float(moved) for splits, moved in zip(late_splits, late_moved)],
            axis=-2,
        )
        late_part = after(late_part, gain_one_grad)
        late_sum = shrink(late_part, along, back)[0]
        output_sum_grad = late_sum[3 * LANES :]
        grad_give = after(pick(grad_cols, 1 - chip), heard[0])
    else:

        def split_rows(a):
            a = a.reshape(2, blocks, 3, LANES // rows, rows, LANES)
            return jnp.moveaxis(a, 3, 2).reshape(2, peers, 3 * rows, LANES)

        late_sum = scatter_cube(split_rows(late_grad[:, :, : 3 * LANES]), [beside, across] + back)
        state_sum = scatter_cube(split_rows(state_weight_grad), [across, beside] + back)
        output_grad = late_grad[:, :, 3 * LANES :].reshape(2, blocks, value_width, LANES // rows, rows)
        output_grad = output_grad.transpose(0, 1, 3, 4, 2).reshape(2, peers, rows, value_width)
        output_sum_grad = scatter_cube(output_grad, [beside, across] + back).T
        grad_give = pick(grad_cols, 1 - chip)
    grad_home = to_float(swap(to_half(grad_give), *across))
    tokens_grad = jnp.stack(ordered(pick(grad_cols, chip), grad_home, chip))
    out_home = to_float(out_moved)
    block_out = to_half(jnp.stack(ordered(out_mine[0] + out_home[1], out_mine[1] + out_home[0], chip)))

    expand_pad = jnp.zeros((rank_count + 1, 2, 2, key_width), jnp.float32)
    expand_pad = lax.dynamic_update_index_in_dim(
        expand_pad, expand_grad[: rank_count + 1].reshape(rank_count + 1, 2, key_width), core, 2
    ).reshape(rank_count + 1, 4 * key_width)
    group_rows = jnp.pad(group_grad, ((0, rank_count), (0, model_width - 4 * key_width - value_width)))
    small_grad = jnp.concatenate(
        [
            0.5 * squeeze_grad,
            0.5 * gain_one_grad,
            0.5 * gain_two_grad,
            jnp.concatenate([expand_pad, group_rows], axis=1),
        ]
    )
    small_grad = sum_everywhere(small_grad)
    mine_grad = lax.dynamic_slice_in_dim(small_grad[: rank_count + 2], seq_index * rows, rows, 1)
    expand_total = small_grad[rank_count + 2 :, : 4 * key_width]
    group_total = small_grad[rank_count + 2 : rank_count + 3, 4 * key_width : 4 * key_width + value_width]

    share = jnp.broadcast_to((head_index == 0).astype(jnp.float32), (8, LANES))
    by_width = lambda a: jnp.moveaxis(a, 0, 2)
    early, early_squares = adam_group(
        share,
        [ffn_sum],
        [(lambda g: g[:2], False), (lambda g: g[2], False)],
        [
            tuple(map(by_width, (ffn_weight, ffn_mean, ffn_square))),
            (down_weight, down_mean, down_square),
        ],
    )
    late, late_squares = adam_group(
        share,
        [late_sum, state_sum, output_sum_grad, mine_grad],
        [
            (lambda l, s, o, m: jnp.concatenate([l[:rows], s[:rows]], axis=1), False),
            (
                lambda l, s, o, m: jnp.concatenate(
                    [s[rows : 2 * rows], s[2 * rows : 3 * rows], l[rows : 2 * rows], l[2 * rows : 3 * rows]],
                    axis=1,
                ),
                False,
            ),
            (lambda l, s, o, m: o[...], False),
            (lambda l, s, o, m: m[:rank_count], True),
            (lambda l, s, o, m: m[rank_count:], True),
        ],
        [
            (query_weight, query_mean, query_square),
            (value_weight, value_mean, value_square),
            (output_weight, output_mean, output_square),
            (squeeze_weight.T, squeeze_mean.T, squeeze_square.T),
            (norms_weight, norms_mean, norms_square),
        ],
    )
    copied, copied_squares = adam_group(
        share,
        [expand_total, group_total],
        [(lambda e, g: e[...], False), (lambda e, g: g[...], False)],
        [
            (expand_weight, expand_mean, expand_square),
            tuple(a[None, :] for a in (group_weight, group_mean, group_square)),
        ],
    )
    squares = sum_everywhere(jnp.concatenate([early_squares, late_squares]))
    squares = jnp.concatenate([squares, copied_squares])
    masters = [
        by_width(ffn_weight), down_weight,
        query_weight, value_weight, output_weight, squeeze_weight.T, norms_weight,
        expand_weight, group_weight[None, :],
    ]
    moments = early + late + copied
    news = whole_call(
        lambda *refs: trust_kernel([0, 1, 16, 17, 18, 19, 20, 32, 33], *refs),
        [squares] + masters + [moment[2] for moment in moments],
        [master.shape for master in masters],
    )
    triples = [(new,) + moment[:2] for new, moment in zip(news, moments)]
    ffn_out, down_out, query_out, value_out, output_out, squeeze_out, norms_out, expand_out, group_out = triples
    ffn_out = tuple(jnp.moveaxis(a, 2, 0) for a in ffn_out)
    squeeze_out = tuple(a.T for a in squeeze_out)
    group_out = tuple(a[0] for a in group_out)
    return (block_out, tokens_grad) + tuple(
        array
        for triple in (
            query_out, value_out, squeeze_out, expand_out, group_out, output_out, ffn_out, down_out, norms_out,
        )
        for array in triple
    )


def solution(mesh):
    in_specs = (
        P(None, "seq", "head"),
        P(None, "seq", "head"),
        P("seq", "head", None),
        P("seq", "head", None),
        P("seq", "head", None),
        P("seq", "head", None),
        P("seq", "head", None),
        P("seq", "head", None),
        P("seq", None),
        P("seq", None),
        P("seq", None),
        P(),
        P(),
        P(),
        P(),
        P(),
        P(),
        P("head", "seq"),
        P("head", "seq"),
        P("head", "seq"),
        P("seq", None, "head"),
        P("seq", None, "head"),
        P("seq", None, "head"),
        P("head", "seq"),
        P("head", "seq"),
        P("head", "seq"),
        P(None, "seq"),
        P(None, "seq"),
        P(None, "seq"),
    )
    out_specs = (
        P(None, "seq", "head"),
        P(None, "seq", "head"),
        P("seq", "head", None),
        P("seq", "head", None),
        P("seq", "head", None),
        P("seq", "head", None),
        P("seq", "head", None),
        P("seq", "head", None),
        P("seq", None),
        P("seq", None),
        P("seq", None),
        P(),
        P(),
        P(),
        P(),
        P(),
        P(),
        P("head", "seq"),
        P("head", "seq"),
        P("head", "seq"),
        P("seq", None, "head"),
        P("seq", None, "head"),
        P("seq", None, "head"),
        P("head", "seq"),
        P("head", "seq"),
        P("head", "seq"),
        P(None, "seq"),
        P(None, "seq"),
        P(None, "seq"),
    )
    return jax.shard_map(
        per_device, mesh=mesh, in_specs=in_specs, out_specs=out_specs, check_vma=False
    )
```

```python
import jax
import jax.numpy as jnp
from jax import lax
from jax.experimental import pallas as pl
from jax.experimental.pallas import tpu as pltpu
from jax.sharding import PartitionSpec as P

SPAN = 64
STEP = 10


eps_norm = 1e-06
gate_scale = 16.0
beta_one = 0.9
beta_two = 0.999
eps_adam = 1e-06
decay_rate = 0.01
learn_rate = 0.5
highest = lax.Precision.HIGHEST


def to_half(value_entries):
    return value_entries.astype(jnp.bfloat16)


def to_float(value_entries):
    return value_entries.astype(jnp.float32)


def mm(pattern, left, right):
    return jnp.einsum(pattern, left, right, preferred_element_type=jnp.float32)


def exact(pattern, left, right):
    return jnp.einsum(pattern, left, right, precision=highest)


def swap(value_entries, axis, bit):
    peers = lax.axis_size(axis)
    return lax.ppermute(value_entries, axis, [(i, i ^ bit) for i in range(peers)])


def bit_of(axis, bit):
    return (lax.axis_index(axis) // bit) % 2


def pick(value_entries, at, axis=0):
    return lax.dynamic_index_in_dim(value_entries, at, axis, keepdims=False)


def ordered(mine, other, upper):
    return (jnp.where(upper == 0, mine, other), jnp.where(upper == 0, other, mine))


def seq_bits():
    bits, bit = [], lax.axis_size("seq") // 2
    while bit:
        bits.append(("seq", bit))
        bit //= 2
    return bits


def cube_rank():
    return [("head", 2)] + seq_bits()


def beside_each_other(part, moved, held, stage):
    low, high = ordered(part, moved, bit_of(*stage))
    held = sorted(held + [stage], key=cube_rank().index)
    return jnp.stack([low, high], axis=held.index(stage)), held


def grow(part, held, stages):
    for stage in stages:
        part, held = beside_each_other(part, swap(part, *stage), held, stage)
    return part, held


def grown(part, held):
    return part.reshape((2, lax.axis_size("seq")) + part.shape[len(held) :])


def gather_cube(part, stages):
    return grown(*grow(part, [], stages))


def split(part, held, stage):
    if held is None:
        held = cube_rank()
        part = part.reshape((2,) * len(held) + part.shape[2:])
    at = held.index(stage)
    return pick(part, bit_of(*stage), at), to_half(pick(part, 1 - bit_of(*stage), at))


def shrink(part, held, stages, pin=lambda at, moved: moved):
    if held is None:
        held = cube_rank()
        part = part.reshape((2,) * len(held) + part.shape[2:])
    held = list(held)
    for number, (axis, bit) in enumerate(stages):
        at = held.index((axis, bit))
        held.pop(at)
        upper = bit_of(axis, bit)
        moved = pin(number, swap(to_half(pick(part, 1 - upper, at)), axis, bit))
        part = to_float(pick(part, upper, at)) + to_float(moved)
    return [part, held]


def scatter_cube(part, stages, pin=lambda at, moved: moved):
    return shrink(part, None, stages, pin)[0]


def sum_everywhere(value_entries):
    for axis, bit in [("head", 1), ("head", 2)] + seq_bits()[::-1]:
        value_entries = value_entries + swap(value_entries, axis, bit)
    return value_entries


tie = lax.optimization_barrier


def scan_blocks(decay, state, reverse, hook):
    before_decay, before_state = (jnp.ones_like(decay), jnp.zeros_like(state))
    size = state.shape[1]
    for number, (axis, bit) in enumerate(seq_bits()[::-1]):
        upper = bit_of(axis, bit) == (0 if reverse else 1)
        high = to_half(decay)
        low = to_half(decay - to_float(high))
        blank = jnp.zeros_like(state[:, :14], jnp.bfloat16)
        message = jnp.concatenate([to_half(state), high, low, blank], axis=1)
        message = to_float(hook(number, swap(message, axis, bit)))
        other_state = message[:, :size]
        other_decay = message[:, size : size + 1] + message[:, size + 1 : size + 2]
        before_state = jnp.where(upper, before_decay * other_state + before_state, before_state)
        before_decay = jnp.where(upper, before_decay * other_decay, before_decay)
        state = jnp.where(
            upper,
            decay * other_state + state,
            other_decay * state + other_state,
        )
        decay = decay * other_decay
    return before_state


TILE = 256
LANES = 128
VALUES = 256
VMEM_LIMIT = 50 * 1024 * 1024
WHOLE_LIMIT = 60 * 1024 * 1024


def mul(left, right, left_dim=1, right_dim=0):
    return lax.dot_general(
        to_half(left),
        to_half(right),
        (((left_dim,), (right_dim,)), ((), ())),
        preferred_element_type=jnp.float32,
    )


def mul_exact(left, right, left_dim=1, right_dim=0):
    return lax.dot_general(
        left,
        right,
        (((left_dim,), (right_dim,)), ((), ())),
        precision=highest,
        preferred_element_type=jnp.float32,
    )


def halves(value_entries):
    high = to_half(value_entries)
    return high, to_half(value_entries - to_float(high))


def mul_ones(ones, right):
    high, low = halves(right)
    return mul(ones, high) + mul(ones, low)


def span_masks():
    row = lax.broadcasted_iota(jnp.int32, (TILE, TILE), 0)
    column = lax.broadcasted_iota(jnp.int32, (TILE, TILE), 1)
    same = (row // SPAN) == (column // SPAN)
    return same & (row >= column), same & (row <= column), row >= column


def ones_where(mask):
    return jnp.where(mask, 1.0, 0.0).astype(jnp.bfloat16)


def log_sigmoid(z):
    decay = jnp.exp(-jnp.abs(z))
    ratio = decay / (2.0 + decay)
    square = ratio * ratio
    series = 1.0 / 15.0
    for odd in (13.0, 11.0, 9.0, 7.0, 5.0, 3.0, 1.0):
        series = series * square + 1.0 / odd
    return jnp.minimum(z, 0.0) - 2.0 * ratio * series


def call(body, steps, ins, outs, reverse=False, scratch=()):
    def spec(shape, axis, period=steps):
        if axis == "smem":
            return pl.BlockSpec(memory_space=pltpu.SMEM)
        block = tuple(n // period if d == axis else n for d, n in enumerate(shape))

        def where(i):
            at = (steps - 1 - i if reverse else i) % period
            return tuple(at if d == axis else 0 for d in range(len(shape)))

        return pl.BlockSpec(block, where)

    return pl.pallas_call(
        body,
        grid=(steps,),
        in_specs=[spec(entry[0].shape, *entry[1:]) for entry in ins],
        out_specs=[spec(shape, axis) for shape, _, axis in outs],
        out_shape=[jax.ShapeDtypeStruct(shape, dtype) for shape, dtype, _ in outs],
        scratch_shapes=list(scratch),
        compiler_params=pltpu.CompilerParams(vmem_limit_bytes=VMEM_LIMIT),
        cost_estimate=pl.CostEstimate(flops=1, bytes_accessed=0, transcendentals=0),
    )(*[entry[0] for entry in ins])


def heads(width):
    return [slice(h * width, (h + 1) * width) for h in range(2)]


def span_rows(j):
    return slice(j * SPAN, (j + 1) * SPAN)


def ends(within):
    return [within[(j + 1) * SPAN - 1 : (j + 1) * SPAN] for j in range(TILE // SPAN)]


def stacked(parts):
    return jnp.concatenate(parts, axis=0)


def spread(rows):
    return stacked([jnp.broadcast_to(row, (SPAN, row.shape[1])) for row in rows])


def whole_tile(within):
    offset, offsets = jnp.zeros_like(within[:1]), []
    for row in ends(within):
        offsets.append(offset)
        offset = offset + row
    return within + spread(offsets)


def four_blocks(place_ref, mine, moved, beside_mine, beside_moved):
    chip, core = (place_ref[0], place_ref[1])
    own = [jnp.where(chip == b, mine, moved) for b in range(2)]
    beside = [jnp.where(chip == b, beside_mine, beside_moved) for b in range(2)]
    return jnp.concatenate(
        [jnp.where(core == l, own[b], beside[b]) for b in range(2) for l in range(2)], axis=1
    )


def two_halves(place_ref, number, mine, beside):
    return jnp.where(place_ref[1] == number // 2, mine, beside)


def first_step(body):
    pl.when(pl.program_id(0) == 0)(body)


def model_rows(ref, h, first, blocks=1):
    parts = [
        ref[h, :, first + LANES * b : first + LANES * (b + 1), :].reshape(-1, LANES)
        for b in range(blocks)
    ]
    return parts[0] if blocks == 1 else jnp.concatenate(parts, axis=1)


def project_kernel(
    place_ref, tokens_ref, moved_ref, beside_ref, beside_moved_ref, first_ref, expand_ref,
    x_ref, normed_ref, key_out_ref, value_out_ref, rank_ref, within_ref, slope_ref, state_ref, log_ref, gain_ref, small_ref,
):
    @first_step
    def _():
        state_ref[...] = jnp.zeros_like(state_ref)
        log_ref[...] = jnp.zeros_like(log_ref)
        small_ref[32:] = jnp.zeros_like(small_ref[32:])
        for s in range(first_ref.shape[1]):
            small_ref[:32, s * LANES : (s + 1) * LANES] = first_ref[0, s, LANES : LANES + 32]
        gain_ref[...] = to_float(small_ref[16:24])

    chip = place_ref[0]
    x = four_blocks(
        place_ref, tokens_ref[chip], moved_ref[0], beside_ref[chip], beside_moved_ref[0]
    )
    x_ref[...] = x
    x = to_float(x)
    scale = lax.rsqrt(jnp.mean(x * x, axis=1, keepdims=True) + eps_norm)
    normed = to_half(x * scale * gain_ref[0:1])
    normed_ref[...] = normed
    key_weight = jnp.concatenate([model_rows(first_ref, h, 0) for h in range(2)], axis=1)
    keys = to_half(mul(normed, key_weight))
    key_out_ref[...] = keys
    values = [to_half(mul(normed, model_rows(first_ref, h, LANES + 32, 2))) for h in range(2)]
    for h, v in enumerate(heads(VALUES)):
        value_out_ref[:, v] = values[h]
    rank_values = mul(normed, small_ref[...], 1, 1)
    column = lax.broadcasted_iota(jnp.int32, rank_values.shape, 1)
    rank_values = jnp.where(column < 16, rank_values, jnp.where(column == 16, 1.0, 0.0))
    rank_ref[...] = rank_values
    rank_high, rank_low = halves(rank_values)
    expand_high, expand_low = halves(expand_ref[...])
    logits = mul(rank_high, expand_high) + (mul(rank_low, expand_high) + mul(rank_high, expand_low))
    decays = log_sigmoid(logits) * (1.0 / gate_scale)
    slope_ref[...] = 1.0 / (gate_scale * (1.0 + jnp.exp(logits)))
    sums = mul_ones(ones_where(span_masks()[2]), decays)
    log_ref[...] += sums[TILE - 1 :]
    for j in range(TILE // SPAN):
        part = sums[span_rows(j)]
        within_ref[span_rows(j), :] = part - sums[j * SPAN - 1 : j * SPAN] if j else part
    closing = sums[TILE - 1 :]
    rest = to_half(to_float(keys) * jnp.exp(closing - sums))
    decay = jnp.exp(closing)
    for h, k in enumerate(heads(LANES)):
        state_ref[h] = state_ref[h] * decay[:, k] + mul(values[h], rest[:, k], 0, 0)


def project_late_kernel(normed_ref, weight_ref, query_ref, gate_ref):
    normed = normed_ref[...]
    for h, (k, v) in enumerate(zip(heads(LANES), heads(VALUES))):
        query_ref[:, k] = to_half(mul(normed, model_rows(weight_ref, h, 0)))
        gate_ref[:, v] = mul(normed, model_rows(weight_ref, h, LANES, 2))


def load_output(late_ref, output_ref):
    for s in range(late_ref.shape[1]):
        output_ref[:, :, s * LANES : (s + 1) * LANES] = late_ref[:, s]


def forward_kernel(
    query_ref, key_ref, value_ref, gate_ref, within_ref, incoming_ref, group_ref,
    recurrent_ref, start_ref, mixed_ref, state_ref,
):
    @first_step
    def _():
        state_ref[...] = incoming_ref[...]

    causal = span_masks()[0]
    for h, (k, v) in enumerate(zip(heads(LANES), heads(VALUES))):
        within = within_ref[:, k]
        closings = ends(within)
        values = value_ref[:, v]
        keys = to_float(key_ref[:, k])
        queries = to_half(to_float(query_ref[:, k]) * jnp.exp(within))
        scores = jnp.where(causal, mul(queries, keys * jnp.exp(-within), 1, 1), 0.0)
        inside = mul(scores, values)
        keys_out = to_half(keys * jnp.exp(spread(closings) - within))
        state = state_ref[h]
        across = []
        for j, closing in enumerate(closings):
            start = to_half(state)
            start_ref[j, h] = start
            across.append(mul(queries[span_rows(j)], start, 1, 1))
            state = state * jnp.exp(closing) + mul(values[span_rows(j)], keys_out[span_rows(j)], 0, 0)
        state_ref[h] = state
        recurrent = (inside + stacked(across)) * LANES ** (-0.5)
        recurrent_ref[:, v] = recurrent
        scale = lax.rsqrt(jnp.mean(recurrent * recurrent, axis=1, keepdims=True) + eps_norm)
        gate = gate_ref[:, v]
        mixed = to_half(recurrent * scale * group_ref[...] * (gate * jax.nn.sigmoid(gate)))
        mixed_ref[:, v] = mixed


def mix_kernel(mixed_ref, weight_ref, part_ref, output_ref):
    @first_step
    def _():
        load_output(weight_ref, output_ref)

    part_ref[...] = to_half(mul(mixed_ref[...], output_ref[...].reshape(2 * VALUES, -1)))


def residual_kernel(x_ref, mine_ref, other_ref, gain_ref, residual_ref, normed_ref):
    residual = to_float(x_ref[...]) + (to_float(mine_ref[...]) + to_float(other_ref[...]))
    scale = lax.rsqrt(jnp.mean(residual * residual, axis=1, keepdims=True) + eps_norm)
    residual_ref[...] = residual
    normed_ref[...] = to_half(residual * scale * gain_ref[1:2])


def feed_forward_kernel(
    other, place_ref, normed_ref, beside_normed_ref, cot_ref, moved_ref, beside_ref, beside_moved_ref, weight_ref,
    hidden_ref, gate_grad_ref, up_grad_ref, keep_ref, give_ref, rows_grad_ref, cot_out_ref, normed_out_ref, all_ref,
):
    width = weight_ref.shape[2]

    @first_step
    def _():
        all_ref[:, width:] = jnp.zeros_like(all_ref[:, width:])
        for s in range(weight_ref.shape[0]):
            all_ref[:, :width, s * LANES : (s + 1) * LANES] = weight_ref[s]

    normed = normed_ref[...]
    if other:
        normed = two_halves(place_ref, pl.program_id(0), normed, beside_normed_ref[...])
        normed_out_ref[...] = normed
    chip = place_ref[0]
    sequence = 1 - chip if other else chip
    moved, beside_moved = (moved_ref[...], beside_moved_ref[...])
    cot = four_blocks(place_ref, cot_ref[sequence], moved, beside_ref[sequence], beside_moved)
    cot_out_ref[...] = cot
    gate = mul(normed, all_ref[0], 1, 1)
    up = mul(normed, all_ref[1], 1, 1)
    hidden_grad = mul(cot, all_ref[2], 1, 1)
    sigmoid = jax.nn.sigmoid(gate)
    silu = gate * sigmoid
    hidden = to_half(silu * up)
    hidden_ref[...] = hidden.T
    gate_grad = to_half(hidden_grad * up * sigmoid * (1.0 + gate * (1.0 - sigmoid)))
    gate_grad_ref[...] = gate_grad.T
    up_grad = to_half(hidden_grad * silu)
    up_grad_ref[...] = up_grad.T
    rows_grad_ref[...] = to_half(mul(gate_grad, all_ref[0]) + mul(up_grad, all_ref[1]))
    out = to_half(mul(hidden, all_ref[2]))
    columns = keep_ref.shape[2]
    for b in range(2):
        low, high = (out[:, (2 * b + l) * columns : (2 * b + l + 1) * columns] for l in range(2))
        keep_ref[b] = jnp.where(place_ref[1] == 0, low, high)
        give_ref[b] = jnp.where(place_ref[1] == 0, high, low)


def feed_forward_weights_kernel(
    own_ref, other_ref, cot_own_ref, cot_other_ref,
    gate_own_ref, gate_other_ref, up_own_ref, up_other_ref, hidden_own_ref, hidden_other_ref,
    out_ref,
):
    width = out_ref.shape[2]
    for i, (left, left_other, right, right_other) in enumerate(
        [
            (gate_own_ref, gate_other_ref, own_ref, other_ref),
            (up_own_ref, up_other_ref, own_ref, other_ref),
            (hidden_own_ref, hidden_other_ref, cot_own_ref, cot_other_ref),
        ]
    ):
        total = to_half(mul(left[...], right[...]) + mul(left_other[...], right_other[...]))
        for s in range(out_ref.shape[0]):
            out_ref[s, i] = total[:width, s * LANES : (s + 1) * LANES]


def mixer_backward_kernel(
    place_ref, residual_ref, cot_ref, mine_ref, other_ref, home_ref, beside_home_ref, gain_ref,
    late_ref, recurrent_ref, gate_ref, query_ref, within_ref, group_ref,
    keep_own_ref, beside_own_ref, keep_other_ref, beside_other_ref,
    grad_ref, half_ref, gain_grad_ref, recurrent_grad_ref, gate_grad_ref, group_grad_ref, state_grad_ref,
    send_ref, stay_ref, output_ref,
):
    @first_step
    def _():
        load_output(late_ref, output_ref)
        gain_grad_ref[...] = jnp.zeros_like(gain_grad_ref)
        group_grad_ref[...] = jnp.zeros_like(group_grad_ref)
        state_grad_ref[...] = jnp.zeros_like(state_grad_ref)

    residual = residual_ref[...]
    scale = lax.rsqrt(jnp.mean(residual * residual, axis=1, keepdims=True) + eps_norm)
    normed = residual * scale
    number = pl.num_programs(0) - 1 - pl.program_id(0)
    home = two_halves(place_ref, number, home_ref[...], beside_home_ref[...])
    pulled = to_float(mine_ref[...]) + to_float(other_ref[...]) + to_float(home)
    gain_grad_ref[...] += jnp.sum(pulled * normed, axis=0, keepdims=True)
    weighted = pulled * gain_ref[1:2]
    grad = to_float(cot_ref[...]) + scale * (
        weighted - normed * jnp.mean(weighted * normed, axis=1, keepdims=True)
    )
    grad_ref[...] = grad
    grad = to_half(grad)
    half_ref[...] = grad

    chip, core = (place_ref[0], place_ref[1])
    columns = keep_own_ref.shape[2]
    own, other = [], []
    for b in range(2):
        low, high = (residual[:, (2 * b + l) * columns : (2 * b + l + 1) * columns] for l in range(2))
        own.append(to_float(keep_own_ref[b]) + to_float(beside_own_ref[b]) + jnp.where(core == 0, low, high))
        other.append(to_float(keep_other_ref[b]) + to_float(beside_other_ref[b]))
    for at, rows in enumerate((own, other)):
        send_ref[at] = to_half(jnp.where(chip == 0, rows[1], rows[0]))
        stay_ref[at] = jnp.where(chip == 0, rows[0], rows[1])

    for h, (k, v) in enumerate(zip(heads(LANES), heads(VALUES))):
        mixed_grad = mul(grad, output_ref[h], 1, 1)
        recurrent = recurrent_ref[:, v]
        gate = gate_ref[:, v]
        scale = lax.rsqrt(jnp.mean(recurrent * recurrent, axis=1, keepdims=True) + eps_norm)
        sigmoid = jax.nn.sigmoid(gate)
        silu = gate * sigmoid
        normed = recurrent * scale
        group = group_ref[...]
        pulled = mixed_grad * normed
        group_grad_ref[...] += jnp.sum(pulled * silu, axis=0, keepdims=True)
        gate_grad_ref[:, v] = to_half(pulled * group * sigmoid * (1.0 + gate * (1.0 - sigmoid)))
        weighted = mixed_grad * group * silu
        recurrent_grad = scale * (weighted - normed * jnp.mean(weighted * normed, axis=1, keepdims=True))
        recurrent_grad = to_half(recurrent_grad * LANES ** (-0.5))
        recurrent_grad_ref[:, v] = recurrent_grad
        sums = whole_tile(within_ref[:, k])
        queries = to_float(query_ref[:, k]) * jnp.exp(sums)
        state_grad_ref[h] = state_grad_ref[h] * jnp.exp(sums[TILE - 1 :]) + mul(recurrent_grad, queries, 0, 0)


def query_backward_kernel(
    query_ref, key_ref, value_ref, within_ref, recurrent_grad_ref, start_ref, gate_grad_ref, weight_ref,
    query_grad_ref, kept_ref, normed_grad_ref,
):
    causal = span_masks()[0]
    total = None
    for h, (k, v) in enumerate(zip(heads(LANES), heads(VALUES))):
        within = within_ref[:, k]
        pulled = recurrent_grad_ref[:, v]
        keys_in = to_float(key_ref[:, k]) * jnp.exp(-within)
        scores_grad = jnp.where(causal, mul(pulled, value_ref[:, v], 1, 1), 0.0)
        across = stacked([mul(pulled[span_rows(j)], start_ref[j, h]) for j in range(TILE // SPAN)])
        query_grad = (mul(scores_grad, keys_in) + across) * jnp.exp(within)
        query_half = to_half(query_grad)
        query_grad_ref[:, k] = query_half
        kept_ref[:, k] = query_grad * to_float(query_ref[:, k])
        part = mul(query_half, model_rows(weight_ref, h, 0), 1, 1) + mul(
            gate_grad_ref[:, v], model_rows(weight_ref, h, LANES, 2), 1, 1
        )
        total = part if total is None else total + part
    normed_grad_ref[...] = to_half(total)


def backward_kernel(
    query_ref, key_ref, value_ref, within_ref, recurrent_grad_ref, start_ref, slope_ref, rank_ref, kept_ref,
    normed_grad_ref, first_ref, expand_ref, later_ref,
    key_grad_ref, value_grad_ref, rank_grad_ref, expand_grad_ref, part_ref, state_grad_ref,
):
    @first_step
    def _():
        state_grad_ref[...] = later_ref[...]
        expand_grad_ref[...] = jnp.zeros_like(expand_grad_ref)

    causal, until, _ = span_masks()
    last = lax.broadcasted_iota(jnp.int32, (TILE, LANES), 0) % SPAN == SPAN - 1
    total = to_float(normed_grad_ref[...])
    sums_grads = []
    for h, (k, v) in enumerate(zip(heads(LANES), heads(VALUES))):
        within = within_ref[:, k]
        closings = ends(within)
        values = value_ref[:, v]
        pulled = recurrent_grad_ref[:, v]
        keys = to_float(key_ref[:, k])
        shrink = jnp.exp(-within)
        rest = jnp.exp(spread(closings) - within)
        queries = to_half(to_float(query_ref[:, k]) * jnp.exp(within))
        keys_in = keys * shrink
        keys_out = keys * rest
        keys_half = to_half(keys_out)
        scores = jnp.where(causal, mul(queries, keys_in, 1, 1), 0.0)
        scores_grad = jnp.where(causal, mul(pulled, values, 1, 1), 0.0)
        keys_in_grad = mul(scores_grad, queries, 0, 0)
        value_in_grad = mul(scores, pulled, 0, 0)
        later = state_grad_ref[h]
        keys_out_grads, value_out_grads, bounds = [], [], []
        for j in reversed(range(TILE // SPAN)):
            at = span_rows(j)
            later_half = to_half(later)
            decay = jnp.exp(closings[j])
            keys_out_grads.insert(0, mul(values[at], later_half))
            value_out_grads.insert(0, mul(keys_half[at], later_half, 1, 1))
            bounds.insert(0, jnp.sum(later * to_float(start_ref[j, h]), axis=0, keepdims=True) * decay)
            later = later * decay + mul(pulled[at], queries[at], 0, 0)
        state_grad_ref[h] = later
        keys_out_grad = stacked(keys_out_grads)
        value_grad = to_half(value_in_grad + stacked(value_out_grads))
        value_grad_ref[:, v] = value_grad
        key_grad = to_half(keys_in_grad * shrink + keys_out_grad * rest)
        key_grad_ref[:, k] = key_grad
        kept = keys_out_grad * keys_out
        bounds = [
            bound + jnp.sum(kept[span_rows(j)], axis=0, keepdims=True) for j, bound in enumerate(bounds)
        ]
        sums_grads.append(
            kept_ref[:, k] - keys_in_grad * keys_in - kept + jnp.where(last, spread(bounds), 0.0)
        )
        total = total + (
            mul(key_grad, model_rows(first_ref, h, 0), 1, 1)
            + mul(value_grad, model_rows(first_ref, h, LANES + 32, 2), 1, 1)
        )
    part_ref[...] = to_half(total)
    logit_grad = mul_ones(ones_where(until), jnp.concatenate(sums_grads, axis=1)) * slope_ref[...]
    rank_grad_ref[...] = mul(expand_ref[:16], logit_grad, 1, 1)
    expand_grad_ref[...] += mul(rank_ref[...], logit_grad, 0, 0)[:24]


def store_whole(place_ref, refs, packs):
    for h in range(2):
        for s in range(2):
            refs[0][h, s] = packs[h][s]


def store_sides(place_ref, refs, packs):
    keep_first, give_first, keep_second, give_second = refs
    cut = keep_first.shape[1]
    chip, side = (place_ref[0], place_ref[2])
    for s in range(2):
        low, high = (packs[h][s][:cut] for h in range(2))
        keep_first[s] = jnp.where(chip == 0, low, high)
        give_first[s] = jnp.where(chip == 0, high, low)
    for h in range(2):
        low, high = (packs[h][s][cut:] for s in range(2))
        keep_second[h, 0] = jnp.where(side == 0, low, high)
        give_second[h, 0] = jnp.where(side == 0, high, low)


def block_rows(total, s):
    rows = to_half(total[s * LANES : (s + 1) * LANES])
    return [rows[:, b * LANES : (b + 1) * LANES] for b in range(total.shape[1] // LANES)]


def weights_kernel(store, place_ref, rows_ref, first_ref, second_ref, *refs):
    rows = rows_ref[...]
    packs = []
    for k, v in zip(heads(LANES), heads(VALUES)):
        first, second = (mul(rows, first_ref[:, k]), mul(rows, second_ref[:, v]))
        packs.append([stacked(block_rows(first, s) + block_rows(second, s)) for s in range(2)])
    store(place_ref, refs, packs)


def late_weights_kernel(store, place_ref, rows_ref, query_ref, gate_ref, mixed_ref, grad_ref, *refs):
    rows = rows_ref[...]
    packs = []
    for k, v in zip(heads(LANES), heads(VALUES)):
        first, second = (mul(rows, query_ref[:, k]), mul(rows, gate_ref[:, v]))
        output = to_half(mul(mixed_ref[v, :], grad_ref[...]))
        packs.append(
            [
                stacked(block_rows(first, s) + block_rows(second, s) + [output[:, s * LANES : (s + 1) * LANES]])
                for s in range(2)
            ]
        )
    store(place_ref, refs, packs)


def inputs_backward_kernel(
    place_ref, x_ref, grad_ref, mine_ref, other_ref, rank_grad_ref, small_ref, gain_ref, normed_ref,
    out_ref, gain_grad_ref, squeeze_grad_ref,
):
    @first_step
    def _():
        gain_grad_ref[...] = jnp.zeros_like(gain_grad_ref)
        squeeze_grad_ref[...] = jnp.zeros_like(squeeze_grad_ref)

    rank_grad = to_half(rank_grad_ref[...])
    x = to_float(x_ref[...])
    scale = lax.rsqrt(jnp.mean(x * x, axis=1, keepdims=True) + eps_norm)
    normed = x * scale
    pulled = (
        to_float(mine_ref[...])
        + to_float(other_ref[...])
        + mul(rank_grad, small_ref[:16], 0, 0)
    )
    squeeze_grad_ref[...] += mul(rank_grad, normed_ref[...])
    gain_grad_ref[...] += jnp.sum(pulled * normed, axis=0, keepdims=True)
    weighted = pulled * gain_ref[0:1]
    grad = grad_ref[...] + scale * (weighted - normed * jnp.mean(weighted * normed, axis=1, keepdims=True))
    columns = out_ref.shape[2]
    for b in range(2):
        low, high = (grad[:, (2 * b + i) * columns : (2 * b + i + 1) * columns] for i in range(2))
        out_ref[b] = jnp.where(place_ref[1] == 0, low, high)


def adam_kernel(count, joins, *refs):
    grads = refs[: len(refs) - 6 * count - 2]
    refs = refs[len(grads) :]
    share, ins, outs = refs[0], refs[1 : 1 + 3 * count], refs[1 + 3 * count :]
    squares = outs[3 * count]
    squares[...] = jnp.zeros_like(squares)
    for p, (join, shared) in enumerate(joins):
        gradient = to_float(join(*grads))
        master, first, second = (ref[...].reshape(gradient.shape) for ref in ins[3 * p : 3 * p + 3])
        new_first, new_second, direction = adam_direction(master, gradient, first, second)
        for ref, value in zip(outs[3 * p : 3 * p + 3], (new_first, new_second, direction)):
            ref[...] = value.reshape(ref.shape)
        for row, value in ((p, master), (8 + p, direction)):
            total = value * value
            while total.ndim > 2:
                total = jnp.sum(total, axis=0)
            total = jnp.sum(jnp.sum(total, axis=0, keepdims=True), axis=1, keepdims=True)
            if shared:
                total = total * share[0:1, 0:1]
            squares[row : row + 1] = jnp.broadcast_to(total, (1, LANES))


def trust_kernel(rows, squares_ref, *refs):
    count = len(rows)
    for p, row in enumerate(rows):
        master, direction, out = refs[p], refs[count + p], refs[2 * count + p]
        norm = jnp.sqrt(squares_ref[row : row + 1, 0:1])
        ratio = norm / (jnp.sqrt(squares_ref[row + 8 : row + 9, 0:1]) + eps_adam)
        shape = (1,) * len(master.shape)
        out[...] = master[...] - (learn_rate * ratio).reshape(shape) * direction[...]


def whole_call(body, ins, outs):
    return pl.pallas_call(
        body,
        out_shape=[jax.ShapeDtypeStruct(shape, jnp.float32) for shape in outs],
        compiler_params=pltpu.CompilerParams(vmem_limit_bytes=WHOLE_LIMIT),
        cost_estimate=pl.CostEstimate(flops=1, bytes_accessed=0, transcendentals=0),
    )(*ins)


def adam_group(share, grads, joins, params):
    count = len(params)
    outs = []
    for param in params:
        outs += [param[0].shape] * 3
    results = whole_call(
        lambda *refs: adam_kernel(count, joins, *refs),
        list(grads) + [share] + [array for param in params for array in param],
        outs + [(16, LANES)],
    )
    return [tuple(results[3 * p : 3 * p + 3]) for p in range(count)], results[-1]


def adam_direction(master, gradient, first_moment, second_moment):
    fix_one = 1.0 - beta_one**STEP
    second_correction = 1.0 - beta_two**STEP
    new_first = beta_one * first_moment + (1.0 - beta_one) * gradient
    new_second = beta_two * second_moment + (1.0 - beta_two) * gradient * gradient
    update_direction = (
        new_first * (1.0 / fix_one) / (jnp.sqrt(new_second * (1.0 / second_correction)) + eps_adam)
        + decay_rate * master
    )
    return (new_first, new_second, update_direction)


def per_device(
    tokens,
    cotangent,
    query_weight,
    query_mean,
    query_square,
    value_weight,
    value_mean,
    value_square,
    squeeze_weight,
    squeeze_mean,
    squeeze_square,
    expand_weight,
    expand_mean,
    expand_square,
    group_weight,
    group_mean,
    group_square,
    output_weight,
    output_mean,
    output_square,
    ffn_weight,
    ffn_mean,
    ffn_square,
    down_weight,
    down_mean,
    down_square,
    norms_weight,
    norms_mean,
    norms_square,
):
    sequences, segment, column_count = tokens.shape
    head_index = lax.axis_index("head")
    chip, core = (head_index // 2, head_index % 2)
    rows = query_weight.shape[0]
    peers = lax.axis_size("seq")
    seq_index = lax.axis_index("seq")
    model_width = rows * peers
    key_width = query_weight.shape[2] // 2
    value_width = value_weight.shape[2] // 2
    ffn_width = ffn_weight.shape[2]
    ffn_padded = -(-ffn_width // 256) * 256
    rank_count = squeeze_weight.shape[1]
    half_segment = segment // 2
    steps = segment // TILE
    half, full = (jnp.bfloat16, jnp.float32)
    aligned = rows % LANES == 0
    blocks = model_width // LANES
    along = seq_bits()[:-1]
    beside = ("seq", 1)
    across = ("head", 2)

    side = bit_of("seq", 1)
    place = jnp.stack([chip, core, side]).astype(jnp.int32)

    ffn_mine = jnp.concatenate([jnp.moveaxis(ffn_weight, 0, 2), down_weight[None]])
    ffn_mine = to_half(ffn_mine if aligned else jnp.moveaxis(ffn_mine, 2, 1))
    small_mine = jnp.concatenate(
        [
            squeeze_weight.T,
            jnp.zeros((16 - rank_count, rows), jnp.float32),
            norms_weight,
            jnp.zeros((14, rows), jnp.float32),
        ]
    )
    key_mine = query_weight[:, 0, key_width:]
    value_mine = value_weight[:, 0, :value_width]
    late_mine = jnp.concatenate(
        [
            query_weight[:, 0, :key_width],
            value_weight[:, 0, value_width : value_width + LANES],
            value_weight[:, 0, value_width + LANES :],
        ]
    )
    rows_moved = swap(pick(tokens, 1 - chip)[None], *across)
    tokens_beside, cot_beside = (swap(tokens, "head", 1), swap(cotangent, "head", 1))
    moved_beside = swap(rows_moved, "head", 1)
    if aligned:
        lines = [[x + 2 * z for z in range(peers // 2)] for x in range(2)]
        value_mine, ffn_mine = tie((to_half(value_mine), ffn_mine))
        ffn_all = lax.all_gather(ffn_mine, "seq", axis=0)
        key_part, held = grow(to_half(jnp.concatenate([key_mine, small_mine])), [], along)
        value_part, held = grow(jnp.concatenate([value_mine[:, :LANES], value_mine[:, LANES:]]), [], along)
        late_mine = to_half(jnp.concatenate([late_mine, output_weight]))
        late_mine, key_part, value_part = tie((late_mine, key_part, value_part))
        late_part, late_held = grow(late_mine, [], along[:1])
        key_all = grown(*grow(key_part, held, [across, beside]))
        value_part, value_held = grow(value_part, held, [beside])
        late_part, key_all = tie((late_part, key_all))
        late_moved = swap(late_part, *along[1])
        value_all = grown(*grow(value_part, value_held, [across]))
        first_all = jnp.concatenate([key_all, value_all], axis=2)

        def next_links(halves, moved):
            grown_halves = [
                beside_each_other(a, other, held, link) for a, other, link in zip(halves, moved, (across, beside))
            ]
            return jnp.concatenate(
                [
                    grown(*grow(*grown_halves[0], [beside])),
                    grown(*grow(*grown_halves[1], [across])),
                ],
                axis=2,
            )

    else:
        ffn_all = lax.all_gather(ffn_mine, "seq", axis=0)
        ffn_all = ffn_all.reshape(blocks, LANES // rows, 3, rows, ffn_width)
        ffn_all = ffn_all.transpose(0, 2, 4, 1, 3).reshape(blocks, 3, ffn_width, LANES)
        stages = along + [across, beside]

        def gather_columns(part):
            part = gather_cube(to_half(part), stages)
            return jnp.moveaxis(part.reshape(2, blocks, LANES, part.shape[-1]), 3, 2)

        def gather_blocks(part):
            count = part.shape[0] // rows
            part = gather_cube(to_half(part), stages).reshape(2, peers, count, rows, LANES)
            part = jnp.moveaxis(part, 2, 1).reshape(2, count, blocks, LANES, LANES)
            return jnp.moveaxis(part, 1, 2).reshape(2, blocks, count * LANES, LANES)

        value_blocks = jnp.concatenate([value_mine[:, :LANES], value_mine[:, LANES:]])
        first_all = jnp.concatenate(
            [gather_blocks(key_mine), gather_columns(small_mine.T), gather_blocks(value_blocks)], axis=2
        )
        late_all = jnp.concatenate([gather_blocks(late_mine), gather_columns(output_weight.T)], axis=2)

    expand_columns = pick(expand_weight.reshape(rank_count + 1, 2, 2, key_width), core, 2)
    expand_columns = jnp.pad(
        expand_columns.reshape(rank_count + 1, 2 * key_width), ((0, LANES - 1 - rank_count), (0, 0))
    )
    (
        input_half, normed, keys, value_entries, rank_values, within, slope, block_state, log_block, gains, small_full,
    ) = call(
        project_kernel,
        steps,
        [
            (place, "smem"),
            (tokens, 1),
            (rows_moved, 1),
            (tokens_beside, 1),
            (moved_beside, 1),
            (first_all, None),
            (expand_columns, None),
        ],
        [
            ((segment, model_width), half, 0),
            ((segment, model_width), half, 0),
            ((segment, 2 * key_width), half, 0),
            ((segment, 2 * value_width), half, 0),
            ((segment, LANES), full, 0),
            ((segment, 2 * key_width), full, 0),
            ((segment, 2 * key_width), full, 0),
            ((2, value_width, key_width), full, None),
            ((1, 2 * key_width), full, None),
            ((8, model_width), full, None),
            ((LANES, model_width), half, None),
        ],
    )
    if aligned:
        late_moved, block_state, log_block = tie((late_moved, block_state, log_block))
        late_part, _ = beside_each_other(late_part, late_moved, late_held, along[1])
        links = {}
        for name, low, cut, high in (
            ("gate", 0, 10 * LANES // 8, 3 * LANES),
            ("output", 3 * LANES, 3 * LANES + 7 * LANES // 8, 5 * LANES),
        ):
            links[name] = [late_part[..., low:cut, :], late_part[..., cut:high, :]]

        def first_links(halves):
            return [swap(halves[0], *across), swap(halves[1], *beside)]

        def second_links(halves, moved):
            sides = [
                beside_each_other(a, other, held, link) for a, other, link in zip(halves, moved, (across, beside))
            ]
            return sides, [swap(sides[0][0], *beside), swap(sides[1][0], *across)]

        def whole_links(sides, moved):
            ends = [
                grown(*beside_each_other(*(a, other, a_held, link)))
                for (a, a_held), other, link in zip(sides, moved, (beside, across))
            ]
            return jnp.concatenate(ends, axis=2)

        gate_moved = first_links(links["gate"])
    cot_given = [pick(cotangent, 1 - chip), pick(cotangent, chip)]

    def project_late(gate_all):
        return call(
            project_late_kernel,
            steps,
            [(normed, 0), (gate_all, None)],
            [((segment, 2 * key_width), half, 0), ((segment, 2 * value_width), full, 0)],
        )

    beside_scan = {}

    def beside_forward(number, message):
        if not aligned:
            return message
        if number == 1:
            message, moved, cot_given[0] = tie((message, gate_moved, cot_given[0]))
            beside_scan["gate"] = second_links(links["gate"], moved)
            beside_scan["output"] = first_links(links["output"])
            beside_scan["cot"] = swap(cot_given[0], *across)
        if number == 2:
            gate_all = whole_links(*beside_scan["gate"])
            out = project_late(gate_all)
            message, out, output_moved, cot_given[1] = tie(
                (message, out, beside_scan["output"], cot_given[1])
            )
            beside_scan.update(gate=gate_all, out=out)
            beside_scan["output"] = second_links(links["output"], output_moved)
        return message

    block_decay = jnp.exp(log_block).reshape(2, 1, key_width)
    state_in = scan_blocks(block_decay, block_state, False, beside_forward)
    if aligned:
        gate_all = beside_scan["gate"]
        queries, gate_values = beside_scan["out"]
        cot_own_moved = beside_scan["cot"]
    else:
        gate_all, output_all = (late_all[:, :, : 3 * LANES], late_all[:, :, 3 * LANES :])
        queries, gate_values = project_late(gate_all)
        cot_own_moved = swap(cot_given[0], *across)
    cot_other_moved = swap(cot_given[1], *across)
    recurrent, starts, mixed_half = call(
        forward_kernel,
        steps,
        [
            (queries, 0),
            (keys, 0),
            (value_entries, 0),
            (gate_values, 0),
            (within, 0),
            (state_in, None),
            (group_weight[None, :], None),
        ],
        [
            ((segment, 2 * value_width), full, 0),
            ((segment // SPAN, 2, value_width, key_width), half, 0),
            ((segment, 2 * value_width), half, 0),
        ],
        scratch=[pltpu.VMEM((2, value_width, key_width), jnp.float32)],
    )
    if aligned:
        output_sides, output_moved = beside_scan["output"]
        recurrent, mixed_half, output_moved, cot_own_moved = tie(
            (recurrent, mixed_half, output_moved, cot_own_moved)
        )
        output_all = whole_links(output_sides, output_moved)
    (mixer_part,) = call(
        mix_kernel,
        steps,
        [(mixed_half, 0), (output_all, None)],
        [((segment, model_width), half, 0)],
        scratch=[pltpu.VMEM((2, value_width, model_width), jnp.bfloat16)],
    )
    mixer_part, cot_other_moved = tie((mixer_part, cot_other_moved))
    mixer_beside = swap(mixer_part, "head", 1)
    cot_others = (cot_own_moved, cot_other_moved)
    cot_others_beside = [swap(a, "head", 1) for a in cot_others]
    mixer_beside, cot_others_beside = tie((mixer_beside, cot_others_beside))
    residual, normed_two = call(
        residual_kernel,
        steps,
        [(input_half, 0), (mixer_part, 0), (mixer_beside, 0), (gains, None)],
        [((segment, model_width), full, 0), ((segment, model_width), half, 0)],
    )

    moved = swap(lax.dynamic_slice_in_dim(normed_two, core * half_segment, half_segment, 0), *across)

    def feed_forward(other, mine, beside_mine):
        return call(
            lambda *refs: feed_forward_kernel(other, *refs),
            steps,
            [(place, "smem"), mine, beside_mine, (cotangent, 1)]
            + [(cot_others[other], 0), (cot_beside, 1), (cot_others_beside[other], 0)]
            + [(ffn_all, None)],
            [((ffn_padded, segment), half, 1)] * 3
            + [((2, segment, column_count), half, 1)] * 2
            + [((segment, model_width), half, 0)] * 2
            + ([((segment, model_width), half, 0)] if other else [((TILE, model_width), half, None)]),
            scratch=[pltpu.VMEM((3, ffn_padded, model_width), jnp.bfloat16)],
        )

    dummy = (place, "smem")
    own = feed_forward(False, (normed_two, 0), dummy)
    moved, own = tie((moved, own))
    other = feed_forward(True, (moved, 0, 2), (swap(moved, "head", 1), 0, 2))
    cot_own, cot_other, normed_two_other = (own[6], other[6], other[7])
    other_rows = other[5].reshape(2, half_segment, model_width)
    other_sum = to_half(
        to_float(pick(other_rows, core)) + to_float(swap(pick(other_rows, 1 - core), "head", 1))
    )
    home = swap(other_sum, *across)
    (ffn_grad,) = call(
        feed_forward_weights_kernel,
        4,
        [
            (normed_two, 1),
            (normed_two_other, 1),
            (cot_own, 1),
            (cot_other, 1),
            (own[1], None),
            (other[1], None),
            (own[2], None),
            (other[2], None),
            (own[0], None),
            (other[0], None),
        ],
        [((blocks, 3, ffn_width, LANES), half, 0)],
    )
    own_grad = own[5]
    own_beside = swap(own_grad, "head", 1)
    ffn_grad, normed, mixed_half = tie((ffn_grad, normed, mixed_half))
    home, ffn_grad, own_beside, normed_t, mixed_t = tie(
        (home, ffn_grad, own_beside, normed.T, mixed_half.T)
    )
    out_beside = [swap(give, "head", 1) for give in (own[4], other[4])]
    (
        residual_grad, residual_half, gain_two_grad, recurrent_grad, gate_grad, group_grad, state_in_grad,
        out_give, out_mine,
    ) = call(
        mixer_backward_kernel,
        steps,
        [
            (place, "smem"),
            (residual, 0),
            (cot_own, 0),
            (own_grad, 0),
            (own_beside, 0),
            (home, 0, 2),
            (swap(home, "head", 1), 0, 2),
            (gains, None),
            (output_all, None),
            (recurrent, 0),
            (gate_values, 0),
            (queries, 0),
            (within, 0),
            (group_weight[None, :], None),
            (own[3], 1),
            (out_beside[0], 1),
            (other[3], 1),
            (out_beside[1], 1),
        ],
        [
            ((segment, model_width), full, 0),
            ((segment, model_width), half, 0),
            ((1, model_width), full, None),
            ((segment, 2 * value_width), half, 0),
            ((segment, 2 * value_width), half, 0),
            ((1, value_width), full, None),
            ((2, value_width, key_width), full, None),
            ((2, segment, column_count), half, 1),
            ((2, segment, column_count), full, 1),
        ],
        reverse=True,
        scratch=[pltpu.VMEM((2, value_width, model_width), jnp.bfloat16)],
    )
    if not aligned:
        ffn_grad = ffn_grad.reshape(blocks, 3, ffn_width, LANES // rows, rows)
        ffn_grad = ffn_grad.transpose(0, 3, 1, 4, 2).reshape(peers, 3, rows, ffn_width)
    if aligned:
        ffn_pair = lax.psum_scatter(
            ffn_grad.reshape((peers // 2, 2) + ffn_grad.shape[1:]),
            "seq",
            scatter_dimension=0,
            tiled=False,
            axis_index_groups=lines,
        )
    else:
        ffn_sum = lax.psum_scatter(ffn_grad, "seq", scatter_dimension=0, tiled=False)
        ffn_sum = jnp.moveaxis(ffn_sum, 1, 2)

    out_moved = swap(out_give, *across)
    query_grad, kept, normed_grad = call(
        query_backward_kernel,
        steps,
        [
            (queries, 0),
            (keys, 0),
            (value_entries, 0),
            (within, 0),
            (recurrent_grad, 0),
            (starts, 0),
            (gate_grad, 0),
            (gate_all, None),
        ],
        [
            ((segment, 2 * key_width), half, 0),
            ((segment, 2 * key_width), full, 0),
            ((segment, model_width), half, 0),
        ],
    )
    def weights_call(body, count, ins):
        height = count * LANES
        if not aligned:
            outs = [((2, blocks, height, LANES), half, 1)]
        else:
            outs = [((blocks, height // 2, LANES), half, 0)] * 2
            outs += [((2, blocks // 2, height // 2, LANES), half, 1)] * 2
        store = store_sides if aligned else store_whole
        return call(lambda *refs: body(store, *refs), 4, [(place, "smem")] + ins, outs)

    late_grads = weights_call(
        late_weights_kernel,
        5,
        [(normed_t, 0), (query_grad, None), (gate_grad, None), (mixed_t, None), (residual_half, 1)],
    )
    beside_scan = {"first": (query_grad, kept, normed_grad), "second": late_grads}

    def beside_backward(number, message):
        which = {1: "first", 2: "second"}.get(number)
        if which and aligned:
            message, beside_scan[which] = tie((message, beside_scan[which]))
        return message

    later_grad = scan_blocks(block_decay, state_in_grad, True, beside_backward)
    (query_grad, kept, normed_grad), late_grads = (beside_scan["first"], beside_scan["second"])
    late_grads, later_grad, out_moved = tie((late_grads, later_grad, out_moved))
    back = along[::-1]
    if aligned:
        first_held = seq_bits()
        second_held = [across] + along

        def sides(grads):
            keep_first, give_first, keep_second, give_second = grads
            links = (2,) * len(first_held)
            return (
                [keep_first.reshape(links + keep_first.shape[1:]), keep_second.reshape(links + keep_second.shape[2:])],
                [swap(give_first.reshape(links + give_first.shape[1:]), *across),
                 swap(give_second.reshape(links + give_second.shape[2:]), *beside)],
            )

        def next_sides(kept, moved):
            splits = [
                split(to_float(a) + to_float(other), held, link)
                for a, other, held, link in zip(kept, moved, (first_held, second_held), (beside, across))
            ]
            return [a for a, _ in splits], [a for _, a in splits]

        def next_moved(gives):
            return [swap(gives[0], *beside), swap(gives[1], *across)]

        def joined(kept, moved):
            return jnp.concatenate([to_float(a) + to_float(b) for a, b in zip(kept, moved)], axis=-2)

        late_kept, late_moved = sides(late_grads)
    key_grad, value_grad, rank_grad_part, expand_grad, normed_part = call(
        backward_kernel,
        steps,
        [
            (queries, 0),
            (keys, 0),
            (value_entries, 0),
            (within, 0),
            (recurrent_grad, 0),
            (starts, 0),
            (slope, 0),
            (rank_values, 0),
            (kept, 0),
            (normed_grad, 0),
            (first_all, None),
            (expand_columns, None),
            (later_grad, None),
        ],
        [
            ((segment, 2 * key_width), half, 0),
            ((segment, 2 * value_width), half, 0),
            ((rank_count, segment), full, 1),
            ((24, 2 * key_width), full, None),
            ((segment, model_width), half, 0),
        ],
        reverse=True,
        scratch=[pltpu.VMEM((2, value_width, key_width), jnp.float32)],
    )
    if aligned:
        key_grad, value_grad, normed_part, rank_grad_part, late_moved = tie(
            (key_grad, value_grad, normed_part, rank_grad_part, late_moved)
        )
    normed_beside, rank_beside = (swap(normed_part, "head", 1), swap(rank_grad_part, "head", 1))
    state_grads = weights_call(
        weights_kernel, 3, [(normed_t, 0), (key_grad, None), (value_grad, None)]
    )
    normed_beside, rank_beside, state_grads = tie(
        (normed_beside, rank_beside, state_grads)
    )
    if aligned:
        state_kept, state_moved = sides(state_grads)
    rank_grad = rank_grad_part + rank_beside
    grad_cols, gain_one_grad, squeeze_grad = call(
        inputs_backward_kernel,
        steps,
        [
            (place, "smem"),
            (input_half, 0),
            (residual_grad, 0),
            (normed_part, 0),
            (normed_beside, 0),
            (rank_grad, 1),
            (small_full, None),
            (gains, None),
            (normed, 0),
        ],
        [
            ((2, segment, column_count), full, 1),
            ((1, model_width), full, None),
            ((rank_count, model_width), full, None),
        ],
    )
    if aligned:
        state_moved, late_moved, gain_one_grad, squeeze_grad, grad_cols = tie(
            (state_moved, late_moved, gain_one_grad, squeeze_grad, grad_cols)
        )
    expand_pad = jnp.zeros((rank_count + 1, 2, 2, key_width), jnp.float32)
    expand_pad = lax.dynamic_update_index_in_dim(
        expand_pad, expand_grad[: rank_count + 1].reshape(rank_count + 1, 2, key_width), core, 2
    ).reshape(rank_count + 1, 4 * key_width)
    group_rows = jnp.pad(group_grad, ((0, rank_count), (0, model_width - 4 * key_width - value_width)))
    small_grad = jnp.concatenate(
        [
            0.5 * squeeze_grad,
            0.5 * gain_one_grad,
            0.5 * gain_two_grad,
            jnp.concatenate([expand_pad, group_rows], axis=1),
        ]
    )
    if aligned:
        small_grad = small_grad + swap(small_grad, "head", 1)
        state_kept, state_gives = next_sides(state_kept, state_moved)
        state_moved = next_moved(state_gives)
        small_moved = swap(small_grad, *across)
        late_kept, late_gives = next_sides(late_kept, late_moved)
        late_moved = next_moved(late_gives)
        grad_give = to_half(pick(grad_cols, 1 - chip))
        state_moved, small_moved, grad_give, ffn_pair = tie((state_moved, small_moved, grad_give, ffn_pair))
        state_kept, state_give = split(joined(state_kept, state_moved), along, back[0])
        state_moved = swap(state_give, *back[0])
        small_grad = small_grad + small_moved
        small_moved = swap(small_grad, *beside)
        ffn_moved = swap(pick(ffn_pair, 1 - side), *beside)
        state_moved, small_moved, late_moved = tie((state_moved, small_moved, late_moved))
        state_kept, state_give = split(to_float(state_kept) + to_float(state_moved), along[:-1], back[1])
        state_moved = swap(state_give, *back[1])
        small_grad = small_grad + small_moved
        small_moved = swap(small_grad, *back[0])
        late_kept, late_give = split(joined(late_kept, late_moved), along, back[0])
        late_moved = swap(late_give, *back[0])
        state_moved, small_moved, late_moved, ffn_moved = tie((state_moved, small_moved, late_moved, ffn_moved))
        state_sum = to_float(state_kept) + to_float(state_moved)
        small_grad = small_grad + small_moved
        small_grad = small_grad + swap(small_grad, *back[1])
        late_sum = shrink(to_float(late_kept) + to_float(late_moved), along[:-1], back[1:])[0]
        ffn_sum = to_float(pick(ffn_pair, side)) + to_float(ffn_moved)
        output_sum_grad = late_sum[3 * LANES :]
    else:

        def split_rows(a):
            a = a.reshape(2, blocks, 3, LANES // rows, rows, LANES)
            return jnp.moveaxis(a, 3, 2).reshape(2, peers, 3 * rows, LANES)

        late_sum = scatter_cube(split_rows(late_grads[0][:, :, : 3 * LANES]), [beside, across] + back)
        state_sum = scatter_cube(split_rows(state_grads[0]), [across, beside] + back)
        output_grad = late_grads[0][:, :, 3 * LANES :].reshape(2, blocks, value_width, LANES // rows, rows)
        output_grad = output_grad.transpose(0, 1, 3, 4, 2).reshape(2, peers, rows, value_width)
        output_sum_grad = scatter_cube(output_grad, [beside, across] + back).T
        grad_give = to_half(pick(grad_cols, 1 - chip))
        small_grad = sum_everywhere(small_grad)
    grad_home = to_float(swap(grad_give, *across))
    tokens_grad = jnp.stack(ordered(pick(grad_cols, chip), grad_home, chip))
    out_home = to_float(out_moved)
    block_out = to_half(jnp.stack(ordered(out_mine[0] + out_home[1], out_mine[1] + out_home[0], chip)))

    mine_grad = lax.dynamic_slice_in_dim(small_grad[: rank_count + 2], seq_index * rows, rows, 1)
    expand_total = small_grad[rank_count + 2 :, : 4 * key_width]
    group_total = small_grad[rank_count + 2 : rank_count + 3, 4 * key_width : 4 * key_width + value_width]

    share = jnp.broadcast_to((head_index == 0).astype(jnp.float32), (8, LANES))
    by_width = lambda a: jnp.moveaxis(a, 0, 2)
    early, early_squares = adam_group(
        share,
        [ffn_sum],
        [(lambda g: g[:2], False), (lambda g: g[2], False)],
        [
            tuple(map(by_width, (ffn_weight, ffn_mean, ffn_square))),
            (down_weight, down_mean, down_square),
        ],
    )
    early_squares, late_sum = tie((early_squares, late_sum))
    late, late_squares = adam_group(
        share,
        [late_sum, state_sum, output_sum_grad, mine_grad],
        [
            (lambda l, s, o, m: jnp.concatenate([l[:rows], s[:rows]], axis=1), False),
            (
                lambda l, s, o, m: jnp.concatenate(
                    [s[rows : 2 * rows], s[2 * rows : 3 * rows], l[rows : 2 * rows], l[2 * rows : 3 * rows]],
                    axis=1,
                ),
                False,
            ),
            (lambda l, s, o, m: o[...], False),
            (lambda l, s, o, m: m[:rank_count], True),
            (lambda l, s, o, m: m[rank_count:], True),
        ],
        [
            (query_weight, query_mean, query_square),
            (value_weight, value_mean, value_square),
            (output_weight, output_mean, output_square),
            (squeeze_weight.T, squeeze_mean.T, squeeze_square.T),
            (norms_weight, norms_mean, norms_square),
        ],
    )
    copied, copied_squares = adam_group(
        share,
        [expand_total, group_total],
        [(lambda e, g: e[...], False), (lambda e, g: g[...], False)],
        [
            (expand_weight, expand_mean, expand_square),
            tuple(a[None, :] for a in (group_weight, group_mean, group_square)),
        ],
    )
    squares = sum_everywhere(jnp.concatenate([early_squares, late_squares]))
    squares = jnp.concatenate([squares, copied_squares])
    masters = [
        by_width(ffn_weight), down_weight,
        query_weight, value_weight, output_weight, squeeze_weight.T, norms_weight,
        expand_weight, group_weight[None, :],
    ]
    moments = early + late + copied
    news = whole_call(
        lambda *refs: trust_kernel([0, 1, 16, 17, 18, 19, 20, 32, 33], *refs),
        [squares] + masters + [moment[2] for moment in moments],
        [master.shape for master in masters],
    )
    triples = [(new,) + moment[:2] for new, moment in zip(news, moments)]
    ffn_out, down_out, query_out, value_out, output_out, squeeze_out, norms_out, expand_out, group_out = triples
    ffn_out = tuple(jnp.moveaxis(a, 2, 0) for a in ffn_out)
    squeeze_out = tuple(a.T for a in squeeze_out)
    group_out = tuple(a[0] for a in group_out)
    return (block_out, tokens_grad) + tuple(
        array
        for triple in (
            query_out, value_out, squeeze_out, expand_out, group_out, output_out, ffn_out, down_out, norms_out,
        )
        for array in triple
    )


def solution(mesh):
    in_specs = (
        P(None, "seq", "head"),
        P(None, "seq", "head"),
        P("seq", "head", None),
        P("seq", "head", None),
        P("seq", "head", None),
        P("seq", "head", None),
        P("seq", "head", None),
        P("seq", "head", None),
        P("seq", None),
        P("seq", None),
        P("seq", None),
        P(),
        P(),
        P(),
        P(),
        P(),
        P(),
        P("head", "seq"),
        P("head", "seq"),
        P("head", "seq"),
        P("seq", None, "head"),
        P("seq", None, "head"),
        P("seq", None, "head"),
        P("head", "seq"),
        P("head", "seq"),
        P("head", "seq"),
        P(None, "seq"),
        P(None, "seq"),
        P(None, "seq"),
    )
    out_specs = (
        P(None, "seq", "head"),
        P(None, "seq", "head"),
        P("seq", "head", None),
        P("seq", "head", None),
        P("seq", "head", None),
        P("seq", "head", None),
        P("seq", "head", None),
        P("seq", "head", None),
        P("seq", None),
        P("seq", None),
        P("seq", None),
        P(),
        P(),
        P(),
        P(),
        P(),
        P(),
        P("head", "seq"),
        P("head", "seq"),
        P("head", "seq"),
        P("seq", None, "head"),
        P("seq", None, "head"),
        P("seq", None, "head"),
        P("head", "seq"),
        P("head", "seq"),
        P("head", "seq"),
        P(None, "seq"),
        P(None, "seq"),
        P(None, "seq"),
    )
    return jax.shard_map(
        per_device, mesh=mesh, in_specs=in_specs, out_specs=out_specs, check_vma=False
    )
```

```python
import jax
import jax.numpy as jnp
from jax import lax
from jax.experimental import pallas as pl
from jax.experimental.pallas import tpu as pltpu
from jax.sharding import PartitionSpec as P

SPAN = 64
STEP = 10


eps_norm = 1e-06
gate_scale = 16.0
beta_one = 0.9
beta_two = 0.999
eps_adam = 1e-06
decay_rate = 0.01
learn_rate = 0.5
highest = lax.Precision.HIGHEST


def to_half(value_entries):
    return value_entries.astype(jnp.bfloat16)


def to_float(value_entries):
    return value_entries.astype(jnp.float32)


def mm(pattern, left, right):
    return jnp.einsum(pattern, left, right, preferred_element_type=jnp.float32)


def exact(pattern, left, right):
    return jnp.einsum(pattern, left, right, precision=highest)


def swap(value_entries, axis, bit):
    peers = lax.axis_size(axis)
    return lax.ppermute(value_entries, axis, [(i, i ^ bit) for i in range(peers)])


def bit_of(axis, bit):
    return (lax.axis_index(axis) // bit) % 2


def pick(value_entries, at, axis=0):
    return lax.dynamic_index_in_dim(value_entries, at, axis, keepdims=False)


def ordered(mine, other, upper):
    return (jnp.where(upper == 0, mine, other), jnp.where(upper == 0, other, mine))


def seq_bits():
    bits, bit = [], lax.axis_size("seq") // 2
    while bit:
        bits.append(("seq", bit))
        bit //= 2
    return bits


def cube_rank():
    return [("head", 2)] + seq_bits()


def beside_each_other(part, moved, held, stage):
    low, high = ordered(part, moved, bit_of(*stage))
    held = sorted(held + [stage], key=cube_rank().index)
    return jnp.stack([low, high], axis=held.index(stage)), held


def grow(part, held, stages):
    for stage in stages:
        part, held = beside_each_other(part, swap(part, *stage), held, stage)
    return part, held


def grown(part, held):
    return part.reshape((2, lax.axis_size("seq")) + part.shape[len(held) :])


def gather_cube(part, stages):
    return grown(*grow(part, [], stages))


def split(part, held, stage):
    if held is None:
        held = cube_rank()
        part = part.reshape((2,) * len(held) + part.shape[2:])
    at = held.index(stage)
    return pick(part, bit_of(*stage), at), to_half(pick(part, 1 - bit_of(*stage), at))


def shrink(part, held, stages, pin=lambda at, moved: moved):
    if held is None:
        held = cube_rank()
        part = part.reshape((2,) * len(held) + part.shape[2:])
    held = list(held)
    for number, (axis, bit) in enumerate(stages):
        at = held.index((axis, bit))
        held.pop(at)
        upper = bit_of(axis, bit)
        moved = pin(number, swap(to_half(pick(part, 1 - upper, at)), axis, bit))
        part = to_float(pick(part, upper, at)) + to_float(moved)
    return [part, held]


def scatter_cube(part, stages, pin=lambda at, moved: moved):
    return shrink(part, None, stages, pin)[0]


def sum_everywhere(value_entries):
    for axis, bit in [("head", 1), ("head", 2)] + seq_bits()[::-1]:
        value_entries = value_entries + swap(value_entries, axis, bit)
    return value_entries


tie = lax.optimization_barrier


def scan_blocks(decay, state, reverse, hook):
    before_decay, before_state = (jnp.ones_like(decay), jnp.zeros_like(state))
    size = state.shape[1]
    for number, (axis, bit) in enumerate(seq_bits()[::-1]):
        upper = bit_of(axis, bit) == (0 if reverse else 1)
        high = to_half(decay)
        low = to_half(decay - to_float(high))
        blank = jnp.zeros_like(state[:, :14], jnp.bfloat16)
        message = jnp.concatenate([to_half(state), high, low, blank], axis=1)
        message = to_float(hook(number, swap(message, axis, bit)))
        other_state = message[:, :size]
        other_decay = message[:, size : size + 1] + message[:, size + 1 : size + 2]
        before_state = jnp.where(upper, before_decay * other_state + before_state, before_state)
        before_decay = jnp.where(upper, before_decay * other_decay, before_decay)
        state = jnp.where(
            upper,
            decay * other_state + state,
            other_decay * state + other_state,
        )
        decay = decay * other_decay
    return before_state


TILE = 256
LANES = 128
VALUES = 256
VMEM_LIMIT = 50 * 1024 * 1024
WHOLE_LIMIT = 60 * 1024 * 1024


def mul(left, right, left_dim=1, right_dim=0):
    return lax.dot_general(
        to_half(left),
        to_half(right),
        (((left_dim,), (right_dim,)), ((), ())),
        preferred_element_type=jnp.float32,
    )


def mul_exact(left, right, left_dim=1, right_dim=0):
    return lax.dot_general(
        left,
        right,
        (((left_dim,), (right_dim,)), ((), ())),
        precision=highest,
        preferred_element_type=jnp.float32,
    )


def halves(value_entries):
    high = to_half(value_entries)
    return high, to_half(value_entries - to_float(high))


def mul_ones(ones, right):
    high, low = halves(right)
    return mul(ones, high) + mul(ones, low)


def span_masks():
    row = lax.broadcasted_iota(jnp.int32, (TILE, TILE), 0)
    column = lax.broadcasted_iota(jnp.int32, (TILE, TILE), 1)
    same = (row // SPAN) == (column // SPAN)
    return same & (row >= column), same & (row <= column), row >= column


def ones_where(mask):
    return jnp.where(mask, 1.0, 0.0).astype(jnp.bfloat16)


def log_sigmoid(z):
    decay = jnp.exp(-jnp.abs(z))
    ratio = decay / (2.0 + decay)
    square = ratio * ratio
    series = 1.0 / 15.0
    for odd in (13.0, 11.0, 9.0, 7.0, 5.0, 3.0, 1.0):
        series = series * square + 1.0 / odd
    return jnp.minimum(z, 0.0) - 2.0 * ratio * series


def call(body, steps, ins, outs, reverse=False, scratch=()):
    def spec(shape, axis, count=steps, at=lambda i: i):
        if axis == "smem":
            return pl.BlockSpec(memory_space=pltpu.SMEM)
        block = tuple(n // count if d == axis else n for d, n in enumerate(shape))

        def where(i):
            number = at(steps - 1 - i if reverse else i)
            return tuple(number if d == axis else 0 for d in range(len(shape)))

        return pl.BlockSpec(block, where)

    return pl.pallas_call(
        body,
        grid=(steps,),
        in_specs=[spec(entry[0].shape, *entry[1:]) for entry in ins],
        out_specs=[spec(shape, axis) for shape, _, axis in outs],
        out_shape=[jax.ShapeDtypeStruct(shape, dtype) for shape, dtype, _ in outs],
        scratch_shapes=list(scratch),
        compiler_params=pltpu.CompilerParams(vmem_limit_bytes=VMEM_LIMIT),
        cost_estimate=pl.CostEstimate(flops=1, bytes_accessed=0, transcendentals=0),
    )(*[entry[0] for entry in ins])


def heads(width):
    return [slice(h * width, (h + 1) * width) for h in range(2)]


def span_rows(j):
    return slice(j * SPAN, (j + 1) * SPAN)


def ends(within):
    return [within[(j + 1) * SPAN - 1 : (j + 1) * SPAN] for j in range(TILE // SPAN)]


def stacked(parts):
    return jnp.concatenate(parts, axis=0)


def spread(rows):
    return stacked([jnp.broadcast_to(row, (SPAN, row.shape[1])) for row in rows])


def whole_tile(within):
    offset, offsets = jnp.zeros_like(within[:1]), []
    for row in ends(within):
        offsets.append(offset)
        offset = offset + row
    return within + spread(offsets)


def four_blocks(place_ref, mine, moved, beside_mine, beside_moved):
    chip, core = (place_ref[0], place_ref[1])
    own = [jnp.where(chip == b, mine, moved) for b in range(2)]
    beside = [jnp.where(chip == b, beside_mine, beside_moved) for b in range(2)]
    return jnp.concatenate(
        [jnp.where(core == l, own[b], beside[b]) for b in range(2) for l in range(2)], axis=1
    )


def from_core(place_ref, number, mine, beside):
    return jnp.where(place_ref[1] == number, mine, beside)


def first_step(body):
    pl.when(pl.program_id(0) == 0)(body)


def model_rows(ref, h, first, blocks=1):
    parts = [
        ref[h, :, first + LANES * b : first + LANES * (b + 1), :].reshape(-1, LANES)
        for b in range(blocks)
    ]
    return parts[0] if blocks == 1 else jnp.concatenate(parts, axis=1)


def project_kernel(
    place_ref, tokens_ref, moved_ref, beside_ref, beside_moved_ref, first_ref, expand_ref,
    x_ref, normed_ref, key_out_ref, value_out_ref, rank_ref, within_ref, slope_ref, state_ref, log_ref, gain_ref, small_ref,
):
    @first_step
    def _():
        state_ref[...] = jnp.zeros_like(state_ref)
        log_ref[...] = jnp.zeros_like(log_ref)
        small_ref[32:] = jnp.zeros_like(small_ref[32:])
        for s in range(first_ref.shape[1]):
            small_ref[:32, s * LANES : (s + 1) * LANES] = first_ref[0, s, LANES : LANES + 32]
        gain_ref[...] = to_float(small_ref[16:24])

    chip = place_ref[0]
    x = four_blocks(
        place_ref, tokens_ref[chip], moved_ref[0], beside_ref[chip], beside_moved_ref[0]
    )
    x_ref[...] = x
    x = to_float(x)
    scale = lax.rsqrt(jnp.mean(x * x, axis=1, keepdims=True) + eps_norm)
    normed = to_half(x * scale * gain_ref[0:1])
    normed_ref[...] = normed
    key_weight = jnp.concatenate([model_rows(first_ref, h, 0) for h in range(2)], axis=1)
    keys = to_half(mul(normed, key_weight))
    key_out_ref[...] = keys
    values = [to_half(mul(normed, model_rows(first_ref, h, LANES + 32, 2))) for h in range(2)]
    for h, v in enumerate(heads(VALUES)):
        value_out_ref[:, v] = values[h]
    rank_values = mul(normed, small_ref[...], 1, 1)
    column = lax.broadcasted_iota(jnp.int32, rank_values.shape, 1)
    rank_values = jnp.where(column < 16, rank_values, jnp.where(column == 16, 1.0, 0.0))
    rank_ref[...] = rank_values
    rank_high, rank_low = halves(rank_values)
    expand_high, expand_low = halves(expand_ref[...])
    logits = mul(rank_high, expand_high) + (mul(rank_low, expand_high) + mul(rank_high, expand_low))
    decays = log_sigmoid(logits) * (1.0 / gate_scale)
    slope_ref[...] = 1.0 / (gate_scale * (1.0 + jnp.exp(logits)))
    sums = mul_ones(ones_where(span_masks()[2]), decays)
    log_ref[...] += sums[TILE - 1 :]
    for j in range(TILE // SPAN):
        part = sums[span_rows(j)]
        within_ref[span_rows(j), :] = part - sums[j * SPAN - 1 : j * SPAN] if j else part
    closing = sums[TILE - 1 :]
    rest = to_half(to_float(keys) * jnp.exp(closing - sums))
    decay = jnp.exp(closing)
    for h, k in enumerate(heads(LANES)):
        state_ref[h] = state_ref[h] * decay[:, k] + mul(values[h], rest[:, k], 0, 0)


def project_late_kernel(normed_ref, weight_ref, query_ref, gate_ref):
    normed = normed_ref[...]
    for h, (k, v) in enumerate(zip(heads(LANES), heads(VALUES))):
        query_ref[:, k] = to_half(mul(normed, model_rows(weight_ref, h, 0)))
        gate_ref[:, v] = mul(normed, model_rows(weight_ref, h, LANES, 2))


def load_output(late_ref, output_ref):
    for s in range(late_ref.shape[1]):
        output_ref[:, :, s * LANES : (s + 1) * LANES] = late_ref[:, s]


def forward_kernel(
    query_ref, key_ref, value_ref, gate_ref, within_ref, incoming_ref, group_ref,
    recurrent_ref, start_ref, mixed_ref, state_ref,
):
    @first_step
    def _():
        state_ref[...] = incoming_ref[...]

    causal = span_masks()[0]
    for h, (k, v) in enumerate(zip(heads(LANES), heads(VALUES))):
        within = within_ref[:, k]
        closings = ends(within)
        values = value_ref[:, v]
        keys = to_float(key_ref[:, k])
        queries = to_half(to_float(query_ref[:, k]) * jnp.exp(within))
        scores = jnp.where(causal, mul(queries, keys * jnp.exp(-within), 1, 1), 0.0)
        inside = mul(scores, values)
        keys_out = to_half(keys * jnp.exp(spread(closings) - within))
        state = state_ref[h]
        across = []
        for j, closing in enumerate(closings):
            start = to_half(state)
            start_ref[j, h] = start
            across.append(mul(queries[span_rows(j)], start, 1, 1))
            state = state * jnp.exp(closing) + mul(values[span_rows(j)], keys_out[span_rows(j)], 0, 0)
        state_ref[h] = state
        recurrent = (inside + stacked(across)) * LANES ** (-0.5)
        recurrent_ref[:, v] = recurrent
        scale = lax.rsqrt(jnp.mean(recurrent * recurrent, axis=1, keepdims=True) + eps_norm)
        gate = gate_ref[:, v]
        mixed = to_half(recurrent * scale * group_ref[...] * (gate * jax.nn.sigmoid(gate)))
        mixed_ref[:, v] = mixed


def mix_kernel(mixed_ref, weight_ref, part_ref, output_ref):
    @first_step
    def _():
        load_output(weight_ref, output_ref)

    part_ref[...] = to_half(mul(mixed_ref[...], output_ref[...].reshape(2 * VALUES, -1)))


def residual_kernel(x_ref, mine_ref, other_ref, gain_ref, residual_ref, normed_ref):
    residual = to_float(x_ref[...]) + (to_float(mine_ref[...]) + to_float(other_ref[...]))
    scale = lax.rsqrt(jnp.mean(residual * residual, axis=1, keepdims=True) + eps_norm)
    residual_ref[...] = residual
    normed_ref[...] = to_half(residual * scale * gain_ref[1:2])


def feed_forward_kernel(
    ring, other, place_ref, normed_ref, beside_normed_ref, cot_ref, moved_ref, beside_ref, beside_moved_ref, weight_ref,
    hidden_ref, gate_grad_ref, up_grad_ref, keep_ref, give_ref, rows_grad_ref, cot_out_ref, normed_out_ref, all_ref,
):
    width = weight_ref.shape[2]

    @first_step
    def _():
        all_ref[:, width:] = jnp.zeros_like(all_ref[:, width:])
        for at, s in enumerate(ring):
            all_ref[:, :width, s * LANES : (s + 1) * LANES] = weight_ref[at]

    normed = normed_ref[...]
    if other:
        normed = from_core(place_ref, pl.program_id(0), normed, beside_normed_ref[...])
        normed_out_ref[...] = normed
    chip = place_ref[0]
    sequence = 1 - chip if other else chip
    moved, beside_moved = (moved_ref[...], beside_moved_ref[...])
    cot = four_blocks(place_ref, cot_ref[sequence], moved, beside_ref[sequence], beside_moved)
    cot_out_ref[...] = cot
    gate = mul(normed, all_ref[0], 1, 1)
    up = mul(normed, all_ref[1], 1, 1)
    hidden_grad = mul(cot, all_ref[2], 1, 1)
    sigmoid = jax.nn.sigmoid(gate)
    silu = gate * sigmoid
    hidden = to_half(silu * up)
    hidden_ref[...] = hidden.T
    gate_grad = to_half(hidden_grad * up * sigmoid * (1.0 + gate * (1.0 - sigmoid)))
    gate_grad_ref[...] = gate_grad.T
    up_grad = to_half(hidden_grad * silu)
    up_grad_ref[...] = up_grad.T
    rows_grad_ref[...] = to_half(mul(gate_grad, all_ref[0]) + mul(up_grad, all_ref[1]))
    out = to_half(mul(hidden, all_ref[2]))
    columns = keep_ref.shape[2]
    for b in range(2):
        low, high = (out[:, (2 * b + l) * columns : (2 * b + l + 1) * columns] for l in range(2))
        keep_ref[b] = jnp.where(place_ref[1] == 0, low, high)
        give_ref[b] = jnp.where(place_ref[1] == 0, high, low)


def feed_forward_weights_kernel(*refs):
    sets, out_ref = [refs[7 * i : 7 * i + 7] for i in range(3)], refs[21]
    width = out_ref.shape[2]
    both = [
        [jnp.concatenate([group[i][...], group[i + 1][...]], axis=1) for i in (0, 2)] for group in sets
    ]
    for i, (left, right) in enumerate(((4, 0), (5, 0), (6, 1))):
        total = sum(mul(group[left][...], pair[right]) for group, pair in zip(sets, both))
        total = to_half(total)
        for s in range(out_ref.shape[0]):
            out_ref[s, i] = total[:width, s * LANES : (s + 1) * LANES]


def mixer_backward_kernel(
    place_ref, residual_ref, cot_ref, mine_ref, other_ref, home_refs, gain_ref,
    late_ref, recurrent_ref, gate_ref, query_ref, within_ref, group_ref,
    keep_own_ref, beside_own_ref, others_refs,
    grad_ref, half_ref, gain_grad_ref, recurrent_grad_ref, gate_grad_ref, group_grad_ref, state_grad_ref,
    send_ref, stay_ref, output_ref,
):
    @first_step
    def _():
        load_output(late_ref, output_ref)
        gain_grad_ref[...] = jnp.zeros_like(gain_grad_ref)
        group_grad_ref[...] = jnp.zeros_like(group_grad_ref)
        state_grad_ref[...] = jnp.zeros_like(state_grad_ref)

    residual = residual_ref[...]
    scale = lax.rsqrt(jnp.mean(residual * residual, axis=1, keepdims=True) + eps_norm)
    normed = residual * scale
    number = pl.num_programs(0) - 1 - pl.program_id(0)
    piece, holder = (number % 2, number // 2)
    home = jnp.where(
        piece == 0,
        from_core(place_ref, holder, home_refs[0][...], home_refs[1][...]),
        from_core(place_ref, holder, home_refs[2][...], home_refs[3][...]),
    )
    pulled = to_float(mine_ref[...]) + to_float(other_ref[...]) + to_float(home)
    gain_grad_ref[...] += jnp.sum(pulled * normed, axis=0, keepdims=True)
    weighted = pulled * gain_ref[1:2]
    grad = to_float(cot_ref[...]) + scale * (
        weighted - normed * jnp.mean(weighted * normed, axis=1, keepdims=True)
    )
    grad_ref[...] = grad
    grad = to_half(grad)
    half_ref[...] = grad

    chip, core = (place_ref[0], place_ref[1])
    columns = keep_own_ref.shape[2]
    own, other = [], []
    for b in range(2):
        low, high = (residual[:, (2 * b + l) * columns : (2 * b + l + 1) * columns] for l in range(2))
        own.append(to_float(keep_own_ref[b]) + to_float(beside_own_ref[b]) + jnp.where(core == 0, low, high))
        keep_other, beside_other = (
            to_float(jnp.where(piece == 0, first[b], second[b])) for first, second in (others_refs[:2], others_refs[2:])
        )
        other.append(keep_other + beside_other)
    for at, rows in enumerate((own, other)):
        send_ref[at] = to_half(jnp.where(chip == 0, rows[1], rows[0]))
        stay_ref[at] = jnp.where(chip == 0, rows[0], rows[1])

    for h, (k, v) in enumerate(zip(heads(LANES), heads(VALUES))):
        mixed_grad = mul(grad, output_ref[h], 1, 1)
        recurrent = recurrent_ref[:, v]
        gate = gate_ref[:, v]
        scale = lax.rsqrt(jnp.mean(recurrent * recurrent, axis=1, keepdims=True) + eps_norm)
        sigmoid = jax.nn.sigmoid(gate)
        silu = gate * sigmoid
        normed = recurrent * scale
        group = group_ref[...]
        pulled = mixed_grad * normed
        group_grad_ref[...] += jnp.sum(pulled * silu, axis=0, keepdims=True)
        gate_grad_ref[:, v] = to_half(pulled * group * sigmoid * (1.0 + gate * (1.0 - sigmoid)))
        weighted = mixed_grad * group * silu
        recurrent_grad = scale * (weighted - normed * jnp.mean(weighted * normed, axis=1, keepdims=True))
        recurrent_grad = to_half(recurrent_grad * LANES ** (-0.5))
        recurrent_grad_ref[:, v] = recurrent_grad
        sums = whole_tile(within_ref[:, k])
        queries = to_float(query_ref[:, k]) * jnp.exp(sums)
        state_grad_ref[h] = state_grad_ref[h] * jnp.exp(sums[TILE - 1 :]) + mul(recurrent_grad, queries, 0, 0)


def query_backward_kernel(
    query_ref, key_ref, value_ref, within_ref, recurrent_grad_ref, start_ref, gate_grad_ref, weight_ref,
    query_grad_ref, kept_ref, normed_grad_ref,
):
    causal = span_masks()[0]
    total = None
    for h, (k, v) in enumerate(zip(heads(LANES), heads(VALUES))):
        within = within_ref[:, k]
        pulled = recurrent_grad_ref[:, v]
        keys_in = to_float(key_ref[:, k]) * jnp.exp(-within)
        scores_grad = jnp.where(causal, mul(pulled, value_ref[:, v], 1, 1), 0.0)
        across = stacked([mul(pulled[span_rows(j)], start_ref[j, h]) for j in range(TILE // SPAN)])
        query_grad = (mul(scores_grad, keys_in) + across) * jnp.exp(within)
        query_half = to_half(query_grad)
        query_grad_ref[:, k] = query_half
        kept_ref[:, k] = query_grad * to_float(query_ref[:, k])
        part = mul(query_half, model_rows(weight_ref, h, 0), 1, 1) + mul(
            gate_grad_ref[:, v], model_rows(weight_ref, h, LANES, 2), 1, 1
        )
        total = part if total is None else total + part
    normed_grad_ref[...] = to_half(total)


def backward_kernel(
    query_ref, key_ref, value_ref, within_ref, recurrent_grad_ref, start_ref, slope_ref, rank_ref, kept_ref,
    normed_grad_ref, first_ref, expand_ref, later_ref,
    key_grad_ref, value_grad_ref, rank_grad_ref, expand_grad_ref, part_ref, state_grad_ref,
):
    @first_step
    def _():
        state_grad_ref[...] = later_ref[...]
        expand_grad_ref[...] = jnp.zeros_like(expand_grad_ref)

    causal, until, _ = span_masks()
    last = lax.broadcasted_iota(jnp.int32, (TILE, LANES), 0) % SPAN == SPAN - 1
    total = to_float(normed_grad_ref[...])
    sums_grads = []
    for h, (k, v) in enumerate(zip(heads(LANES), heads(VALUES))):
        within = within_ref[:, k]
        closings = ends(within)
        values = value_ref[:, v]
        pulled = recurrent_grad_ref[:, v]
        keys = to_float(key_ref[:, k])
        shrink = jnp.exp(-within)
        rest = jnp.exp(spread(closings) - within)
        queries = to_half(to_float(query_ref[:, k]) * jnp.exp(within))
        keys_in = keys * shrink
        keys_out = keys * rest
        keys_half = to_half(keys_out)
        scores = jnp.where(causal, mul(queries, keys_in, 1, 1), 0.0)
        scores_grad = jnp.where(causal, mul(pulled, values, 1, 1), 0.0)
        keys_in_grad = mul(scores_grad, queries, 0, 0)
        value_in_grad = mul(scores, pulled, 0, 0)
        later = state_grad_ref[h]
        keys_out_grads, value_out_grads, bounds = [], [], []
        for j in reversed(range(TILE // SPAN)):
            at = span_rows(j)
            later_half = to_half(later)
            decay = jnp.exp(closings[j])
            keys_out_grads.insert(0, mul(values[at], later_half))
            value_out_grads.insert(0, mul(keys_half[at], later_half, 1, 1))
            bounds.insert(0, jnp.sum(later * to_float(start_ref[j, h]), axis=0, keepdims=True) * decay)
            later = later * decay + mul(pulled[at], queries[at], 0, 0)
        state_grad_ref[h] = later
        keys_out_grad = stacked(keys_out_grads)
        value_grad = to_half(value_in_grad + stacked(value_out_grads))
        value_grad_ref[:, v] = value_grad
        key_grad = to_half(keys_in_grad * shrink + keys_out_grad * rest)
        key_grad_ref[:, k] = key_grad
        kept = keys_out_grad * keys_out
        bounds = [
            bound + jnp.sum(kept[span_rows(j)], axis=0, keepdims=True) for j, bound in enumerate(bounds)
        ]
        sums_grads.append(
            kept_ref[:, k] - keys_in_grad * keys_in - kept + jnp.where(last, spread(bounds), 0.0)
        )
        total = total + (
            mul(key_grad, model_rows(first_ref, h, 0), 1, 1)
            + mul(value_grad, model_rows(first_ref, h, LANES + 32, 2), 1, 1)
        )
    part_ref[...] = to_half(total)
    logit_grad = mul_ones(ones_where(until), jnp.concatenate(sums_grads, axis=1)) * slope_ref[...]
    rank_grad_ref[...] = mul(expand_ref[:16], logit_grad, 1, 1)
    expand_grad_ref[...] += mul(rank_ref[...], logit_grad, 0, 0)[:24]


def store_whole(place_ref, refs, packs):
    for h in range(2):
        for s in range(2):
            refs[0][h, s] = packs[h][s]


def store_sides(place_ref, refs, packs):
    keep_first, give_first, keep_second, give_second = refs
    cut = keep_first.shape[1]
    chip, side = (place_ref[0], place_ref[2])
    for s in range(2):
        low, high = (packs[h][s][:cut] for h in range(2))
        keep_first[s] = jnp.where(chip == 0, low, high)
        give_first[s] = jnp.where(chip == 0, high, low)
    for h in range(2):
        low, high = (packs[h][s][cut:] for s in range(2))
        keep_second[h, 0] = jnp.where(side == 0, low, high)
        give_second[h, 0] = jnp.where(side == 0, high, low)


def block_rows(total, s):
    rows = to_half(total[s * LANES : (s + 1) * LANES])
    return [rows[:, b * LANES : (b + 1) * LANES] for b in range(total.shape[1] // LANES)]


def weights_kernel(store, place_ref, rows_ref, first_ref, second_ref, *refs):
    rows = rows_ref[...]
    packs = []
    for k, v in zip(heads(LANES), heads(VALUES)):
        first, second = (mul(rows, first_ref[:, k]), mul(rows, second_ref[:, v]))
        packs.append([stacked(block_rows(first, s) + block_rows(second, s)) for s in range(2)])
    store(place_ref, refs, packs)


def late_weights_kernel(store, place_ref, rows_ref, query_ref, gate_ref, mixed_ref, grad_ref, *refs):
    rows = rows_ref[...]
    packs = []
    for k, v in zip(heads(LANES), heads(VALUES)):
        first, second = (mul(rows, query_ref[:, k]), mul(rows, gate_ref[:, v]))
        output = to_half(mul(mixed_ref[v, :], grad_ref[...]))
        packs.append(
            [
                stacked(block_rows(first, s) + block_rows(second, s) + [output[:, s * LANES : (s + 1) * LANES]])
                for s in range(2)
            ]
        )
    store(place_ref, refs, packs)


def inputs_backward_kernel(
    place_ref, x_ref, grad_ref, mine_ref, other_ref, rank_grad_ref, small_ref, gain_ref, normed_ref,
    out_ref, gain_grad_ref, squeeze_grad_ref,
):
    @first_step
    def _():
        gain_grad_ref[...] = jnp.zeros_like(gain_grad_ref)
        squeeze_grad_ref[...] = jnp.zeros_like(squeeze_grad_ref)

    rank_grad = to_half(rank_grad_ref[...])
    x = to_float(x_ref[...])
    scale = lax.rsqrt(jnp.mean(x * x, axis=1, keepdims=True) + eps_norm)
    normed = x * scale
    pulled = (
        to_float(mine_ref[...])
        + to_float(other_ref[...])
        + mul(rank_grad, small_ref[:16], 0, 0)
    )
    squeeze_grad_ref[...] += mul(rank_grad, normed_ref[...])
    gain_grad_ref[...] += jnp.sum(pulled * normed, axis=0, keepdims=True)
    weighted = pulled * gain_ref[0:1]
    grad = grad_ref[...] + scale * (weighted - normed * jnp.mean(weighted * normed, axis=1, keepdims=True))
    columns = out_ref.shape[2]
    for b in range(2):
        low, high = (grad[:, (2 * b + i) * columns : (2 * b + i + 1) * columns] for i in range(2))
        out_ref[b] = jnp.where(place_ref[1] == 0, low, high)


def adam_kernel(count, joins, *refs):
    grads = refs[: len(refs) - 6 * count - 2]
    refs = refs[len(grads) :]
    share, ins, outs = refs[0], refs[1 : 1 + 3 * count], refs[1 + 3 * count :]
    squares = outs[3 * count]
    squares[...] = jnp.zeros_like(squares)
    for p, (join, shared) in enumerate(joins):
        gradient = to_float(join(*grads))
        master, first, second = (ref[...].reshape(gradient.shape) for ref in ins[3 * p : 3 * p + 3])
        new_first, new_second, direction = adam_direction(master, gradient, first, second)
        for ref, value in zip(outs[3 * p : 3 * p + 3], (new_first, new_second, direction)):
            ref[...] = value.reshape(ref.shape)
        for row, value in ((p, master), (8 + p, direction)):
            total = value * value
            while total.ndim > 2:
                total = jnp.sum(total, axis=0)
            total = jnp.sum(jnp.sum(total, axis=0, keepdims=True), axis=1, keepdims=True)
            if shared:
                total = total * share[shared - 1 : shared, 0:1]
            squares[row : row + 1] = jnp.broadcast_to(total, (1, LANES))


def trust_kernel(rows, squares_ref, *refs):
    count = len(rows)
    for p, row in enumerate(rows):
        master, direction, out = refs[p], refs[count + p], refs[2 * count + p]
        norm = jnp.sqrt(squares_ref[row : row + 1, 0:1])
        ratio = norm / (jnp.sqrt(squares_ref[row + 8 : row + 9, 0:1]) + eps_adam)
        shape = (1,) * len(master.shape)
        out[...] = master[...] - (learn_rate * ratio).reshape(shape) * direction[...]


def whole_call(body, ins, outs):
    return pl.pallas_call(
        body,
        out_shape=[jax.ShapeDtypeStruct(shape, jnp.float32) for shape in outs],
        compiler_params=pltpu.CompilerParams(vmem_limit_bytes=WHOLE_LIMIT),
        cost_estimate=pl.CostEstimate(flops=1, bytes_accessed=0, transcendentals=0),
    )(*ins)


def adam_group(share, grads, joins, params):
    count = len(params)
    outs = []
    for param in params:
        outs += [param[0].shape] * 3
    results = whole_call(
        lambda *refs: adam_kernel(count, joins, *refs),
        list(grads) + [share] + [array for param in params for array in param],
        outs + [(16, LANES)],
    )
    return [tuple(results[3 * p : 3 * p + 3]) for p in range(count)], results[-1]


def adam_direction(master, gradient, first_moment, second_moment):
    fix_one = 1.0 - beta_one**STEP
    second_correction = 1.0 - beta_two**STEP
    new_first = beta_one * first_moment + (1.0 - beta_one) * gradient
    new_second = beta_two * second_moment + (1.0 - beta_two) * gradient * gradient
    update_direction = (
        new_first * (1.0 / fix_one) / (jnp.sqrt(new_second * (1.0 / second_correction)) + eps_adam)
        + decay_rate * master
    )
    return (new_first, new_second, update_direction)


def per_device(
    tokens,
    cotangent,
    query_weight,
    query_mean,
    query_square,
    value_weight,
    value_mean,
    value_square,
    squeeze_weight,
    squeeze_mean,
    squeeze_square,
    expand_weight,
    expand_mean,
    expand_square,
    group_weight,
    group_mean,
    group_square,
    output_weight,
    output_mean,
    output_square,
    ffn_weight,
    ffn_mean,
    ffn_square,
    down_weight,
    down_mean,
    down_square,
    norms_weight,
    norms_mean,
    norms_square,
):
    sequences, segment, column_count = tokens.shape
    head_index = lax.axis_index("head")
    chip, core = (head_index // 2, head_index % 2)
    rows = query_weight.shape[0]
    peers = lax.axis_size("seq")
    seq_index = lax.axis_index("seq")
    model_width = rows * peers
    key_width = query_weight.shape[2] // 2
    value_width = value_weight.shape[2] // 2
    ffn_width = ffn_weight.shape[2]
    ffn_padded = -(-ffn_width // 256) * 256
    rank_count = squeeze_weight.shape[1]
    half_segment = segment // 2
    steps = segment // TILE
    half, full = (jnp.bfloat16, jnp.float32)
    aligned = rows % LANES == 0
    blocks = model_width // LANES
    along = seq_bits()[:-1]
    beside = ("seq", 1)
    across = ("head", 2)

    side = bit_of("seq", 1)
    place = jnp.stack([chip, core, side]).astype(jnp.int32)

    ring = list(range(peers))
    if aligned:
        ring = ring[::2] + ring[1::2][::-1]

    def ring_block(at):
        return jnp.where(at < blocks // 2, 2 * at, 2 * blocks - 1 - 2 * at) if aligned else at

    ffn_mine = jnp.concatenate([jnp.moveaxis(ffn_weight, 0, 2), down_weight[None]])
    ffn_mine = to_half(ffn_mine if aligned else jnp.moveaxis(ffn_mine, 2, 1))
    small_mine = jnp.concatenate(
        [
            squeeze_weight.T,
            jnp.zeros((16 - rank_count, rows), jnp.float32),
            norms_weight,
            jnp.zeros((14, rows), jnp.float32),
        ]
    )
    key_mine = query_weight[:, 0, key_width:]
    value_mine = value_weight[:, 0, :value_width]
    late_mine = jnp.concatenate(
        [
            query_weight[:, 0, :key_width],
            value_weight[:, 0, value_width : value_width + LANES],
            value_weight[:, 0, value_width + LANES :],
        ]
    )
    rows_moved = swap(pick(tokens, 1 - chip)[None], *across)
    tokens_beside, cot_beside = (swap(tokens, "head", 1), swap(cotangent, "head", 1))
    moved_beside = swap(rows_moved, "head", 1)
    if aligned:
        value_mine, ffn_mine = tie((to_half(value_mine), ffn_mine))
        ffn_all = lax.all_gather(ffn_mine, "seq", axis=0, axis_index_groups=[ring])
        key_part, held = grow(to_half(jnp.concatenate([key_mine, small_mine])), [], along)
        value_part, held = grow(jnp.concatenate([value_mine[:, :LANES], value_mine[:, LANES:]]), [], along)
        late_mine = to_half(jnp.concatenate([late_mine, output_weight]))
        late_mine, key_part, value_part = tie((late_mine, key_part, value_part))
        late_part, late_held = grow(late_mine, [], along[:1])
        key_all = grown(*grow(key_part, held, [across, beside]))
        value_part, value_held = grow(value_part, held, [beside])
        late_part, key_all = tie((late_part, key_all))
        late_moved = swap(late_part, *along[1])
        value_all = grown(*grow(value_part, value_held, [across]))
        first_all = jnp.concatenate([key_all, value_all], axis=2)

        def next_links(halves, moved):
            grown_halves = [
                beside_each_other(a, other, held, link) for a, other, link in zip(halves, moved, (across, beside))
            ]
            return jnp.concatenate(
                [
                    grown(*grow(*grown_halves[0], [beside])),
                    grown(*grow(*grown_halves[1], [across])),
                ],
                axis=2,
            )

    else:
        ffn_all = lax.all_gather(ffn_mine, "seq", axis=0)
        ffn_all = ffn_all.reshape(blocks, LANES // rows, 3, rows, ffn_width)
        ffn_all = ffn_all.transpose(0, 2, 4, 1, 3).reshape(blocks, 3, ffn_width, LANES)
        stages = along + [across, beside]

        def gather_columns(part):
            part = gather_cube(to_half(part), stages)
            return jnp.moveaxis(part.reshape(2, blocks, LANES, part.shape[-1]), 3, 2)

        def gather_blocks(part):
            count = part.shape[0] // rows
            part = gather_cube(to_half(part), stages).reshape(2, peers, count, rows, LANES)
            part = jnp.moveaxis(part, 2, 1).reshape(2, count, blocks, LANES, LANES)
            return jnp.moveaxis(part, 1, 2).reshape(2, blocks, count * LANES, LANES)

        value_blocks = jnp.concatenate([value_mine[:, :LANES], value_mine[:, LANES:]])
        first_all = jnp.concatenate(
            [gather_blocks(key_mine), gather_columns(small_mine.T), gather_blocks(value_blocks)], axis=2
        )
        late_all = jnp.concatenate([gather_blocks(late_mine), gather_columns(output_weight.T)], axis=2)

    expand_columns = pick(expand_weight.reshape(rank_count + 1, 2, 2, key_width), core, 2)
    expand_columns = jnp.pad(
        expand_columns.reshape(rank_count + 1, 2 * key_width), ((0, LANES - 1 - rank_count), (0, 0))
    )
    (
        input_half, normed, keys, value_entries, rank_values, within, slope, block_state, log_block, gains, small_full,
    ) = call(
        project_kernel,
        steps,
        [
            (place, "smem"),
            (tokens, 1),
            (rows_moved, 1),
            (tokens_beside, 1),
            (moved_beside, 1),
            (first_all, None),
            (expand_columns, None),
        ],
        [
            ((segment, model_width), half, 0),
            ((segment, model_width), half, 0),
            ((segment, 2 * key_width), half, 0),
            ((segment, 2 * value_width), half, 0),
            ((segment, LANES), full, 0),
            ((segment, 2 * key_width), full, 0),
            ((segment, 2 * key_width), full, 0),
            ((2, value_width, key_width), full, None),
            ((1, 2 * key_width), full, None),
            ((8, model_width), full, None),
            ((LANES, model_width), half, None),
        ],
    )
    if aligned:
        late_moved, block_state, log_block = tie((late_moved, block_state, log_block))
        late_part, _ = beside_each_other(late_part, late_moved, late_held, along[1])
        links = {}
        for name, low, cut, high in (
            ("gate", 0, 11 * LANES // 8, 3 * LANES),
            ("output", 3 * LANES, 3 * LANES + 7 * LANES // 8, 5 * LANES),
        ):
            links[name] = [late_part[..., low:cut, :], late_part[..., cut:high, :]]

        def first_links(halves):
            return [swap(halves[0], *across), swap(halves[1], *beside)]

        def second_links(halves, moved):
            sides = [
                beside_each_other(a, other, held, link) for a, other, link in zip(halves, moved, (across, beside))
            ]
            return sides, [swap(sides[0][0], *beside), swap(sides[1][0], *across)]

        def whole_links(sides, moved):
            ends = [
                grown(*beside_each_other(*(a, other, a_held, link)))
                for (a, a_held), other, link in zip(sides, moved, (beside, across))
            ]
            return jnp.concatenate(ends, axis=2)

        gate_moved = first_links(links["gate"])
    cot_given = [pick(cotangent, 1 - chip), pick(cotangent, chip)]

    def project_late(gate_all):
        return call(
            project_late_kernel,
            steps,
            [(normed, 0), (gate_all, None)],
            [((segment, 2 * key_width), half, 0), ((segment, 2 * value_width), full, 0)],
        )

    beside_scan = {}

    def beside_forward(number, message):
        if not aligned:
            return message
        if number == 0:
            beside_scan["normed"] = normed.T
            message, beside_scan["normed"] = tie((message, beside_scan["normed"]))
        if number == 1:
            message, moved, cot_given[0] = tie((message, gate_moved, cot_given[0]))
            beside_scan["gate"] = second_links(links["gate"], moved)
            beside_scan["output"] = first_links(links["output"])
            beside_scan["cot"] = swap(cot_given[0], *across)
        if number == 2:
            gate_all = whole_links(*beside_scan["gate"])
            out = project_late(gate_all)
            message, out, output_moved, cot_given[1] = tie(
                (message, out, beside_scan["output"], cot_given[1])
            )
            beside_scan.update(gate=gate_all, out=out)
            beside_scan["output"] = second_links(links["output"], output_moved)
        return message

    block_decay = jnp.exp(log_block).reshape(2, 1, key_width)
    state_in = scan_blocks(block_decay, block_state, False, beside_forward)
    if aligned:
        gate_all = beside_scan["gate"]
        queries, gate_values = beside_scan["out"]
        cot_own_moved = beside_scan["cot"]
        normed_t = beside_scan["normed"]
    else:
        gate_all, output_all = (late_all[:, :, : 3 * LANES], late_all[:, :, 3 * LANES :])
        queries, gate_values = project_late(gate_all)
        cot_own_moved = swap(cot_given[0], *across)
        normed_t = normed.T
    recurrent, starts, mixed_half = call(
        forward_kernel,
        steps,
        [
            (queries, 0),
            (keys, 0),
            (value_entries, 0),
            (gate_values, 0),
            (within, 0),
            (state_in, None),
            (group_weight[None, :], None),
        ],
        [
            ((segment, 2 * value_width), full, 0),
            ((segment // SPAN, 2, value_width, key_width), half, 0),
            ((segment, 2 * value_width), half, 0),
        ],
        scratch=[pltpu.VMEM((2, value_width, key_width), jnp.float32)],
    )
    if aligned:
        output_sides, output_moved = beside_scan["output"]
        recurrent, mixed_half, output_moved, cot_own_moved = tie(
            (recurrent, mixed_half, output_moved, cot_own_moved)
        )
        output_all = whole_links(output_sides, output_moved)
    (mixer_part,) = call(
        mix_kernel,
        steps,
        [(mixed_half, 0), (output_all, None)],
        [((segment, model_width), half, 0)],
        scratch=[pltpu.VMEM((2, value_width, model_width), jnp.bfloat16)],
    )
    mixer_beside, cot_own_beside = (swap(mixer_part, "head", 1), swap(cot_own_moved, "head", 1))
    mixer_beside, cot_own_beside, mixed_t = tie((mixer_beside, cot_own_beside, mixed_half.T))
    residual, normed_two = call(
        residual_kernel,
        steps,
        [(input_half, 0), (mixer_part, 0), (mixer_beside, 0), (gains, None)],
        [((segment, model_width), full, 0), ((segment, model_width), half, 0)],
    )

    def piece_of(rows_of_all, p):
        return lax.dynamic_slice_in_dim(rows_of_all, core * half_segment + p * TILE, TILE, 0)

    moved = [swap(piece_of(normed_two, p), *across) for p in range(2)]
    normed_two, cot_given[1] = tie((normed_two, cot_given[1]))
    cot_other_moved = swap(cot_given[1], *across)

    def feed_forward(piece, mine, beside_mine, cots):
        other = piece is not None
        tiles = (4, lambda i: 2 * i + piece) if other else ()
        width = 2 * TILE if other else segment
        return call(
            lambda *refs: feed_forward_kernel(ring if aligned else range(blocks), other, *refs),
            width // TILE,
            [(place, "smem"), mine, beside_mine, (cotangent, 1, *tiles)]
            + [(cots[0], 0, *tiles), (cot_beside, 1, *tiles), (cots[1], 0, *tiles)]
            + [(ffn_all, None)],
            [((ffn_padded, width), half, 1)] * 3
            + [((2, width, column_count), half, 1)] * 2
            + [((width, model_width), half, 0)] * 2
            + ([((width, model_width), half, 0)] if other else [((TILE, model_width), half, None)]),
            scratch=[pltpu.VMEM((3, ffn_padded, model_width), jnp.bfloat16)],
        )

    own = feed_forward(None, (normed_two, 0), (place, "smem"), (cot_own_moved, cot_own_beside))
    moved[0], cot_other_moved, own = tie((moved[0], cot_other_moved, own))
    cots = (cot_other_moved, swap(cot_other_moved, "head", 1))
    others, homes = [], []
    for p in range(2):
        if p:
            moved[p], others[0] = tie((moved[p], others[0]))
        others.append(feed_forward(p, (moved[p], None), (swap(moved[p], "head", 1), None), cots))
        other_rows = others[p][5].reshape(2, TILE, model_width)
        other_sum = to_half(
            to_float(pick(other_rows, core)) + to_float(swap(pick(other_rows, 1 - core), "head", 1))
        )
        homes.append(swap(other_sum, *across))
    (ffn_grad,) = call(
        feed_forward_weights_kernel,
        4,
        [
            entry
            for rows_of_all, group in ((normed_two, own), (others[0][7], others[0]), (others[1][7], others[1]))
            for entry in (
                (rows_of_all, 1, blocks, lambda i: ring_block(2 * i)),
                (rows_of_all, 1, blocks, lambda i: ring_block(2 * i + 1)),
                (group[6], 1, blocks, lambda i: ring_block(2 * i)),
                (group[6], 1, blocks, lambda i: ring_block(2 * i + 1)),
                (group[1], None),
                (group[2], None),
                (group[0], None),
            )
        ],
        [((blocks, 3, ffn_width, LANES), half, 0)],
    )
    own_grad = own[5]
    beside_own = [swap(a, "head", 1) for a in (own_grad, own[4], others[0][4], others[1][4])]
    ffn_grad, beside_own = tie((ffn_grad, beside_own))
    own_beside, out_beside = (beside_own[0], beside_own[1:])
    homes, ffn_grad = tie((homes, ffn_grad))
    homes = [a for home in homes for a in (home, swap(home, "head", 1))]
    by_piece = (2, lambda i: i // 2)
    (
        residual_grad, residual_half, gain_two_grad, recurrent_grad, gate_grad, group_grad, state_in_grad,
        out_give, out_mine,
    ) = call(
        lambda *refs: mixer_backward_kernel(*refs[:5], refs[5:9], *refs[9:18], refs[18:22], *refs[22:]),
        steps,
        [
            (place, "smem"),
            (residual, 0),
            (own[6], 0),
            (own_grad, 0),
            (own_beside, 0),
            *[(home, None) for home in homes],
            (gains, None),
            (output_all, None),
            (recurrent, 0),
            (gate_values, 0),
            (queries, 0),
            (within, 0),
            (group_weight[None, :], None),
            (own[3], 1),
            (out_beside[0], 1),
            *[(a, 1, *by_piece) for a in (others[0][3], others[1][3], out_beside[1], out_beside[2])],
        ],
        [
            ((segment, model_width), full, 0),
            ((segment, model_width), half, 0),
            ((1, model_width), full, None),
            ((segment, 2 * value_width), half, 0),
            ((segment, 2 * value_width), half, 0),
            ((1, value_width), full, None),
            ((2, value_width, key_width), full, None),
            ((2, segment, column_count), half, 1),
            ((2, segment, column_count), full, 1),
        ],
        reverse=True,
        scratch=[pltpu.VMEM((2, value_width, model_width), jnp.bfloat16)],
    )
    if not aligned:
        ffn_grad = ffn_grad.reshape(blocks, 3, ffn_width, LANES // rows, rows)
        ffn_grad = ffn_grad.transpose(0, 3, 1, 4, 2).reshape(peers, 3, rows, ffn_width)
    if aligned:
        ffn_sum = lax.psum_scatter(
            ffn_grad, "seq", scatter_dimension=0, tiled=False, axis_index_groups=[ring]
        )
    else:
        ffn_sum = lax.psum_scatter(ffn_grad, "seq", scatter_dimension=0, tiled=False)
        ffn_sum = jnp.moveaxis(ffn_sum, 1, 2)

    out_moved = swap(out_give, *across)
    query_grad, kept, normed_grad = call(
        query_backward_kernel,
        steps,
        [
            (queries, 0),
            (keys, 0),
            (value_entries, 0),
            (within, 0),
            (recurrent_grad, 0),
            (starts, 0),
            (gate_grad, 0),
            (gate_all, None),
        ],
        [
            ((segment, 2 * key_width), half, 0),
            ((segment, 2 * key_width), full, 0),
            ((segment, model_width), half, 0),
        ],
    )
    def weights_call(body, count, ins):
        height = count * LANES
        if not aligned:
            outs = [((2, blocks, height, LANES), half, 1)]
        else:
            outs = [((blocks, height // 2, LANES), half, 0)] * 2
            outs += [((2, blocks // 2, height // 2, LANES), half, 1)] * 2
        store = store_sides if aligned else store_whole
        return call(lambda *refs: body(store, *refs), 4, [(place, "smem")] + ins, outs)

    late_grads = weights_call(
        late_weights_kernel,
        5,
        [(normed_t, 0), (query_grad, None), (gate_grad, None), (mixed_t, None), (residual_half, 1)],
    )
    beside_scan = {"first": (query_grad, kept, normed_grad), "second": late_grads}

    def beside_backward(number, message):
        which = {1: "first", 2: "second"}.get(number)
        if which and aligned:
            message, beside_scan[which] = tie((message, beside_scan[which]))
        return message

    later_grad = scan_blocks(block_decay, state_in_grad, True, beside_backward)
    (query_grad, kept, normed_grad), late_grads = (beside_scan["first"], beside_scan["second"])
    late_grads, later_grad, out_moved, ffn_sum = tie((late_grads, later_grad, out_moved, ffn_sum))
    back = along[::-1]
    if aligned:
        first_held = seq_bits()
        second_held = [across] + along

        def sides(grads):
            keep_first, give_first, keep_second, give_second = grads
            links = (2,) * len(first_held)
            return (
                [keep_first.reshape(links + keep_first.shape[1:]), keep_second.reshape(links + keep_second.shape[2:])],
                [swap(give_first.reshape(links + give_first.shape[1:]), *across),
                 swap(give_second.reshape(links + give_second.shape[2:]), *beside)],
            )

        def next_sides(kept, moved):
            splits = [
                split(to_float(a) + to_float(other), held, link)
                for a, other, held, link in zip(kept, moved, (first_held, second_held), (beside, across))
            ]
            return [a for a, _ in splits], [a for _, a in splits]

        def next_moved(gives):
            return [swap(gives[0], *beside), swap(gives[1], *across)]

        def joined(kept, moved):
            return jnp.concatenate([to_float(a) + to_float(b) for a, b in zip(kept, moved)], axis=-2)

        late_kept, late_moved = sides(late_grads)
    key_grad, value_grad, rank_grad_part, expand_grad, normed_part = call(
        backward_kernel,
        steps,
        [
            (queries, 0),
            (keys, 0),
            (value_entries, 0),
            (within, 0),
            (recurrent_grad, 0),
            (starts, 0),
            (slope, 0),
            (rank_values, 0),
            (kept, 0),
            (normed_grad, 0),
            (first_all, None),
            (expand_columns, None),
            (later_grad, None),
        ],
        [
            ((segment, 2 * key_width), half, 0),
            ((segment, 2 * value_width), half, 0),
            ((rank_count, segment), full, 1),
            ((24, 2 * key_width), full, None),
            ((segment, model_width), half, 0),
        ],
        reverse=True,
        scratch=[pltpu.VMEM((2, value_width, key_width), jnp.float32)],
    )
    if aligned:
        key_grad, value_grad, normed_part, rank_grad_part, late_moved = tie(
            (key_grad, value_grad, normed_part, rank_grad_part, late_moved)
        )
    normed_beside, rank_beside = (swap(normed_part, "head", 1), swap(rank_grad_part, "head", 1))
    state_grads = weights_call(
        weights_kernel, 3, [(normed_t, 0), (key_grad, None), (value_grad, None)]
    )
    normed_beside, rank_beside, state_grads = tie(
        (normed_beside, rank_beside, state_grads)
    )
    if aligned:
        state_kept, state_moved = sides(state_grads)
    rank_grad = rank_grad_part + rank_beside
    grad_cols, gain_one_grad, squeeze_grad = call(
        inputs_backward_kernel,
        steps,
        [
            (place, "smem"),
            (input_half, 0),
            (residual_grad, 0),
            (normed_part, 0),
            (normed_beside, 0),
            (rank_grad, 1),
            (small_full, None),
            (gains, None),
            (normed, 0),
        ],
        [
            ((2, segment, column_count), full, 1),
            ((1, model_width), full, None),
            ((rank_count, model_width), full, None),
        ],
    )
    once = jnp.where(jnp.arange(8) == 0, (head_index == 0).astype(jnp.float32), 0.25 / peers)
    share = jnp.broadcast_to(once[:, None], (8, LANES))
    by_width = lambda a: jnp.moveaxis(a, 0, 2)

    def optimize_early(ffn_sum):
        return adam_group(
            share,
            [ffn_sum],
            [(lambda g: g[:2], 0), (lambda g: g[2], 0)],
            [
                tuple(map(by_width, (ffn_weight, ffn_mean, ffn_square))),
                (down_weight, down_mean, down_square),
            ],
        )

    if aligned:
        state_moved, late_moved, gain_one_grad, squeeze_grad, grad_cols = tie(
            (state_moved, late_moved, gain_one_grad, squeeze_grad, grad_cols)
        )
    expand_pad = jnp.zeros((rank_count + 1, 2, 2, key_width), jnp.float32)
    expand_pad = lax.dynamic_update_index_in_dim(
        expand_pad, expand_grad[: rank_count + 1].reshape(rank_count + 1, 2, key_width), core, 2
    ).reshape(rank_count + 1, 4 * key_width)
    group_rows = jnp.pad(group_grad, ((0, rank_count), (0, model_width - 4 * key_width - value_width)))
    small_grad = jnp.concatenate(
        [
            0.5 * squeeze_grad,
            0.5 * gain_one_grad,
            0.5 * gain_two_grad,
            jnp.concatenate([expand_pad, group_rows], axis=1),
        ]
    )
    if aligned:
        small_grad = small_grad + swap(small_grad, "head", 1)
        state_kept, state_gives = next_sides(state_kept, state_moved)
        state_moved = next_moved(state_gives)
        small_moved = swap(small_grad, *across)
        late_kept, late_gives = next_sides(late_kept, late_moved)
        late_moved = next_moved(late_gives)
        grad_give = to_half(pick(grad_cols, 1 - chip))
        state_moved, small_moved, grad_give = tie((state_moved, small_moved, grad_give))
        state_kept, state_give = split(joined(state_kept, state_moved), along, back[0])
        state_moved = swap(state_give, *back[0])
        small_grad = small_grad + small_moved
        small_moved = swap(small_grad, *beside)
        state_moved, small_moved, late_moved = tie((state_moved, small_moved, late_moved))
        state_kept, state_give = split(to_float(state_kept) + to_float(state_moved), along[:-1], back[1])
        state_moved = swap(state_give, *back[1])
        small_grad = small_grad + small_moved
        small_moved = swap(small_grad, *back[0])
        late_kept, late_give = split(joined(late_kept, late_moved), along, back[0])
        late_moved = swap(late_give, *back[0])
        state_moved, small_moved = tie((state_moved, small_moved))
        state_sum = to_float(state_kept) + to_float(state_moved)
        small_grad = small_grad + small_moved
        small_moved = swap(small_grad, *back[1])
        early, early_squares = optimize_early(ffn_sum)
        early, early_squares, small_moved, late_moved = tie((early, early_squares, small_moved, late_moved))
        small_grad = small_grad + small_moved
        late_sum = shrink(to_float(late_kept) + to_float(late_moved), along[:-1], back[1:])[0]
        output_sum_grad = late_sum[3 * LANES :]
    else:

        def split_rows(a):
            a = a.reshape(2, blocks, 3, LANES // rows, rows, LANES)
            return jnp.moveaxis(a, 3, 2).reshape(2, peers, 3 * rows, LANES)

        late_sum = scatter_cube(split_rows(late_grads[0][:, :, : 3 * LANES]), [beside, across] + back)
        state_sum = scatter_cube(split_rows(state_grads[0]), [across, beside] + back)
        output_grad = late_grads[0][:, :, 3 * LANES :].reshape(2, blocks, value_width, LANES // rows, rows)
        output_grad = output_grad.transpose(0, 1, 3, 4, 2).reshape(2, peers, rows, value_width)
        output_sum_grad = scatter_cube(output_grad, [beside, across] + back).T
        grad_give = to_half(pick(grad_cols, 1 - chip))
        small_grad = sum_everywhere(small_grad)
        early, early_squares = optimize_early(ffn_sum)
    grad_home = to_float(swap(grad_give, *across))
    tokens_grad = jnp.stack(ordered(pick(grad_cols, chip), grad_home, chip))
    out_home = to_float(out_moved)
    block_out = to_half(jnp.stack(ordered(out_mine[0] + out_home[1], out_mine[1] + out_home[0], chip)))

    mine_grad = lax.dynamic_slice_in_dim(small_grad[: rank_count + 2], seq_index * rows, rows, 1)
    expand_total = small_grad[rank_count + 2 :, : 4 * key_width]
    group_total = small_grad[rank_count + 2 : rank_count + 3, 4 * key_width : 4 * key_width + value_width]

    late, late_squares = adam_group(
        share,
        [late_sum, state_sum, output_sum_grad, mine_grad, expand_total, group_total],
        [
            (lambda l, s, *_: jnp.concatenate([l[:rows], s[:rows]], axis=1), 0),
            (
                lambda l, s, *_: jnp.concatenate(
                    [s[rows : 2 * rows], s[2 * rows : 3 * rows], l[rows : 2 * rows], l[2 * rows : 3 * rows]],
                    axis=1,
                ),
                0,
            ),
            (lambda l, s, o, *_: o[...], 0),
            (lambda l, s, o, m, e, g: m[:rank_count], 1),
            (lambda l, s, o, m, e, g: m[rank_count:], 1),
            (lambda l, s, o, m, e, g: e[...], 2),
            (lambda l, s, o, m, e, g: g[...], 2),
        ],
        [
            (query_weight, query_mean, query_square),
            (value_weight, value_mean, value_square),
            (output_weight, output_mean, output_square),
            (squeeze_weight.T, squeeze_mean.T, squeeze_square.T),
            (norms_weight, norms_mean, norms_square),
            (expand_weight, expand_mean, expand_square),
            tuple(a[None, :] for a in (group_weight, group_mean, group_square)),
        ],
    )
    squares = sum_everywhere(jnp.concatenate([early_squares, late_squares]))
    masters = [
        by_width(ffn_weight), down_weight,
        query_weight, value_weight, output_weight, squeeze_weight.T, norms_weight,
        expand_weight, group_weight[None, :],
    ]
    moments = early + late
    news = whole_call(
        lambda *refs: trust_kernel([0, 1, 16, 17, 18, 19, 20, 21, 22], *refs),
        [squares] + masters + [moment[2] for moment in moments],
        [master.shape for master in masters],
    )
    triples = [(new,) + moment[:2] for new, moment in zip(news, moments)]
    ffn_out, down_out, query_out, value_out, output_out, squeeze_out, norms_out, expand_out, group_out = triples
    ffn_out = tuple(jnp.moveaxis(a, 2, 0) for a in ffn_out)
    squeeze_out = tuple(a.T for a in squeeze_out)
    group_out = tuple(a[0] for a in group_out)
    return (block_out, tokens_grad) + tuple(
        array
        for triple in (
            query_out, value_out, squeeze_out, expand_out, group_out, output_out, ffn_out, down_out, norms_out,
        )
        for array in triple
    )


def solution(mesh):
    in_specs = (
        P(None, "seq", "head"),
        P(None, "seq", "head"),
        P("seq", "head", None),
        P("seq", "head", None),
        P("seq", "head", None),
        P("seq", "head", None),
        P("seq", "head", None),
        P("seq", "head", None),
        P("seq", None),
        P("seq", None),
        P("seq", None),
        P(),
        P(),
        P(),
        P(),
        P(),
        P(),
        P("head", "seq"),
        P("head", "seq"),
        P("head", "seq"),
        P("seq", None, "head"),
        P("seq", None, "head"),
        P("seq", None, "head"),
        P("head", "seq"),
        P("head", "seq"),
        P("head", "seq"),
        P(None, "seq"),
        P(None, "seq"),
        P(None, "seq"),
    )
    out_specs = (
        P(None, "seq", "head"),
        P(None, "seq", "head"),
        P("seq", "head", None),
        P("seq", "head", None),
        P("seq", "head", None),
        P("seq", "head", None),
        P("seq", "head", None),
        P("seq", "head", None),
        P("seq", None),
        P("seq", None),
        P("seq", None),
        P(),
        P(),
        P(),
        P(),
        P(),
        P(),
        P("head", "seq"),
        P("head", "seq"),
        P("head", "seq"),
        P("seq", None, "head"),
        P("seq", None, "head"),
        P("seq", None, "head"),
        P("head", "seq"),
        P("head", "seq"),
        P("head", "seq"),
        P(None, "seq"),
        P(None, "seq"),
        P(None, "seq"),
    )
    return jax.shard_map(
        per_device, mesh=mesh, in_specs=in_specs, out_specs=out_specs, check_vma=False
    )
```

```python
import jax
import jax.numpy as jnp
from jax import lax
from jax.experimental import pallas as pl
from jax.experimental.pallas import tpu as pltpu
from jax.sharding import PartitionSpec as P

SPAN = 64
STEP = 10


eps_norm = 1e-06
gate_scale = 16.0
beta_one = 0.9
beta_two = 0.999
eps_adam = 1e-06
decay_rate = 0.01
learn_rate = 0.5
highest = lax.Precision.HIGHEST


def to_half(value_entries):
    return value_entries.astype(jnp.bfloat16)


def to_float(value_entries):
    return value_entries.astype(jnp.float32)


def mm(pattern, left, right):
    return jnp.einsum(pattern, left, right, preferred_element_type=jnp.float32)


def exact(pattern, left, right):
    return jnp.einsum(pattern, left, right, precision=highest)


def swap(value_entries, axis, bit):
    peers = lax.axis_size(axis)
    return lax.ppermute(value_entries, axis, [(i, i ^ bit) for i in range(peers)])


def bit_of(axis, bit):
    return (lax.axis_index(axis) // bit) % 2


def pick(value_entries, at, axis=0):
    return lax.dynamic_index_in_dim(value_entries, at, axis, keepdims=False)


def ordered(mine, other, upper):
    return (jnp.where(upper == 0, mine, other), jnp.where(upper == 0, other, mine))


def seq_bits():
    bits, bit = [], lax.axis_size("seq") // 2
    while bit:
        bits.append(("seq", bit))
        bit //= 2
    return bits


def cube_rank():
    return [("head", 2)] + seq_bits()


def beside_each_other(part, moved, held, stage):
    low, high = ordered(part, moved, bit_of(*stage))
    held = sorted(held + [stage], key=cube_rank().index)
    return jnp.stack([low, high], axis=held.index(stage)), held


def grow(part, held, stages):
    for stage in stages:
        part, held = beside_each_other(part, swap(part, *stage), held, stage)
    return part, held


def grown(part, held):
    return part.reshape((2, lax.axis_size("seq")) + part.shape[len(held) :])


def gather_cube(part, stages):
    return grown(*grow(part, [], stages))


def split(part, held, stage):
    if held is None:
        held = cube_rank()
        part = part.reshape((2,) * len(held) + part.shape[2:])
    at = held.index(stage)
    return pick(part, bit_of(*stage), at), to_half(pick(part, 1 - bit_of(*stage), at))


def shrink(part, held, stages, pin=lambda at, moved: moved):
    if held is None:
        held = cube_rank()
        part = part.reshape((2,) * len(held) + part.shape[2:])
    held = list(held)
    for number, (axis, bit) in enumerate(stages):
        at = held.index((axis, bit))
        held.pop(at)
        upper = bit_of(axis, bit)
        moved = pin(number, swap(to_half(pick(part, 1 - upper, at)), axis, bit))
        part = to_float(pick(part, upper, at)) + to_float(moved)
    return [part, held]


def scatter_cube(part, stages, pin=lambda at, moved: moved):
    return shrink(part, None, stages, pin)[0]


def sum_everywhere(value_entries):
    for axis, bit in [("head", 1), ("head", 2)] + seq_bits()[::-1]:
        value_entries = value_entries + swap(value_entries, axis, bit)
    return value_entries


tie = lax.optimization_barrier


def scan_blocks(decay, state, reverse, hook):
    before_decay, before_state = (jnp.ones_like(decay), jnp.zeros_like(state))
    size = state.shape[1]
    for number, (axis, bit) in enumerate(seq_bits()[::-1]):
        upper = bit_of(axis, bit) == (0 if reverse else 1)
        high = to_half(decay)
        low = to_half(decay - to_float(high))
        blank = jnp.zeros_like(state[:, :14], jnp.bfloat16)
        message = jnp.concatenate([to_half(state), high, low, blank], axis=1)
        message = to_float(hook(number, swap(message, axis, bit)))
        other_state = message[:, :size]
        other_decay = message[:, size : size + 1] + message[:, size + 1 : size + 2]
        before_state = jnp.where(upper, before_decay * other_state + before_state, before_state)
        before_decay = jnp.where(upper, before_decay * other_decay, before_decay)
        state = jnp.where(
            upper,
            decay * other_state + state,
            other_decay * state + other_state,
        )
        decay = decay * other_decay
    return before_state


TILE = 256
LANES = 128
VALUES = 256
VMEM_LIMIT = 47 * 1024 * 1024
WHOLE_LIMIT = 60 * 1024 * 1024


def mul(left, right, left_dim=1, right_dim=0):
    return lax.dot_general(
        to_half(left),
        to_half(right),
        (((left_dim,), (right_dim,)), ((), ())),
        preferred_element_type=jnp.float32,
    )


def mul_exact(left, right, left_dim=1, right_dim=0):
    return lax.dot_general(
        left,
        right,
        (((left_dim,), (right_dim,)), ((), ())),
        precision=highest,
        preferred_element_type=jnp.float32,
    )


def halves(value_entries):
    high = to_half(value_entries)
    return high, to_half(value_entries - to_float(high))


def mul_ones(ones, right):
    high, low = halves(right)
    return mul(ones, high) + mul(ones, low)


def span_masks():
    row = lax.broadcasted_iota(jnp.int32, (TILE, TILE), 0)
    column = lax.broadcasted_iota(jnp.int32, (TILE, TILE), 1)
    same = (row // SPAN) == (column // SPAN)
    return same & (row >= column), same & (row <= column), row >= column


def ones_where(mask):
    return jnp.where(mask, 1.0, 0.0).astype(jnp.bfloat16)


def log_sigmoid(z):
    decay = jnp.exp(-jnp.abs(z))
    ratio = decay / (2.0 + decay)
    square = ratio * ratio
    series = 1.0 / 15.0
    for odd in (13.0, 11.0, 9.0, 7.0, 5.0, 3.0, 1.0):
        series = series * square + 1.0 / odd
    return jnp.minimum(z, 0.0) - 2.0 * ratio * series


def call(body, steps, ins, outs, reverse=False, scratch=()):
    def spec(shape, axis, count=steps, at=lambda i: i):
        if axis == "smem":
            return pl.BlockSpec(memory_space=pltpu.SMEM)
        block = tuple(n // count if d == axis else n for d, n in enumerate(shape))

        def where(i):
            number = at(steps - 1 - i if reverse else i)
            return tuple(number if d == axis else 0 for d in range(len(shape)))

        return pl.BlockSpec(block, where)

    return pl.pallas_call(
        body,
        grid=(steps,),
        in_specs=[spec(entry[0].shape, *entry[1:]) for entry in ins],
        out_specs=[spec(shape, axis) for shape, _, axis in outs],
        out_shape=[jax.ShapeDtypeStruct(shape, dtype) for shape, dtype, _ in outs],
        scratch_shapes=list(scratch),
        compiler_params=pltpu.CompilerParams(vmem_limit_bytes=VMEM_LIMIT),
        cost_estimate=pl.CostEstimate(flops=1, bytes_accessed=0, transcendentals=0),
    )(*[entry[0] for entry in ins])


def heads(width):
    return [slice(h * width, (h + 1) * width) for h in range(2)]


def span_rows(j):
    return slice(j * SPAN, (j + 1) * SPAN)


def ends(within):
    return [within[(j + 1) * SPAN - 1 : (j + 1) * SPAN] for j in range(TILE // SPAN)]


def stacked(parts):
    return jnp.concatenate(parts, axis=0)


def spread(rows):
    return stacked([jnp.broadcast_to(row, (SPAN, row.shape[1])) for row in rows])


def whole_tile(within):
    offset, offsets = jnp.zeros_like(within[:1]), []
    for row in ends(within):
        offsets.append(offset)
        offset = offset + row
    return within + spread(offsets)


def four_blocks(place_ref, mine, moved, beside_mine, beside_moved):
    chip, core = (place_ref[0], place_ref[1])
    own = [jnp.where(chip == b, mine, moved) for b in range(2)]
    beside = [jnp.where(chip == b, beside_mine, beside_moved) for b in range(2)]
    return jnp.concatenate(
        [jnp.where(core == l, own[b], beside[b]) for b in range(2) for l in range(2)], axis=1
    )


def from_core(place_ref, number, mine, beside):
    return jnp.where(place_ref[1] == number, mine, beside)


def first_step(body):
    pl.when(pl.program_id(0) == 0)(body)


def model_rows(ref, h, first, blocks=1):
    parts = [
        ref[h, :, first + LANES * b : first + LANES * (b + 1), :].reshape(-1, LANES)
        for b in range(blocks)
    ]
    return parts[0] if blocks == 1 else jnp.concatenate(parts, axis=1)


def project_kernel(
    place_ref, tokens_ref, moved_ref, beside_ref, beside_moved_ref, first_ref, expand_ref,
    x_ref, normed_ref, key_out_ref, value_out_ref, rank_ref, within_ref, slope_ref, state_ref, log_ref, gain_ref, small_ref,
):
    @first_step
    def _():
        state_ref[...] = jnp.zeros_like(state_ref)
        log_ref[...] = jnp.zeros_like(log_ref)
        small_ref[32:] = jnp.zeros_like(small_ref[32:])
        for s in range(first_ref.shape[1]):
            small_ref[:32, s * LANES : (s + 1) * LANES] = first_ref[0, s, LANES : LANES + 32]
        gain_ref[...] = to_float(small_ref[16:24])

    chip = place_ref[0]
    x = four_blocks(
        place_ref, tokens_ref[chip], moved_ref[0], beside_ref[chip], beside_moved_ref[0]
    )
    x_ref[...] = x
    x = to_float(x)
    scale = lax.rsqrt(jnp.mean(x * x, axis=1, keepdims=True) + eps_norm)
    normed = to_half(x * scale * gain_ref[0:1])
    normed_ref[...] = normed
    key_weight = jnp.concatenate([model_rows(first_ref, h, 0) for h in range(2)], axis=1)
    keys = to_half(mul(normed, key_weight))
    key_out_ref[...] = keys
    values = [to_half(mul(normed, model_rows(first_ref, h, LANES + 32, 2))) for h in range(2)]
    for h, v in enumerate(heads(VALUES)):
        value_out_ref[:, v] = values[h]
    rank_values = mul(normed, small_ref[...], 1, 1)
    column = lax.broadcasted_iota(jnp.int32, rank_values.shape, 1)
    rank_values = jnp.where(column < 16, rank_values, jnp.where(column == 16, 1.0, 0.0))
    rank_ref[...] = rank_values
    rank_high, rank_low = halves(rank_values)
    expand_high, expand_low = halves(expand_ref[...])
    logits = mul(rank_high, expand_high) + (mul(rank_low, expand_high) + mul(rank_high, expand_low))
    decays = log_sigmoid(logits) * (1.0 / gate_scale)
    slope_ref[...] = 1.0 / (gate_scale * (1.0 + jnp.exp(logits)))
    sums = mul_ones(ones_where(span_masks()[2]), decays)
    log_ref[...] += sums[TILE - 1 :]
    for j in range(TILE // SPAN):
        part = sums[span_rows(j)]
        within_ref[span_rows(j), :] = part - sums[j * SPAN - 1 : j * SPAN] if j else part
    closing = sums[TILE - 1 :]
    rest = to_half(to_float(keys) * jnp.exp(closing - sums))
    decay = jnp.exp(closing)
    for h, k in enumerate(heads(LANES)):
        state_ref[h] = state_ref[h] * decay[:, k] + mul(values[h], rest[:, k], 0, 0)


def project_late_kernel(normed_ref, weight_ref, query_ref, gate_ref, normed_t_ref):
    normed = normed_ref[...]
    normed_t_ref[...] = normed.T
    for h, (k, v) in enumerate(zip(heads(LANES), heads(VALUES))):
        query_ref[:, k] = to_half(mul(normed, model_rows(weight_ref, h, 0)))
        gate_ref[:, v] = mul(normed, model_rows(weight_ref, h, LANES, 2))


def load_output(late_ref, output_ref):
    for s in range(late_ref.shape[1]):
        output_ref[:, :, s * LANES : (s + 1) * LANES] = late_ref[:, s]


def forward_kernel(
    query_ref, key_ref, value_ref, gate_ref, within_ref, incoming_ref, group_ref,
    recurrent_ref, start_ref, mixed_ref, state_ref,
):
    @first_step
    def _():
        state_ref[...] = incoming_ref[...]

    causal = span_masks()[0]
    for h, (k, v) in enumerate(zip(heads(LANES), heads(VALUES))):
        within = within_ref[:, k]
        closings = ends(within)
        values = value_ref[:, v]
        keys = to_float(key_ref[:, k])
        queries = to_half(to_float(query_ref[:, k]) * jnp.exp(within))
        scores = jnp.where(causal, mul(queries, keys * jnp.exp(-within), 1, 1), 0.0)
        inside = mul(scores, values)
        keys_out = to_half(keys * jnp.exp(spread(closings) - within))
        state = state_ref[h]
        across = []
        for j, closing in enumerate(closings):
            start = to_half(state)
            start_ref[j, h] = start
            across.append(mul(queries[span_rows(j)], start, 1, 1))
            state = state * jnp.exp(closing) + mul(values[span_rows(j)], keys_out[span_rows(j)], 0, 0)
        state_ref[h] = state
        recurrent = (inside + stacked(across)) * LANES ** (-0.5)
        recurrent_ref[:, v] = recurrent
        scale = lax.rsqrt(jnp.mean(recurrent * recurrent, axis=1, keepdims=True) + eps_norm)
        gate = gate_ref[:, v]
        mixed = to_half(recurrent * scale * group_ref[...] * (gate * jax.nn.sigmoid(gate)))
        mixed_ref[:, v] = mixed


def mix_kernel(mixed_ref, weight_ref, part_ref, mixed_t_ref, output_ref):
    @first_step
    def _():
        load_output(weight_ref, output_ref)

    mixed = mixed_ref[...]
    mixed_t_ref[...] = mixed.T
    part_ref[...] = to_half(mul(mixed, output_ref[...].reshape(2 * VALUES, -1)))


def residual_kernel(place_ref, x_ref, mine_ref, other_ref, gain_ref, residual_ref, normed_ref, *piece_refs):
    residual = to_float(x_ref[...]) + (to_float(mine_ref[...]) + to_float(other_ref[...]))
    scale = lax.rsqrt(jnp.mean(residual * residual, axis=1, keepdims=True) + eps_norm)
    residual_ref[...] = residual
    normed = to_half(residual * scale * gain_ref[1:2])
    normed_ref[...] = normed
    for p, piece_ref in enumerate(piece_refs):

        @pl.when(pl.program_id(0) == 2 * place_ref[1] + p)
        def _(piece_ref=piece_ref):
            piece_ref[...] = normed


def feed_forward_kernel(
    ring, other, place_ref, normed_ref, beside_normed_ref, cot_ref, moved_ref, beside_ref, beside_moved_ref, weight_ref,
    hidden_ref, gate_grad_ref, up_grad_ref, keep_ref, give_ref, *refs,
):
    if other:
        keep_rows_ref, give_rows_ref, cot_out_ref, normed_out_ref, all_ref = refs
    else:
        rows_grad_ref, cot_out_ref, all_ref = refs
    width = weight_ref.shape[2]

    @first_step
    def _():
        all_ref[:, width:] = jnp.zeros_like(all_ref[:, width:])
        for at, s in enumerate(ring):
            all_ref[:, :width, s * LANES : (s + 1) * LANES] = weight_ref[at]

    normed = normed_ref[...]
    if other:
        normed = from_core(place_ref, pl.program_id(0), normed, beside_normed_ref[...])
        normed_out_ref[...] = normed
    chip = place_ref[0]
    sequence = 1 - chip if other else chip
    moved, beside_moved = (moved_ref[...], beside_moved_ref[...])
    cot = four_blocks(place_ref, cot_ref[sequence], moved, beside_ref[sequence], beside_moved)
    cot_out_ref[...] = cot
    gate = mul(normed, all_ref[0], 1, 1)
    up = mul(normed, all_ref[1], 1, 1)
    hidden_grad = mul(cot, all_ref[2], 1, 1)
    sigmoid = jax.nn.sigmoid(gate)
    silu = gate * sigmoid
    hidden = to_half(silu * up)
    hidden_ref[...] = hidden.T
    gate_grad = to_half(hidden_grad * up * sigmoid * (1.0 + gate * (1.0 - sigmoid)))
    gate_grad_ref[...] = gate_grad.T
    up_grad = to_half(hidden_grad * silu)
    up_grad_ref[...] = up_grad.T
    rows_grad = to_half(mul(gate_grad, all_ref[0]) + mul(up_grad, all_ref[1]))
    if other:

        @pl.when(pl.program_id(0) == place_ref[1])
        def _():
            keep_rows_ref[...] = rows_grad

        @pl.when(pl.program_id(0) != place_ref[1])
        def _():
            give_rows_ref[...] = rows_grad

    else:
        rows_grad_ref[...] = rows_grad
    out = to_half(mul(hidden, all_ref[2]))
    columns = keep_ref.shape[2]
    for b in range(2):
        low, high = (out[:, (2 * b + l) * columns : (2 * b + l + 1) * columns] for l in range(2))
        keep_ref[b] = jnp.where(place_ref[1] == 0, low, high)
        give_ref[b] = jnp.where(place_ref[1] == 0, high, low)


def feed_forward_weights_kernel(*refs):
    sets, out_ref = [refs[7 * i : 7 * i + 7] for i in range(3)], refs[21]
    width = out_ref.shape[2]
    both = [
        [jnp.concatenate([group[i][...], group[i + 1][...]], axis=1) for i in (0, 2)] for group in sets
    ]
    for i, (left, right) in enumerate(((4, 0), (5, 0), (6, 1))):
        total = sum(mul(group[left][...], pair[right]) for group, pair in zip(sets, both))
        total = to_half(total)
        for s in range(out_ref.shape[0]):
            out_ref[s, i] = total[:width, s * LANES : (s + 1) * LANES]


def mixer_backward_kernel(
    place_ref, residual_ref, cot_ref, mine_ref, other_ref, home_refs, gain_ref,
    late_ref, recurrent_ref, gate_ref, query_ref, within_ref, group_ref,
    keep_own_ref, beside_own_ref, others_refs,
    grad_ref, half_ref, gain_grad_ref, recurrent_grad_ref, gate_grad_ref, group_grad_ref, state_grad_ref,
    send_ref, stay_ref, output_ref,
):
    @first_step
    def _():
        load_output(late_ref, output_ref)
        gain_grad_ref[...] = jnp.zeros_like(gain_grad_ref)
        group_grad_ref[...] = jnp.zeros_like(group_grad_ref)
        state_grad_ref[...] = jnp.zeros_like(state_grad_ref)

    residual = residual_ref[...]
    scale = lax.rsqrt(jnp.mean(residual * residual, axis=1, keepdims=True) + eps_norm)
    normed = residual * scale
    number = pl.num_programs(0) - 1 - pl.program_id(0)
    piece, holder = (number % 2, number // 2)
    home = jnp.where(
        piece == 0,
        from_core(place_ref, holder, home_refs[0][...], home_refs[1][...]),
        from_core(place_ref, holder, home_refs[2][...], home_refs[3][...]),
    )
    pulled = to_float(mine_ref[...]) + to_float(other_ref[...]) + to_float(home)
    gain_grad_ref[...] += jnp.sum(pulled * normed, axis=0, keepdims=True)
    weighted = pulled * gain_ref[1:2]
    grad = to_float(cot_ref[...]) + scale * (
        weighted - normed * jnp.mean(weighted * normed, axis=1, keepdims=True)
    )
    grad_ref[...] = grad
    grad = to_half(grad)
    half_ref[...] = grad

    chip, core = (place_ref[0], place_ref[1])
    columns = keep_own_ref.shape[2]
    own, other = [], []
    for b in range(2):
        low, high = (residual[:, (2 * b + l) * columns : (2 * b + l + 1) * columns] for l in range(2))
        own.append(to_float(keep_own_ref[b]) + to_float(beside_own_ref[b]) + jnp.where(core == 0, low, high))
        keep_other, beside_other = (
            to_float(jnp.where(piece == 0, first[b], second[b])) for first, second in (others_refs[:2], others_refs[2:])
        )
        other.append(keep_other + beside_other)
    for at, rows in enumerate((own, other)):
        send_ref[at] = to_half(jnp.where(chip == 0, rows[1], rows[0]))
        stay_ref[at] = jnp.where(chip == 0, rows[0], rows[1])

    for h, (k, v) in enumerate(zip(heads(LANES), heads(VALUES))):
        mixed_grad = mul(grad, output_ref[h], 1, 1)
        recurrent = recurrent_ref[:, v]
        gate = gate_ref[:, v]
        scale = lax.rsqrt(jnp.mean(recurrent * recurrent, axis=1, keepdims=True) + eps_norm)
        sigmoid = jax.nn.sigmoid(gate)
        silu = gate * sigmoid
        normed = recurrent * scale
        group = group_ref[...]
        pulled = mixed_grad * normed
        group_grad_ref[...] += jnp.sum(pulled * silu, axis=0, keepdims=True)
        gate_grad_ref[:, v] = to_half(pulled * group * sigmoid * (1.0 + gate * (1.0 - sigmoid)))
        weighted = mixed_grad * group * silu
        recurrent_grad = scale * (weighted - normed * jnp.mean(weighted * normed, axis=1, keepdims=True))
        recurrent_grad = to_half(recurrent_grad * LANES ** (-0.5))
        recurrent_grad_ref[:, v] = recurrent_grad
        sums = whole_tile(within_ref[:, k])
        queries = to_float(query_ref[:, k]) * jnp.exp(sums)
        state_grad_ref[h] = state_grad_ref[h] * jnp.exp(sums[TILE - 1 :]) + mul(recurrent_grad, queries, 0, 0)


def query_backward_kernel(
    query_ref, key_ref, value_ref, within_ref, recurrent_grad_ref, start_ref, gate_grad_ref, weight_ref,
    query_grad_ref, kept_ref, normed_grad_ref,
):
    causal = span_masks()[0]
    total = None
    for h, (k, v) in enumerate(zip(heads(LANES), heads(VALUES))):
        within = within_ref[:, k]
        pulled = recurrent_grad_ref[:, v]
        keys_in = to_float(key_ref[:, k]) * jnp.exp(-within)
        scores_grad = jnp.where(causal, mul(pulled, value_ref[:, v], 1, 1), 0.0)
        across = stacked([mul(pulled[span_rows(j)], start_ref[j, h]) for j in range(TILE // SPAN)])
        query_grad = (mul(scores_grad, keys_in) + across) * jnp.exp(within)
        query_half = to_half(query_grad)
        query_grad_ref[:, k] = query_half
        kept_ref[:, k] = query_grad * to_float(query_ref[:, k])
        part = mul(query_half, model_rows(weight_ref, h, 0), 1, 1) + mul(
            gate_grad_ref[:, v], model_rows(weight_ref, h, LANES, 2), 1, 1
        )
        total = part if total is None else total + part
    normed_grad_ref[...] = to_half(total)


def backward_kernel(
    query_ref, key_ref, value_ref, within_ref, recurrent_grad_ref, start_ref, slope_ref, rank_ref, kept_ref,
    normed_grad_ref, first_ref, expand_ref, later_ref,
    key_grad_ref, value_grad_ref, rank_grad_ref, expand_grad_ref, part_ref, state_grad_ref,
):
    @first_step
    def _():
        state_grad_ref[...] = later_ref[...]
        expand_grad_ref[...] = jnp.zeros_like(expand_grad_ref)

    causal, until, _ = span_masks()
    last = lax.broadcasted_iota(jnp.int32, (TILE, LANES), 0) % SPAN == SPAN - 1
    total = to_float(normed_grad_ref[...])
    sums_grads = []
    for h, (k, v) in enumerate(zip(heads(LANES), heads(VALUES))):
        within = within_ref[:, k]
        closings = ends(within)
        values = value_ref[:, v]
        pulled = recurrent_grad_ref[:, v]
        keys = to_float(key_ref[:, k])
        shrink = jnp.exp(-within)
        rest = jnp.exp(spread(closings) - within)
        queries = to_half(to_float(query_ref[:, k]) * jnp.exp(within))
        keys_in = keys * shrink
        keys_out = keys * rest
        keys_half = to_half(keys_out)
        scores = jnp.where(causal, mul(queries, keys_in, 1, 1), 0.0)
        scores_grad = jnp.where(causal, mul(pulled, values, 1, 1), 0.0)
        keys_in_grad = mul(scores_grad, queries, 0, 0)
        value_in_grad = mul(scores, pulled, 0, 0)
        later = state_grad_ref[h]
        keys_out_grads, value_out_grads, bounds = [], [], []
        for j in reversed(range(TILE // SPAN)):
            at = span_rows(j)
            later_half = to_half(later)
            decay = jnp.exp(closings[j])
            keys_out_grads.insert(0, mul(values[at], later_half))
            value_out_grads.insert(0, mul(keys_half[at], later_half, 1, 1))
            bounds.insert(0, jnp.sum(later * to_float(start_ref[j, h]), axis=0, keepdims=True) * decay)
            later = later * decay + mul(pulled[at], queries[at], 0, 0)
        state_grad_ref[h] = later
        keys_out_grad = stacked(keys_out_grads)
        value_grad = to_half(value_in_grad + stacked(value_out_grads))
        value_grad_ref[:, v] = value_grad
        key_grad = to_half(keys_in_grad * shrink + keys_out_grad * rest)
        key_grad_ref[:, k] = key_grad
        kept = keys_out_grad * keys_out
        bounds = [
            bound + jnp.sum(kept[span_rows(j)], axis=0, keepdims=True) for j, bound in enumerate(bounds)
        ]
        sums_grads.append(
            kept_ref[:, k] - keys_in_grad * keys_in - kept + jnp.where(last, spread(bounds), 0.0)
        )
        total = total + (
            mul(key_grad, model_rows(first_ref, h, 0), 1, 1)
            + mul(value_grad, model_rows(first_ref, h, LANES + 32, 2), 1, 1)
        )
    part_ref[...] = to_half(total)
    logit_grad = mul_ones(ones_where(until), jnp.concatenate(sums_grads, axis=1)) * slope_ref[...]
    rank_grad_ref[...] = mul(expand_ref[:16], logit_grad, 1, 1)
    expand_grad_ref[...] += mul(rank_ref[...], logit_grad, 0, 0)[:24]


def store_whole(place_ref, refs, packs):
    for h in range(2):
        for s in range(2):
            refs[0][h, s] = packs[h][s]


def store_sides(place_ref, refs, packs):
    keep_first, give_first, keep_second, give_second = refs
    cut = keep_first.shape[1]
    chip, side = (place_ref[0], place_ref[2])
    for s in range(2):
        low, high = (packs[h][s][:cut] for h in range(2))
        keep_first[s] = jnp.where(chip == 0, low, high)
        give_first[s] = jnp.where(chip == 0, high, low)
    for h in range(2):
        low, high = (packs[h][s][cut:] for s in range(2))
        keep_second[h, 0] = jnp.where(side == 0, low, high)
        give_second[h, 0] = jnp.where(side == 0, high, low)


def block_rows(total, s):
    rows = to_half(total[s * LANES : (s + 1) * LANES])
    return [rows[:, b * LANES : (b + 1) * LANES] for b in range(total.shape[1] // LANES)]


def weights_kernel(store, place_ref, rows_ref, first_ref, second_ref, *refs):
    rows = rows_ref[...]
    packs = []
    for k, v in zip(heads(LANES), heads(VALUES)):
        first, second = (mul(rows, first_ref[:, k]), mul(rows, second_ref[:, v]))
        packs.append([stacked(block_rows(first, s) + block_rows(second, s)) for s in range(2)])
    store(place_ref, refs, packs)


def late_weights_kernel(store, place_ref, rows_ref, query_ref, gate_ref, mixed_ref, grad_ref, *refs):
    rows = rows_ref[...]
    packs = []
    for k, v in zip(heads(LANES), heads(VALUES)):
        first, second = (mul(rows, query_ref[:, k]), mul(rows, gate_ref[:, v]))
        output = to_half(mul(mixed_ref[v, :], grad_ref[...]))
        packs.append(
            [
                stacked(block_rows(first, s) + block_rows(second, s) + [output[:, s * LANES : (s + 1) * LANES]])
                for s in range(2)
            ]
        )
    store(place_ref, refs, packs)


def inputs_backward_kernel(
    place_ref, x_ref, grad_ref, mine_ref, other_ref, rank_grad_ref, small_ref, gain_ref, normed_ref,
    out_ref, gain_grad_ref, squeeze_grad_ref,
):
    @first_step
    def _():
        gain_grad_ref[...] = jnp.zeros_like(gain_grad_ref)
        squeeze_grad_ref[...] = jnp.zeros_like(squeeze_grad_ref)

    rank_grad = to_half(rank_grad_ref[...])
    x = to_float(x_ref[...])
    scale = lax.rsqrt(jnp.mean(x * x, axis=1, keepdims=True) + eps_norm)
    normed = x * scale
    pulled = (
        to_float(mine_ref[...])
        + to_float(other_ref[...])
        + mul(rank_grad, small_ref[:16], 0, 0)
    )
    squeeze_grad_ref[...] += mul(rank_grad, normed_ref[...])
    gain_grad_ref[...] += jnp.sum(pulled * normed, axis=0, keepdims=True)
    weighted = pulled * gain_ref[0:1]
    grad = grad_ref[...] + scale * (weighted - normed * jnp.mean(weighted * normed, axis=1, keepdims=True))
    columns = out_ref.shape[2]
    for b in range(2):
        low, high = (grad[:, (2 * b + i) * columns : (2 * b + i + 1) * columns] for i in range(2))
        out_ref[b] = jnp.where(place_ref[1] == 0, low, high)


def adam_kernel(count, joins, *refs):
    grads = refs[: len(refs) - 6 * count - 2]
    refs = refs[len(grads) :]
    share, ins, outs = refs[0], refs[1 : 1 + 3 * count], refs[1 + 3 * count :]
    squares = outs[3 * count]
    squares[...] = jnp.zeros_like(squares)
    for p, (join, shared) in enumerate(joins):
        gradient = to_float(join(*grads))
        master, first, second = (ref[...].reshape(gradient.shape) for ref in ins[3 * p : 3 * p + 3])
        new_first, new_second, direction = adam_direction(master, gradient, first, second)
        for ref, value in zip(outs[3 * p : 3 * p + 3], (new_first, new_second, direction)):
            ref[...] = value.reshape(ref.shape)
        for row, value in ((p, master), (8 + p, direction)):
            total = value * value
            while total.ndim > 2:
                total = jnp.sum(total, axis=0)
            total = jnp.sum(jnp.sum(total, axis=0, keepdims=True), axis=1, keepdims=True)
            if shared:
                total = total * share[shared - 1 : shared, 0:1]
            squares[row : row + 1] = jnp.broadcast_to(total, (1, LANES))


def trust_kernel(rows, squares_ref, *refs):
    count = len(rows)
    for p, row in enumerate(rows):
        master, direction, out = refs[p], refs[count + p], refs[2 * count + p]
        norm = jnp.sqrt(squares_ref[row : row + 1, 0:1])
        ratio = norm / (jnp.sqrt(squares_ref[row + 8 : row + 9, 0:1]) + eps_adam)
        shape = (1,) * len(master.shape)
        out[...] = master[...] - (learn_rate * ratio).reshape(shape) * direction[...]


def whole_call(body, ins, outs):
    return pl.pallas_call(
        body,
        out_shape=[jax.ShapeDtypeStruct(shape, jnp.float32) for shape in outs],
        compiler_params=pltpu.CompilerParams(vmem_limit_bytes=WHOLE_LIMIT),
        cost_estimate=pl.CostEstimate(flops=1, bytes_accessed=0, transcendentals=0),
    )(*ins)


def adam_group(share, grads, joins, params):
    count = len(params)
    outs = []
    for param in params:
        outs += [param[0].shape] * 3
    results = whole_call(
        lambda *refs: adam_kernel(count, joins, *refs),
        list(grads) + [share] + [array for param in params for array in param],
        outs + [(16, LANES)],
    )
    return [tuple(results[3 * p : 3 * p + 3]) for p in range(count)], results[-1]


def adam_direction(master, gradient, first_moment, second_moment):
    fix_one = 1.0 - beta_one**STEP
    second_correction = 1.0 - beta_two**STEP
    new_first = beta_one * first_moment + (1.0 - beta_one) * gradient
    new_second = beta_two * second_moment + (1.0 - beta_two) * gradient * gradient
    update_direction = (
        new_first * (1.0 / fix_one) / (jnp.sqrt(new_second * (1.0 / second_correction)) + eps_adam)
        + decay_rate * master
    )
    return (new_first, new_second, update_direction)


def per_device(
    tokens,
    cotangent,
    query_weight,
    query_mean,
    query_square,
    value_weight,
    value_mean,
    value_square,
    squeeze_weight,
    squeeze_mean,
    squeeze_square,
    expand_weight,
    expand_mean,
    expand_square,
    group_weight,
    group_mean,
    group_square,
    output_weight,
    output_mean,
    output_square,
    ffn_weight,
    ffn_mean,
    ffn_square,
    down_weight,
    down_mean,
    down_square,
    norms_weight,
    norms_mean,
    norms_square,
):
    sequences, segment, column_count = tokens.shape
    head_index = lax.axis_index("head")
    chip, core = (head_index // 2, head_index % 2)
    rows = query_weight.shape[0]
    peers = lax.axis_size("seq")
    seq_index = lax.axis_index("seq")
    model_width = rows * peers
    key_width = query_weight.shape[2] // 2
    value_width = value_weight.shape[2] // 2
    ffn_width = ffn_weight.shape[2]
    ffn_padded = -(-ffn_width // 256) * 256
    rank_count = squeeze_weight.shape[1]
    half_segment = segment // 2
    steps = segment // TILE
    half, full = (jnp.bfloat16, jnp.float32)
    aligned = rows % LANES == 0
    blocks = model_width // LANES
    along = seq_bits()[:-1]
    beside = ("seq", 1)
    across = ("head", 2)

    side = bit_of("seq", 1)
    place = jnp.stack([chip, core, side]).astype(jnp.int32)

    ring = list(range(peers))
    if aligned:
        ring = ring[::2] + ring[1::2][::-1]

    def ring_block(at):
        return jnp.where(at < blocks // 2, 2 * at, 2 * blocks - 1 - 2 * at) if aligned else at

    ffn_mine = jnp.concatenate([jnp.moveaxis(ffn_weight, 0, 2), down_weight[None]])
    ffn_mine = to_half(ffn_mine if aligned else jnp.moveaxis(ffn_mine, 2, 1))
    small_mine = jnp.concatenate(
        [
            squeeze_weight.T,
            jnp.zeros((16 - rank_count, rows), jnp.float32),
            norms_weight,
            jnp.zeros((14, rows), jnp.float32),
        ]
    )
    key_mine = query_weight[:, 0, key_width:]
    value_mine = value_weight[:, 0, :value_width]
    late_mine = jnp.concatenate(
        [
            query_weight[:, 0, :key_width],
            value_weight[:, 0, value_width : value_width + LANES],
            value_weight[:, 0, value_width + LANES :],
        ]
    )
    rows_moved = swap(pick(tokens, 1 - chip)[None], *across)
    tokens_beside, cot_beside = (swap(tokens, "head", 1), swap(cotangent, "head", 1))
    moved_beside = swap(rows_moved, "head", 1)
    if aligned:
        value_mine, ffn_mine = tie((to_half(value_mine), ffn_mine))
        ffn_all = lax.all_gather(ffn_mine, "seq", axis=0, axis_index_groups=[ring])
        key_part, held = grow(to_half(jnp.concatenate([key_mine, small_mine])), [], along)
        value_part, held = grow(jnp.concatenate([value_mine[:, :LANES], value_mine[:, LANES:]]), [], along)
        late_mine = to_half(jnp.concatenate([late_mine, output_weight]))
        late_mine, key_part, value_part = tie((late_mine, key_part, value_part))
        late_part, late_held = grow(late_mine, [], along[:1])
        key_all = grown(*grow(key_part, held, [across, beside]))
        value_part, value_held = grow(value_part, held, [beside])
        late_part, key_all = tie((late_part, key_all))
        late_moved = swap(late_part, *along[1])
        value_all = grown(*grow(value_part, value_held, [across]))
        first_all = jnp.concatenate([key_all, value_all], axis=2)

        def next_links(halves, moved):
            grown_halves = [
                beside_each_other(a, other, held, link) for a, other, link in zip(halves, moved, (across, beside))
            ]
            return jnp.concatenate(
                [
                    grown(*grow(*grown_halves[0], [beside])),
                    grown(*grow(*grown_halves[1], [across])),
                ],
                axis=2,
            )

    else:
        ffn_all = lax.all_gather(ffn_mine, "seq", axis=0)
        ffn_all = ffn_all.reshape(blocks, LANES // rows, 3, rows, ffn_width)
        ffn_all = ffn_all.transpose(0, 2, 4, 1, 3).reshape(blocks, 3, ffn_width, LANES)
        stages = along + [across, beside]

        def gather_columns(part):
            part = gather_cube(to_half(part), stages)
            return jnp.moveaxis(part.reshape(2, blocks, LANES, part.shape[-1]), 3, 2)

        def gather_blocks(part):
            count = part.shape[0] // rows
            part = gather_cube(to_half(part), stages).reshape(2, peers, count, rows, LANES)
            part = jnp.moveaxis(part, 2, 1).reshape(2, count, blocks, LANES, LANES)
            return jnp.moveaxis(part, 1, 2).reshape(2, blocks, count * LANES, LANES)

        value_blocks = jnp.concatenate([value_mine[:, :LANES], value_mine[:, LANES:]])
        first_all = jnp.concatenate(
            [gather_blocks(key_mine), gather_columns(small_mine.T), gather_blocks(value_blocks)], axis=2
        )
        late_all = jnp.concatenate([gather_blocks(late_mine), gather_columns(output_weight.T)], axis=2)

    expand_columns = pick(expand_weight.reshape(rank_count + 1, 2, 2, key_width), core, 2)
    expand_columns = jnp.pad(
        expand_columns.reshape(rank_count + 1, 2 * key_width), ((0, LANES - 1 - rank_count), (0, 0))
    )
    (
        input_half, normed, keys, value_entries, rank_values, within, slope, block_state, log_block, gains, small_full,
    ) = call(
        project_kernel,
        steps,
        [
            (place, "smem"),
            (tokens, 1),
            (rows_moved, 1),
            (tokens_beside, 1),
            (moved_beside, 1),
            (first_all, None),
            (expand_columns, None),
        ],
        [
            ((segment, model_width), half, 0),
            ((segment, model_width), half, 0),
            ((segment, 2 * key_width), half, 0),
            ((segment, 2 * value_width), half, 0),
            ((segment, LANES), full, 0),
            ((segment, 2 * key_width), full, 0),
            ((segment, 2 * key_width), full, 0),
            ((2, value_width, key_width), full, None),
            ((1, 2 * key_width), full, None),
            ((8, model_width), full, None),
            ((LANES, model_width), half, None),
        ],
    )
    if aligned:
        late_moved, block_state, log_block = tie((late_moved, block_state, log_block))
        late_part, _ = beside_each_other(late_part, late_moved, late_held, along[1])
        links = {}
        for name, low, cut, high in (
            ("gate", 0, 11 * LANES // 8, 3 * LANES),
            ("output", 3 * LANES, 3 * LANES + 7 * LANES // 8, 5 * LANES),
        ):
            links[name] = [late_part[..., low:cut, :], late_part[..., cut:high, :]]

        def first_links(halves):
            return [swap(halves[0], *across), swap(halves[1], *beside)]

        def second_links(halves, moved):
            sides = [
                beside_each_other(a, other, held, link) for a, other, link in zip(halves, moved, (across, beside))
            ]
            return sides, [swap(sides[0][0], *beside), swap(sides[1][0], *across)]

        def whole_links(sides, moved):
            ends = [
                grown(*beside_each_other(*(a, other, a_held, link)))
                for (a, a_held), other, link in zip(sides, moved, (beside, across))
            ]
            return jnp.concatenate(ends, axis=2)

        gate_moved = first_links(links["gate"])
    cot_given = [pick(cotangent, 1 - chip), pick(cotangent, chip)]

    def project_late(gate_all):
        return call(
            project_late_kernel,
            steps,
            [(normed, 0), (gate_all, None)],
            [
                ((segment, 2 * key_width), half, 0),
                ((segment, 2 * value_width), full, 0),
                ((model_width, segment), half, 1),
            ],
        )

    beside_scan = {}

    def beside_forward(number, message):
        if not aligned:
            return message
        if number == 0:
            message, moved, cot_given[0] = tie((message, gate_moved, cot_given[0]))
            beside_scan["gate"] = second_links(links["gate"], moved)
            beside_scan["output"] = first_links(links["output"])
            beside_scan["cot"] = swap(cot_given[0], *across)
        if number == 2:
            gate_all = whole_links(*beside_scan["gate"])
            out = project_late(gate_all)
            message, out, output_moved, cot_given[1] = tie(
                (message, out, beside_scan["output"], cot_given[1])
            )
            beside_scan.update(gate=gate_all, out=out)
            beside_scan["output"] = second_links(links["output"], output_moved)
        return message

    block_decay = jnp.exp(log_block).reshape(2, 1, key_width)
    state_in = scan_blocks(block_decay, block_state, False, beside_forward)
    if aligned:
        gate_all = beside_scan["gate"]
        queries, gate_values, normed_t = beside_scan["out"]
        cot_own_moved = beside_scan["cot"]
    else:
        gate_all, output_all = (late_all[:, :, : 3 * LANES], late_all[:, :, 3 * LANES :])
        queries, gate_values, normed_t = project_late(gate_all)
        cot_own_moved = swap(cot_given[0], *across)
    recurrent, starts, mixed_half = call(
        forward_kernel,
        steps,
        [
            (queries, 0),
            (keys, 0),
            (value_entries, 0),
            (gate_values, 0),
            (within, 0),
            (state_in, None),
            (group_weight[None, :], None),
        ],
        [
            ((segment, 2 * value_width), full, 0),
            ((segment // SPAN, 2, value_width, key_width), half, 0),
            ((segment, 2 * value_width), half, 0),
        ],
        scratch=[pltpu.VMEM((2, value_width, key_width), jnp.float32)],
    )
    if aligned:
        output_sides, output_moved = beside_scan["output"]
        recurrent, mixed_half, output_moved, cot_own_moved = tie(
            (recurrent, mixed_half, output_moved, cot_own_moved)
        )
        output_all = whole_links(output_sides, output_moved)
    mixer_part, mixed_t = call(
        mix_kernel,
        steps,
        [(mixed_half, 0), (output_all, None)],
        [((segment, model_width), half, 0), ((2 * value_width, segment), half, 1)],
        scratch=[pltpu.VMEM((2, value_width, model_width), jnp.bfloat16)],
    )
    mixer_beside, cot_own_beside = (swap(mixer_part, "head", 1), swap(cot_own_moved, "head", 1))
    mixer_beside, cot_own_beside = tie((mixer_beside, cot_own_beside))
    residual, normed_two, *pieces = call(
        residual_kernel,
        steps,
        [(place, "smem"), (input_half, 0), (mixer_part, 0), (mixer_beside, 0), (gains, None)],
        [((segment, model_width), full, 0), ((segment, model_width), half, 0)]
        + [((TILE, model_width), half, None)] * 2,
    )

    moved = [swap(piece, *across) for piece in pieces]
    normed_two, cot_given[1] = tie((normed_two, cot_given[1]))
    cot_other_moved = swap(cot_given[1], *across)

    def feed_forward(piece, mine, beside_mine, cots):
        other = piece is not None
        tiles = (4, lambda i: 2 * i + piece) if other else ()
        width = 2 * TILE if other else segment
        return call(
            lambda *refs: feed_forward_kernel(ring if aligned else range(blocks), other, *refs),
            width // TILE,
            [(place, "smem"), mine, beside_mine, (cotangent, 1, *tiles)]
            + [(cots[0], 0, *tiles), (cot_beside, 1, *tiles), (cots[1], 0, *tiles)]
            + [(ffn_all, None)],
            [((ffn_padded, width), half, 1)] * 3
            + [((2, width, column_count), half, 1)] * 2
            + ([((TILE, model_width), half, None)] * 2 if other else [((width, model_width), half, 0)])
            + [((width, model_width), half, 0)] * (2 if other else 1),
            scratch=[pltpu.VMEM((3, ffn_padded, model_width), jnp.bfloat16)],
        )

    own = feed_forward(None, (normed_two, 0), (place, "smem"), (cot_own_moved, cot_own_beside))
    moved[0], cot_other_moved, own = tie((moved[0], cot_other_moved, own))
    cots = (cot_other_moved, swap(cot_other_moved, "head", 1))
    others, sums, homes = [], [], []
    for p in range(2):
        if p:
            moved[p], sums[0] = tie((moved[p], sums[0]))
            homes.append(swap(sums[0], *across))
        others.append(feed_forward(p, (moved[p], None), (swap(moved[p], "head", 1), None), cots))
        if not p:
            moved[1], others[0] = tie((moved[1], others[0]))
        sums.append(to_half(to_float(others[p][5]) + to_float(swap(others[p][6], "head", 1))))
    homes[0], others[1] = tie((homes[0], others[1]))
    homes.append(swap(sums[1], *across))
    (ffn_grad,) = call(
        feed_forward_weights_kernel,
        4,
        [
            entry
            for rows_of_all, cot_of_all, group in (
                (normed_two, own[6], own), (others[0][8], others[0][7], others[0]), (others[1][8], others[1][7], others[1])
            )
            for entry in (
                (rows_of_all, 1, blocks, lambda i: ring_block(2 * i)),
                (rows_of_all, 1, blocks, lambda i: ring_block(2 * i + 1)),
                (cot_of_all, 1, blocks, lambda i: ring_block(2 * i)),
                (cot_of_all, 1, blocks, lambda i: ring_block(2 * i + 1)),
                (group[1], None),
                (group[2], None),
                (group[0], None),
            )
        ],
        [((blocks, 3, ffn_width, LANES), half, 0)],
    )
    own_grad = own[5]
    beside_own = [swap(a, "head", 1) for a in (own_grad, own[4], others[0][4], others[1][4])]
    ffn_grad, beside_own = tie((ffn_grad, beside_own))
    own_beside, out_beside = (beside_own[0], beside_own[1:])
    homes, ffn_grad = tie((homes, ffn_grad))
    homes = [a for home in homes for a in (home, swap(home, "head", 1))]
    by_piece = (2, lambda i: i // 2)
    (
        residual_grad, residual_half, gain_two_grad, recurrent_grad, gate_grad, group_grad, state_in_grad,
        out_give, out_mine,
    ) = call(
        lambda *refs: mixer_backward_kernel(*refs[:5], refs[5:9], *refs[9:18], refs[18:22], *refs[22:]),
        steps,
        [
            (place, "smem"),
            (residual, 0),
            (own[6], 0),
            (own_grad, 0),
            (own_beside, 0),
            *[(home, None) for home in homes],
            (gains, None),
            (output_all, None),
            (recurrent, 0),
            (gate_values, 0),
            (queries, 0),
            (within, 0),
            (group_weight[None, :], None),
            (own[3], 1),
            (out_beside[0], 1),
            *[(a, 1, *by_piece) for a in (others[0][3], others[1][3], out_beside[1], out_beside[2])],
        ],
        [
            ((segment, model_width), full, 0),
            ((segment, model_width), half, 0),
            ((1, model_width), full, None),
            ((segment, 2 * value_width), half, 0),
            ((segment, 2 * value_width), half, 0),
            ((1, value_width), full, None),
            ((2, value_width, key_width), full, None),
            ((2, segment, column_count), half, 1),
            ((2, segment, column_count), full, 1),
        ],
        reverse=True,
        scratch=[pltpu.VMEM((2, value_width, model_width), jnp.bfloat16)],
    )
    if not aligned:
        ffn_grad = ffn_grad.reshape(blocks, 3, ffn_width, LANES // rows, rows)
        ffn_grad = ffn_grad.transpose(0, 3, 1, 4, 2).reshape(peers, 3, rows, ffn_width)
    if aligned:
        ffn_sum = lax.psum_scatter(
            ffn_grad, "seq", scatter_dimension=0, tiled=False, axis_index_groups=[ring]
        )
    else:
        ffn_sum = lax.psum_scatter(ffn_grad, "seq", scatter_dimension=0, tiled=False)
        ffn_sum = jnp.moveaxis(ffn_sum, 1, 2)

    out_moved = swap(out_give, *across)
    query_grad, kept, normed_grad = call(
        query_backward_kernel,
        steps,
        [
            (queries, 0),
            (keys, 0),
            (value_entries, 0),
            (within, 0),
            (recurrent_grad, 0),
            (starts, 0),
            (gate_grad, 0),
            (gate_all, None),
        ],
        [
            ((segment, 2 * key_width), half, 0),
            ((segment, 2 * key_width), full, 0),
            ((segment, model_width), half, 0),
        ],
    )
    def weights_call(body, count, ins):
        height = count * LANES
        if not aligned:
            outs = [((2, blocks, height, LANES), half, 1)]
        else:
            outs = [((blocks, height // 2, LANES), half, 0)] * 2
            outs += [((2, blocks // 2, height // 2, LANES), half, 1)] * 2
        store = store_sides if aligned else store_whole
        return call(lambda *refs: body(store, *refs), 4, [(place, "smem")] + ins, outs)

    late_grads = weights_call(
        late_weights_kernel,
        5,
        [(normed_t, 0), (query_grad, None), (gate_grad, None), (mixed_t, None), (residual_half, 1)],
    )
    beside_scan = {"first": (query_grad, kept, normed_grad), "second": late_grads}

    def beside_backward(number, message):
        which = {1: "first", 2: "second"}.get(number)
        if which and aligned:
            message, beside_scan[which] = tie((message, beside_scan[which]))
        return message

    later_grad = scan_blocks(block_decay, state_in_grad, True, beside_backward)
    (query_grad, kept, normed_grad), late_grads = (beside_scan["first"], beside_scan["second"])
    late_grads, later_grad, out_moved, ffn_sum = tie((late_grads, later_grad, out_moved, ffn_sum))
    back = along[::-1]
    if aligned:
        first_held = seq_bits()
        second_held = [across] + along

        def sides(grads):
            keep_first, give_first, keep_second, give_second = grads
            links = (2,) * len(first_held)
            return (
                [keep_first.reshape(links + keep_first.shape[1:]), keep_second.reshape(links + keep_second.shape[2:])],
                [swap(give_first.reshape(links + give_first.shape[1:]), *across),
                 swap(give_second.reshape(links + give_second.shape[2:]), *beside)],
            )

        def next_sides(kept, moved):
            splits = [
                split(to_float(a) + to_float(other), held, link)
                for a, other, held, link in zip(kept, moved, (first_held, second_held), (beside, across))
            ]
            return [a for a, _ in splits], [a for _, a in splits]

        def next_moved(gives):
            return [swap(gives[0], *beside), swap(gives[1], *across)]

        def joined(kept, moved):
            return jnp.concatenate([to_float(a) + to_float(b) for a, b in zip(kept, moved)], axis=-2)

        late_kept, late_moved = sides(late_grads)
    key_grad, value_grad, rank_grad_part, expand_grad, normed_part = call(
        backward_kernel,
        steps,
        [
            (queries, 0),
            (keys, 0),
            (value_entries, 0),
            (within, 0),
            (recurrent_grad, 0),
            (starts, 0),
            (slope, 0),
            (rank_values, 0),
            (kept, 0),
            (normed_grad, 0),
            (first_all, None),
            (expand_columns, None),
            (later_grad, None),
        ],
        [
            ((segment, 2 * key_width), half, 0),
            ((segment, 2 * value_width), half, 0),
            ((rank_count, segment), full, 1),
            ((24, 2 * key_width), full, None),
            ((segment, model_width), half, 0),
        ],
        reverse=True,
        scratch=[pltpu.VMEM((2, value_width, key_width), jnp.float32)],
    )
    if aligned:
        key_grad, value_grad, normed_part, rank_grad_part, late_moved = tie(
            (key_grad, value_grad, normed_part, rank_grad_part, late_moved)
        )
    normed_beside, rank_beside = (swap(normed_part, "head", 1), swap(rank_grad_part, "head", 1))
    state_grads = weights_call(
        weights_kernel, 3, [(normed_t, 0), (key_grad, None), (value_grad, None)]
    )
    normed_beside, rank_beside, state_grads = tie(
        (normed_beside, rank_beside, state_grads)
    )
    if aligned:
        state_kept, state_moved = sides(state_grads)
    rank_grad = rank_grad_part + rank_beside
    grad_cols, gain_one_grad, squeeze_grad = call(
        inputs_backward_kernel,
        steps,
        [
            (place, "smem"),
            (input_half, 0),
            (residual_grad, 0),
            (normed_part, 0),
            (normed_beside, 0),
            (rank_grad, 1),
            (small_full, None),
            (gains, None),
            (normed, 0),
        ],
        [
            ((2, segment, column_count), full, 1),
            ((1, model_width), full, None),
            ((rank_count, model_width), full, None),
        ],
    )
    once = jnp.where(jnp.arange(8) == 0, (head_index == 0).astype(jnp.float32), 0.25 / peers)
    share = jnp.broadcast_to(once[:, None], (8, LANES))
    by_width = lambda a: jnp.moveaxis(a, 0, 2)

    def optimize_early(ffn_sum):
        return adam_group(
            share,
            [ffn_sum],
            [(lambda g: g[:2], 0), (lambda g: g[2], 0)],
            [
                tuple(map(by_width, (ffn_weight, ffn_mean, ffn_square))),
                (down_weight, down_mean, down_square),
            ],
        )

    if aligned:
        state_moved, late_moved, gain_one_grad, squeeze_grad, grad_cols = tie(
            (state_moved, late_moved, gain_one_grad, squeeze_grad, grad_cols)
        )
    expand_pad = jnp.zeros((rank_count + 1, 2, 2, key_width), jnp.float32)
    expand_pad = lax.dynamic_update_index_in_dim(
        expand_pad, expand_grad[: rank_count + 1].reshape(rank_count + 1, 2, key_width), core, 2
    ).reshape(rank_count + 1, 4 * key_width)
    group_rows = jnp.pad(group_grad, ((0, rank_count), (0, model_width - 4 * key_width - value_width)))
    small_grad = jnp.concatenate(
        [
            0.5 * squeeze_grad,
            0.5 * gain_one_grad,
            0.5 * gain_two_grad,
            jnp.concatenate([expand_pad, group_rows], axis=1),
        ]
    )
    if aligned:
        small_grad = small_grad + swap(small_grad, "head", 1)
        state_kept, state_gives = next_sides(state_kept, state_moved)
        state_moved = next_moved(state_gives)
        small_moved = swap(small_grad, *across)
        late_kept, late_gives = next_sides(late_kept, late_moved)
        late_moved = next_moved(late_gives)
        grad_give = to_half(pick(grad_cols, 1 - chip))
        state_moved, small_moved, grad_give = tie((state_moved, small_moved, grad_give))
        state_kept, state_give = split(joined(state_kept, state_moved), along, back[0])
        state_moved = swap(state_give, *back[0])
        small_grad = small_grad + small_moved
        small_moved = swap(small_grad, *beside)
        state_moved, small_moved, late_moved = tie((state_moved, small_moved, late_moved))
        state_kept, state_give = split(to_float(state_kept) + to_float(state_moved), along[:-1], back[1])
        state_moved = swap(state_give, *back[1])
        small_grad = small_grad + small_moved
        small_moved = swap(small_grad, *back[0])
        late_kept, late_give = split(joined(late_kept, late_moved), along, back[0])
        late_moved = swap(late_give, *back[0])
        state_moved, small_moved = tie((state_moved, small_moved))
        state_sum = to_float(state_kept) + to_float(state_moved)
        small_grad = small_grad + small_moved
        small_moved = swap(small_grad, *back[1])
        early, early_squares = optimize_early(ffn_sum)
        early, early_squares, small_moved, late_moved = tie((early, early_squares, small_moved, late_moved))
        small_grad = small_grad + small_moved
        late_sum = shrink(to_float(late_kept) + to_float(late_moved), along[:-1], back[1:])[0]
        output_sum_grad = late_sum[3 * LANES :]
    else:

        def split_rows(a):
            a = a.reshape(2, blocks, 3, LANES // rows, rows, LANES)
            return jnp.moveaxis(a, 3, 2).reshape(2, peers, 3 * rows, LANES)

        late_sum = scatter_cube(split_rows(late_grads[0][:, :, : 3 * LANES]), [beside, across] + back)
        state_sum = scatter_cube(split_rows(state_grads[0]), [across, beside] + back)
        output_grad = late_grads[0][:, :, 3 * LANES :].reshape(2, blocks, value_width, LANES // rows, rows)
        output_grad = output_grad.transpose(0, 1, 3, 4, 2).reshape(2, peers, rows, value_width)
        output_sum_grad = scatter_cube(output_grad, [beside, across] + back).T
        grad_give = to_half(pick(grad_cols, 1 - chip))
        small_grad = sum_everywhere(small_grad)
        early, early_squares = optimize_early(ffn_sum)
    grad_home = to_float(swap(grad_give, *across))
    tokens_grad = jnp.stack(ordered(pick(grad_cols, chip), grad_home, chip))
    out_home = to_float(out_moved)
    block_out = to_half(jnp.stack(ordered(out_mine[0] + out_home[1], out_mine[1] + out_home[0], chip)))

    mine_grad = lax.dynamic_slice_in_dim(small_grad[: rank_count + 2], seq_index * rows, rows, 1)
    expand_total = small_grad[rank_count + 2 :, : 4 * key_width]
    group_total = small_grad[rank_count + 2 : rank_count + 3, 4 * key_width : 4 * key_width + value_width]

    late, late_squares = adam_group(
        share,
        [late_sum, state_sum, output_sum_grad, mine_grad, expand_total, group_total],
        [
            (lambda l, s, *_: jnp.concatenate([l[:rows], s[:rows]], axis=1), 0),
            (
                lambda l, s, *_: jnp.concatenate(
                    [s[rows : 2 * rows], s[2 * rows : 3 * rows], l[rows : 2 * rows], l[2 * rows : 3 * rows]],
                    axis=1,
                ),
                0,
            ),
            (lambda l, s, o, *_: o[...], 0),
            (lambda l, s, o, m, e, g: m[:rank_count], 1),
            (lambda l, s, o, m, e, g: m[rank_count:], 1),
            (lambda l, s, o, m, e, g: e[...], 2),
            (lambda l, s, o, m, e, g: g[...], 2),
        ],
        [
            (query_weight, query_mean, query_square),
            (value_weight, value_mean, value_square),
            (output_weight, output_mean, output_square),
            (squeeze_weight.T, squeeze_mean.T, squeeze_square.T),
            (norms_weight, norms_mean, norms_square),
            (expand_weight, expand_mean, expand_square),
            tuple(a[None, :] for a in (group_weight, group_mean, group_square)),
        ],
    )
    squares = sum_everywhere(jnp.concatenate([early_squares, late_squares]))
    masters = [
        by_width(ffn_weight), down_weight,
        query_weight, value_weight, output_weight, squeeze_weight.T, norms_weight,
        expand_weight, group_weight[None, :],
    ]
    moments = early + late
    news = whole_call(
        lambda *refs: trust_kernel([0, 1, 16, 17, 18, 19, 20, 21, 22], *refs),
        [squares] + masters + [moment[2] for moment in moments],
        [master.shape for master in masters],
    )
    triples = [(new,) + moment[:2] for new, moment in zip(news, moments)]
    ffn_out, down_out, query_out, value_out, output_out, squeeze_out, norms_out, expand_out, group_out = triples
    ffn_out = tuple(jnp.moveaxis(a, 2, 0) for a in ffn_out)
    squeeze_out = tuple(a.T for a in squeeze_out)
    group_out = tuple(a[0] for a in group_out)
    return (block_out, tokens_grad) + tuple(
        array
        for triple in (
            query_out, value_out, squeeze_out, expand_out, group_out, output_out, ffn_out, down_out, norms_out,
        )
        for array in triple
    )


def solution(mesh):
    in_specs = (
        P(None, "seq", "head"),
        P(None, "seq", "head"),
        P("seq", "head", None),
        P("seq", "head", None),
        P("seq", "head", None),
        P("seq", "head", None),
        P("seq", "head", None),
        P("seq", "head", None),
        P("seq", None),
        P("seq", None),
        P("seq", None),
        P(),
        P(),
        P(),
        P(),
        P(),
        P(),
        P("head", "seq"),
        P("head", "seq"),
        P("head", "seq"),
        P("seq", None, "head"),
        P("seq", None, "head"),
        P("seq", None, "head"),
        P("head", "seq"),
        P("head", "seq"),
        P("head", "seq"),
        P(None, "seq"),
        P(None, "seq"),
        P(None, "seq"),
    )
    out_specs = (
        P(None, "seq", "head"),
        P(None, "seq", "head"),
        P("seq", "head", None),
        P("seq", "head", None),
        P("seq", "head", None),
        P("seq", "head", None),
        P("seq", "head", None),
        P("seq", "head", None),
        P("seq", None),
        P("seq", None),
        P("seq", None),
        P(),
        P(),
        P(),
        P(),
        P(),
        P(),
        P("head", "seq"),
        P("head", "seq"),
        P("head", "seq"),
        P("seq", None, "head"),
        P("seq", None, "head"),
        P("seq", None, "head"),
        P("head", "seq"),
        P("head", "seq"),
        P("head", "seq"),
        P(None, "seq"),
        P(None, "seq"),
        P(None, "seq"),
    )
    return jax.shard_map(
        per_device, mesh=mesh, in_specs=in_specs, out_specs=out_specs, check_vma=False
    )
```
